32 devices in a mesh: section: 2 (over core), mp: 2 (over y), dp: 8 (over z, x).
Axes of the slice: x: 2, y: 2, z: 4, core: 2. Of those that a mesh axis runs over, the one named last changes fastest.
Arguments:
- inputs: bfloat16 [2, 16, 1024, 1024], P('section', 'dp', 'mp'), may hold values from -6 to 6
- segment_ids: int32 [2, 16, 1024], P(None, 'dp'), may hold values from 0 to 3, never falling along the last dimension, each value on 1 to 512 neighbouring positions
- cotangent: bfloat16 [2, 16, 1024, 1024], P('section', 'dp', 'mp'), may hold values from -6 to 6
- norm_gains: float32 [2, 2, 1024], P('section'), may hold values from 0.1 to 1.9
- cross_gain: float32 [1024], replicated, may hold values from 0.1 to 1.9
- self_qkv: bfloat16 [2, 1024, 3, 1024], P('section', None, None, 'mp'), may hold values from -0.1875 to 0.1875
- self_out: bfloat16 [2, 1024, 1024], P('section', 'mp'), may hold values from -1.5 to 1.5
- cross_kv: bfloat16 [2, 1024, 1024], P('section', None, 'mp'), may hold values from -0.1875 to 0.1875
- cross_vo: bfloat16 [2, 1024, 1024], P('section', None, 'mp'), may hold values from -0.5 to 0.5
- ffn_in: bfloat16 [2, 1024, 4096], P('section', None, 'mp'), may hold values from -0.1875 to 0.1875
- ffn_out: bfloat16 [2, 4096, 1024], P('section', 'mp'), may hold values from -0.09375 to 0.09375
- adapter_down: bfloat16 [2, 1024, 512], P('section', None, 'mp'), may hold values from -0.1875 to 0.1875
- adapter_down_bias: float32 [2, 512], P('section', 'mp'), may hold values from -3 to 3
- adapter_up: bfloat16 [2, 512, 1024], P('section', 'mp'), may hold values from -0.0625 to 0.0625
- adapter_up_bias: float32 [2, 1024], P('section'), may hold values from -0.5 to 0.5
Outputs:
- outputs: bfloat16 [2, 16, 1024, 1024], P('section', 'dp', 'mp')
- input_grads: float32 [2, 16, 1024, 1024], P('section', 'dp', 'mp')
- down_grad: float32 [2, 1024, 512], P('section', None, 'mp')
- down_bias_grad: float32 [2, 512], P('section', 'mp')
- up_grad: float32 [2, 512, 1024], P('section', 'mp')
- up_bias_grad: float32 [2, 1024], P('section')
The draws below stay inside these ranges and needn't reach their ends.
Inputs may be any that keep to these rules, and one draw needn't show every extreme that they name: `segment_ids`: in each packed row the document numbers run 0 to 3 in order, each document taking 1 to 512 slots and one exactly 512.
All inputs are finite; a program needn't handle non-finite values.
Results may differ from the reference program's by a relative error of at most 0.025.
Values may be sent and summed in bfloat16 or wider, within the bound.
No kernel may reach another device: no remote copies, remote signals or barrier semaphores. Data moves between devices by JAX's collectives and lax.ppermute only.
A program may use at most 320 MiB of HBM per device.

```python
import math
import jax
import jax.numpy as jnp
import numpy as np
from jax import lax

D = 1024
HEADS = 16
FF = 4096
ADAPTER = 512
HEADDIM = 64
SEQ = 1024
DOCS = 4
MOSTDOC = 512
ROWS = 16


def levels(stream_key, dims, shards, low, high):
    gain = 1.0
    for dim, parts in shards:
        heights = jax.random.uniform(jax.random.fold_in(jax.random.fold_in(stream_key, 6), dim), (parts,), jnp.float32, low / len(shards), high / len(shards))
        gain = gain * jnp.repeat(jnp.exp(heights), dims[dim] // parts).reshape((-1,) + (1,) * (len(dims) - 1 - dim))
    return gain


def length_profile(amount, total, reach, skew):
    loads = [(1 << 20) // math.isqrt(rank ** skew) + 1 for rank in range(2, amount + 1)]
    rest, given = total - reach - (amount - 1), [1] * (amount - 1)
    while rest > 0:
        movable = [i for i in range(amount - 1) if given[i] < reach]
        pool, remaining = sum([loads[i] for i in movable]), rest
        for i in movable:
            more = min(reach - given[i], max(1, remaining * loads[i] // pool), rest)
            given[i] = given[i] + more
            rest = rest - more
    return np.array([reach] + given)


def uneven(key, number_of, total, most, skew):
    if number_of == 2:
        one = jax.random.randint(key, (), max(1, total - most), min(most, total - 1) + 1)
        return jnp.stack([one, total - one])
    tallies = jnp.asarray(length_profile(number_of, total, most, skew), jnp.int32)
    couples = (number_of - 1) // 2
    giver, sink = tallies[1:1 + 2 * couples:2], tallies[2:2 + 2 * couples:2]
    room = jnp.minimum(giver - 1, most - sink)
    passed = jax.random.randint(jax.random.fold_in(key, 1), (couples,), 0, 1 << 20) % (room + 1)
    tallies = tallies.at[1:1 + 2 * couples:2].set(giver - passed).at[2:2 + 2 * couples:2].set(sink + passed)
    return tallies[jax.random.permutation(jax.random.fold_in(key, 2), number_of)]


def gaussian(stream_key, dims, deviation, most, shards=(), kind=jnp.bfloat16):
    entries = deviation * jax.random.normal(stream_key, dims, jnp.float32)
    if shards:
        entries = entries * levels(stream_key, dims, shards, -0.22, 0.18)
    return jnp.clip(entries, -most, most).astype(kind)


def setup_inputs(seed: int = 0) -> dict:
    key_of = jax.random.split(jax.random.key(seed), 16)
    return {
        "inputs": gaussian(key_of[0], (2, ROWS, SEQ, D), 1.0, 6.0, ((0, 2), (1, 8), (2, 2))),
        "segment_ids": jax.vmap(lambda own: jnp.searchsorted(jnp.cumsum(uneven(own, DOCS, SEQ, MOSTDOC, 1)), jnp.arange(SEQ), side="right"))(jax.random.split(key_of[1], 2 * ROWS)).reshape((2, ROWS, SEQ)).astype(jnp.int32),
        "cotangent": gaussian(key_of[2], (2, ROWS, SEQ, D), 1.0, 6.0, ((0, 2), (1, 8), (2, 2))),
        "norm_gains": jnp.clip(1.0 + 0.18 * jax.random.normal(key_of[3], (2, 2, D), jnp.float32), 0.1, 1.9),
        "cross_gain": jnp.clip(1.0 + 0.18 * jax.random.normal(key_of[4], (D,), jnp.float32), 0.1, 1.9),
        "self_qkv": gaussian(key_of[5], (2, D, 3, D), D ** -0.5, 0.1875, ((0, 2), (3, 2))),
        "self_out": gaussian(key_of[6], (2, D, D), (D // 64) ** -0.5, 1.5, ((0, 2), (1, 2))),
        "cross_kv": gaussian(key_of[7], (2, D, D), D ** -0.5, 0.1875, ((0, 2), (2, 2))),
        "cross_vo": gaussian(key_of[8], (2, D, D), (D // 8) ** -0.5, 0.5, ((0, 2), (2, 2))),
        "ffn_in": gaussian(key_of[9], (2, D, FF), D ** -0.5, 0.1875, ((0, 2), (2, 2))),
        "ffn_out": gaussian(key_of[10], (2, FF, D), FF ** -0.5, 0.09375, ((0, 2), (1, 2))),
        "adapter_down": gaussian(key_of[11], (2, D, ADAPTER), D ** -0.5, 0.1875, ((0, 2), (2, 2))),
        "adapter_down_bias": gaussian(key_of[12], (2, ADAPTER), 0.5, 3.0, ((0, 2), (1, 2)), jnp.float32),
        "adapter_up": gaussian(key_of[13], (2, ADAPTER, D), (ADAPTER * 16) ** -0.5, 0.0625, ((0, 2), (1, 2))),
        "adapter_up_bias": gaussian(key_of[14], (2, D), 0.1, 0.5, ((0, 2),), jnp.float32),
    }


@jax.custom_vjp
def low(v):
    return lax.optimization_barrier(v.astype(jnp.bfloat16)).astype(jnp.float32)

@jax.custom_vjp
def low_back(v):
    return v

def low_keep(v):
    return (low(v), None)

def low_pass(kept, grad):
    return (grad,)

def back_keep(v):
    return (v, None)

def back_low(kept, grad):
    return (low(grad),)
low.defvjp(low_keep, low_pass)
low_back.defvjp(back_keep, back_low)

def product(left, right):
    return jnp.dot(left, right, precision=lax.Precision.HIGHEST, preferred_element_type=jnp.float32)

def both_round(value):
    return low_back(low(value))

def layer_norm(value, gain_vec):
    center = value - lax.optimization_barrier(jnp.mean(value, -1, keepdims=True))
    spread = lax.optimization_barrier(jnp.mean(center * center, -1, keepdims=True))
    return center * lax.rsqrt(spread + 1e-05) * gain_vec

def gelu_exact(value):
    return jax.nn.gelu(value, approximate=False)

def attend(queries, key_rows, value_rows, allowed):
    query_count = queries.shape[0]
    key_count = key_rows.shape[0]
    query_heads = queries.reshape(query_count, HEADS, HEADDIM)
    key_heads = key_rows.reshape(key_count, HEADS, HEADDIM)
    value_heads = value_rows.reshape(key_count, HEADS, HEADDIM)
    scores = jnp.einsum('qhd,khd->hqk', query_heads, key_heads, precision=lax.Precision.HIGHEST) * HEADDIM ** (-0.5)
    scores = low_back(scores)
    scores = jnp.where(allowed[None], scores, -1e+30)
    attn_probs = jnp.exp(scores - jax.nn.logsumexp(scores, -1, keepdims=True))
    mixed_rows = jnp.einsum('hqk,khd->qhd', low(attn_probs), value_heads, precision=lax.Precision.HIGHEST)
    return both_round(mixed_rows.reshape(query_count, D))

def self_block(rows_in, qkv_weight, out_weight, allowed):
    packed = product(rows_in, qkv_weight.reshape(D, 3 * D))
    queries = both_round(packed[:, :D])
    key_rows = both_round(packed[:, D:2 * D])
    value_rows = both_round(packed[:, 2 * D:])
    return low_back(product(attend(queries, key_rows, value_rows, allowed), out_weight))

def ffn_branch(rows_low, up_weight, down_weight, adapt_down, adapt_bias, adapt_up, adapt_up_bias):
    hidden = low(gelu_exact(low_back(product(rows_low, up_weight))))
    adapter_act = low(gelu_exact(low_back(product(rows_low, adapt_down) + adapt_bias)))
    return low_back(product(hidden, down_weight) + 4.0 * (product(adapter_act, adapt_up) + adapt_up_bias))

def both_layers(x_pair, seg_pair, adapter_set, frozen_set):
    norm_gains, cross_gain, self_qkv, self_out, cross_kv, cross_vo, ffn_in, ffn_out = frozen_set
    adapt_down, adapt_bias, adapt_up, adapt_up_bias = adapter_set
    enc_seg = seg_pair[0]
    dec_seg = seg_pair[1]
    positions = jnp.arange(SEQ)
    enc_allowed = enc_seg[:, None] == enc_seg[None, :]
    dec_allowed = (dec_seg[:, None] == dec_seg[None, :]) & (positions[:, None] >= positions[None, :])
    cross_allowed = dec_seg[:, None] == enc_seg[None, :]
    enc_rows = x_pair[0]
    first = layer_norm(enc_rows + self_block(enc_rows, self_qkv[0], self_out[0], enc_allowed), norm_gains[0, 0])
    enc_out = layer_norm(first + ffn_branch(low(first), ffn_in[0], ffn_out[0], adapt_down[0], adapt_bias[0], adapt_up[0], adapt_up_bias[0]), norm_gains[0, 1])
    enc_low = low(enc_out)
    cross_keys = both_round(product(enc_low, cross_kv[0]))
    cross_values = both_round(product(enc_low, cross_vo[0]))
    dec_rows = x_pair[1]
    dec_first = layer_norm(dec_rows + self_block(dec_rows, self_qkv[1], self_out[1], dec_allowed), norm_gains[1, 0])
    cross_query = both_round(product(low(dec_first), cross_kv[1]))
    cross_mixed = attend(cross_query, cross_keys, cross_values, cross_allowed)
    cross_out = low_back(product(cross_mixed, cross_vo[1].T))
    second = layer_norm(dec_first + cross_out, cross_gain)
    dec_out = layer_norm(second + ffn_branch(low(second), ffn_in[1], ffn_out[1], adapt_down[1], adapt_bias[1], adapt_up[1], adapt_up_bias[1]), norm_gains[1, 1])
    return jnp.stack([enc_out, dec_out])

def reference(inputs, segment_ids, cotangent, norm_gains, cross_gain, self_qkv, self_out, cross_kv, cross_vo, ffn_in, ffn_out, adapter_down, adapter_down_bias, adapter_up, adapter_up_bias):
    frozen_set = (norm_gains.astype(jnp.float32), cross_gain.astype(jnp.float32), self_qkv.astype(jnp.float32), self_out.astype(jnp.float32), cross_kv.astype(jnp.float32), cross_vo.astype(jnp.float32), ffn_in.astype(jnp.float32), ffn_out.astype(jnp.float32))
    adapter_set = (adapter_down.astype(jnp.float32), adapter_down_bias.astype(jnp.float32), adapter_up.astype(jnp.float32), adapter_up_bias.astype(jnp.float32))

    def one_row(running, row_data):
        x_pair, seg_pair, cot_pair = row_data

        def forward_fn(x_values, adapter_values):
            return both_layers(x_values, seg_pair, adapter_values, frozen_set)
        layer_outs, pull_back = jax.vjp(forward_fn, x_pair.astype(jnp.float32), adapter_set)
        x_grad, adapter_grad = pull_back(cot_pair.astype(jnp.float32))
        running = tuple((a + b for a, b in zip(running, adapter_grad)))
        return (running, (layer_outs.astype(jnp.bfloat16), x_grad))
    start_sums = tuple((jnp.zeros(v.shape, jnp.float32) for v in adapter_set))
    row_inputs = jnp.transpose(inputs, (1, 0, 2, 3))
    row_segs = jnp.transpose(segment_ids, (1, 0, 2))
    row_cots = jnp.transpose(cotangent, (1, 0, 2, 3))
    grad_sums, (layer_outs, x_grads) = lax.scan(one_row, start_sums, (row_inputs, row_segs, row_cots))
    outputs = jnp.transpose(layer_outs, (1, 0, 2, 3))
    input_grads = jnp.transpose(x_grads, (1, 0, 2, 3))
    return (outputs, input_grads, grad_sums[0], grad_sums[1], grad_sums[2], grad_sums[3])
```

```python
import functools

import jax
import jax.numpy as jnp
from jax import lax
from jax.experimental import pallas as pl
from jax.experimental.pallas import tpu as pltpu
from jax.sharding import PartitionSpec as P

HEADDIM = 64
BUNCH = 4
WIDE = BUNCH * HEADDIM
CHUNK = 512
SCALE = HEADDIM**-0.5
HIDDEN_MASK = -1e30
VMEM_LIMIT = 60 * 1024 * 1024
BF16 = jnp.bfloat16
F32 = jnp.float32


def dot_nn(left, right):
    return lax.dot_general(left, right, (((1,), (0,)), ((), ())), preferred_element_type=F32)


def dot_nt(left, right):
    return lax.dot_general(left, right, (((1,), (1,)), ((), ())), preferred_element_type=F32)


def dot_tn(left, right):
    return lax.dot_general(left, right, (((0,), (0,)), ((), ())), preferred_element_type=F32)


class Stream:
    def __init__(self, parts, cut, count):
        self.parts = parts
        self.cut = cut
        self.count = count

    @property
    def arrays(self):
        return [a for part in self.parts for a in part]


def column_cut(width):
    return lambda ref, k: ref.at[:, pl.ds(pl.multiple_of(k * width, width), width)]


def row_cut(width):
    return lambda ref, k: ref.at[pl.ds(pl.multiple_of(k * width, width), width), :]


def stack_cut(width):
    return lambda ref, k: ref.at[:, :, pl.ds(pl.multiple_of(k * width, width), width)]


def issue(stream, refs, buf, sem, layer, step, slot):
    mine = lax.axis_index("section") == layer
    base = 0
    for i in range(len(stream.parts)):
        own, other = refs[2 * i], refs[2 * i + 1]
        here = (step >= base) & (step < base + stream.count)
        k = jnp.clip(step - base, 0, stream.count - 1)

        @pl.when(here & mine)
        def _():
            pltpu.make_async_copy(stream.cut(own, k), buf.at[slot], sem.at[slot]).start()

        @pl.when(here & jnp.logical_not(mine))
        def _():
            pltpu.make_async_copy(stream.cut(other, k), buf.at[slot], sem.at[slot]).start()

        base += stream.count


def await_chunk(stream, refs, buf, sem, slot):
    pltpu.make_async_copy(stream.cut(refs[0], 0), buf.at[slot], sem.at[slot]).wait()


def advance(streams, stream_refs, bufs, sems, layer, step, steps):
    slot = lax.rem(step, 2)

    @pl.when(step == 0)
    def _():
        for s, r, b, m in zip(streams, stream_refs, bufs, sems):
            issue(s, r, b, m, layer, 0, 0)

    @pl.when(step + 1 < steps)
    def _():
        for s, r, b, m in zip(streams, stream_refs, bufs, sems):
            issue(s, r, b, m, layer, step + 1, 1 - slot)

    for s, r, b, m in zip(streams, stream_refs, bufs, sems):
        await_chunk(s, r, b, m, slot)
    return slot


def call(body, steps, operands, in_blocks, streams, out_shapes, out_blocks, bufs, scratch, cost):
    arrays = [a for s in streams for a in s.arrays]
    counts = [len(s.arrays) for s in streams]
    n_ops, n_out = len(operands), len(out_shapes)

    def kernel(*refs):
        ins, rest = refs[:n_ops], refs[n_ops:]
        stream_refs = []
        for n in counts:
            stream_refs.append(rest[:n])
            rest = rest[n:]
        outs, rest = rest[:n_out], rest[n_out:]
        buf_refs, rest = rest[: len(bufs)], rest[len(bufs) :]
        sems, extra = rest[: len(bufs)], rest[len(bufs) :]
        body(ins, stream_refs, outs, buf_refs, sems, extra)

    return pl.pallas_call(
        kernel,
        grid=(steps,),
        in_specs=list(in_blocks) + [pl.BlockSpec(memory_space=pl.ANY)] * len(arrays),
        out_specs=tuple(out_blocks),
        out_shape=tuple(out_shapes),
        scratch_shapes=[pltpu.VMEM((2,) + tuple(b), BF16) for b in bufs]
        + [pltpu.SemaphoreType.DMA((2,)) for _ in bufs]
        + list(scratch),
        compiler_params=pltpu.CompilerParams(
            dimension_semantics=("arbitrary",), vmem_limit_bytes=VMEM_LIMIT
        ),
        cost_estimate=pl.CostEstimate(
            flops=int(cost), bytes_accessed=int(cost // 500), transcendentals=0
        ),
    )(*operands, *arrays)


def whole(shape):
    zeros = (0,) * len(shape)
    return pl.BlockSpec(tuple(shape), lambda i: zeros)


def per_step(shape, first=0, last=None):
    def index(i):
        k = jnp.maximum(i - first, 0)
        if last is not None:
            k = jnp.minimum(k, last)
        return (k,) + (0,) * len(shape)

    return pl.BlockSpec((1,) + tuple(shape), index)


def shaped(shape, dtype):
    return jax.ShapeDtypeStruct(tuple(shape), dtype)


def normalized(value):
    center = value - jnp.mean(value, -1, keepdims=True)
    spread = jnp.mean(center * center, -1, keepdims=True)
    inverse = lax.rsqrt(spread + 1e-05)
    return center * inverse, inverse


def norm_slope(grad, hat, inverse, gain):
    scaled = grad * gain
    along = jnp.mean(scaled * hat, -1, keepdims=True)
    return inverse * (scaled - jnp.mean(scaled, -1, keepdims=True) - hat * along)


def gelu_pair(value):
    below = 0.5 + 0.5 * lax.erf(value * (0.5**0.5))
    density = jnp.exp(value * value * -0.5) * 0.3989422804014327
    return value * below, below + value * density


def only_head(value, head):
    lane = lax.broadcasted_iota(jnp.int32, (1, WIDE), 1)
    keep = (lane >= head * HEADDIM) & (lane < (head + 1) * HEADDIM)
    return jnp.where(keep, value, jnp.zeros_like(value))


def attend(q, k, v, bias_ref, out_ref, block):
    rows = q.shape[0]
    scaled = q * jnp.asarray(SCALE, BF16)
    for first in range(0, rows, block):
        part = slice(first, first + block)
        total = None
        for head in range(BUNCH):
            scores = dot_nt(only_head(scaled[part], head), k) + bias_ref[part, :]
            peak = jnp.max(scores, -1, keepdims=True)
            powers = jnp.exp(scores - peak)
            share = 1.0 / jnp.sum(powers, -1, keepdims=True)
            mixed = dot_nn((powers * share).astype(BF16), only_head(v, head))
            total = mixed if total is None else total + mixed
        out_ref[part, :] = total


def attend_slope(q, k, v, grad, bias_ref, dq_ref, dk_ref, dv_ref, block):
    rows = q.shape[0]
    scaled = q * jnp.asarray(SCALE, BF16)
    for first in range(0, rows, block):
        part = slice(first, first + block)
        dq_total = None
        for head in range(BUNCH):
            q_head = only_head(scaled[part], head)
            g_head = only_head(grad[part], head)
            scores = dot_nt(k, q_head) + bias_ref[:, part]
            peak = jnp.max(scores, 0, keepdims=True)
            powers = jnp.exp(scores - peak)
            share = 1.0 / jnp.sum(powers, 0, keepdims=True)
            probs = powers * share
            prob_grad = dot_nt(v, g_head)
            inner = jnp.sum(probs * prob_grad, 0, keepdims=True)
            score_grad = (probs * (prob_grad - inner)).astype(BF16)
            dv_part = dot_nn(probs.astype(BF16), g_head)
            dk_part = dot_nn(score_grad, q_head)
            if first == 0 and head == 0:
                dv_ref[...] = dv_part
                dk_ref[...] = dk_part
            else:
                dv_ref[...] += dv_part
                dk_ref[...] += dk_part
            dq_part = dot_tn(score_grad, only_head(k, head))
            dq_total = dq_part if dq_total is None else dq_total + dq_part
        dq_ref[part, :] = dq_total * SCALE


def fill_bias(bias_ref, row_seg, col_seg, order):
    seen = row_seg == col_seg
    if order:
        shape = bias_ref.shape
        r = lax.broadcasted_iota(jnp.int32, shape, 0)
        c = lax.broadcasted_iota(jnp.int32, shape, 1)
        seen = seen & ((c <= r) if order == 1 else (r <= c))
    bias_ref[...] = jnp.where(seen, 0.0, HIDDEN_MASK)


def self_forward(layer, x, seg_col, seg_row, gain, qkv, out):
    rows, width = x.shape
    steps = len(qkv.parts) * qkv.count

    def body(ins, wrefs, outs, bufs, sems, extra):
        x_ref, segc_ref, segr_ref, gain_ref = ins
        qkv_ref, hat_ref, inv_ref = outs
        acc, bias, mixed = extra
        step = pl.program_id(0)
        slot = advance((qkv, out), wrefs, bufs, sems, layer, step, steps)

        @pl.when(step == 0)
        def _():
            fill_bias(bias, segc_ref[...], segr_ref[...], 1 if layer == 1 else 0)
            acc[...] = x_ref[...].astype(F32)

        x_rows = x_ref[...]
        w = bufs[0].at[slot]
        q = dot_nn(x_rows, w[0]).astype(BF16)
        k = dot_nn(x_rows, w[1]).astype(BF16)
        v = dot_nn(x_rows, w[2]).astype(BF16)
        qkv_ref[0, 0] = q
        qkv_ref[0, 1] = k
        qkv_ref[0, 2] = v
        attend(q, k, v, bias, mixed, 256)
        acc[...] += dot_nn(mixed[...].astype(BF16), bufs[1][slot])

        @pl.when(step == steps - 1)
        def _():
            hat, inverse = normalized(acc[...])
            hat_ref[...] = hat.astype(BF16)
            inv_ref[...] = inverse

    return call(
        body,
        steps,
        [x, seg_col, seg_row, gain],
        [whole(x.shape), whole(seg_col.shape), whole(seg_row.shape), whole(gain.shape)],
        [qkv, out],
        [shaped((steps, 3, rows, WIDE), BF16), shaped((rows, width), BF16), shaped((rows, 1), F32)],
        [per_step((3, rows, WIDE)), whole((rows, width)), whole((rows, 1))],
        [(3, width, WIDE), (WIDE, width)],
        [
            pltpu.VMEM((rows, width), F32),
            pltpu.VMEM((rows, rows), F32),
            pltpu.VMEM((rows, WIDE), F32),
        ],
        steps * (2 * rows * width * WIDE * 4 + 16 * rows * rows * WIDE),
    )


def self_backward(layer, grad, saved, seg_col, seg_row, qkv, out):
    rows, width = grad.shape
    steps = len(qkv.parts) * qkv.count

    def body(ins, wrefs, outs, bufs, sems, extra):
        g_ref, saved_ref, segc_ref, segr_ref = ins
        (dx_ref,) = outs
        acc, bias, dq, dk, dv = extra
        step = pl.program_id(0)
        slot = advance((qkv, out), wrefs, bufs, sems, layer, step, steps)

        @pl.when(step == 0)
        def _():
            fill_bias(bias, segc_ref[...], segr_ref[...], 2 if layer == 1 else 0)
            acc[...] = g_ref[...].astype(F32)

        mixed_grad = dot_nt(g_ref[...], bufs[1][slot]).astype(BF16)
        attend_slope(
            saved_ref[0, 0], saved_ref[0, 1], saved_ref[0, 2], mixed_grad, bias, dq, dk, dv, 256
        )
        w = bufs[0].at[slot]
        acc[...] += (
            dot_nt(dq[...].astype(BF16), w[0])
            + dot_nt(dk[...].astype(BF16), w[1])
            + dot_nt(dv[...].astype(BF16), w[2])
        )

        @pl.when(step == steps - 1)
        def _():
            dx_ref[...] = acc[...].astype(BF16)

    return call(
        body,
        steps,
        [grad, saved, seg_col, seg_row],
        [whole(grad.shape), per_step((3, rows, WIDE)), whole(seg_col.shape), whole(seg_row.shape)],
        [qkv, out],
        [shaped((rows, width), BF16)],
        [whole((rows, width))],
        [(3, width, WIDE), (WIDE, width)],
        [
            pltpu.VMEM((rows, width), F32),
            pltpu.VMEM((rows, rows), F32),
            pltpu.VMEM((rows, WIDE), F32),
            pltpu.VMEM((rows, WIDE), F32),
            pltpu.VMEM((rows, WIDE), F32),
        ],
        steps * (2 * rows * width * WIDE * 4 + 40 * rows * rows * WIDE),
    )[0]


def cross_forward(hat, gain, kv_own, kv_away, seg_col, keys_row, query_w, out_w):
    rows, width = hat.shape
    steps = len(query_w.parts) * query_w.count

    def body(ins, wrefs, outs, bufs, sems, extra):
        hat_ref, gain_ref, own_ref, away_ref, segc_ref, keysr_ref = ins
        q_ref, nhat_ref, inv_ref = outs
        acc, low, bias, mixed, keys, values = extra
        step = pl.program_id(0)
        slot = advance((query_w, out_w), wrefs, bufs, sems, 1, step, steps)

        @pl.when(step == 0)
        def _():
            fill_bias(bias, segc_ref[...], keysr_ref[...], 0)
            first = hat_ref[...].astype(F32) * gain_ref[...]
            acc[...] = first
            low[...] = first.astype(BF16)

        q = dot_nn(low[...], bufs[0][slot]).astype(BF16)
        q_ref[0] = q
        keys[:rows] = own_ref[0, 0]
        keys[rows:] = away_ref[0, 0]
        values[:rows] = own_ref[0, 1]
        values[rows:] = away_ref[0, 1]
        attend(q, keys[...], values[...], bias, mixed, 256)
        acc[...] += dot_nt(mixed[...].astype(BF16), bufs[1][slot])

        @pl.when(step == steps - 1)
        def _():
            nhat, inverse = normalized(acc[...])
            nhat_ref[...] = nhat.astype(BF16)
            inv_ref[...] = inverse

    return call(
        body,
        steps,
        [hat, gain, kv_own, kv_away, seg_col, keys_row],
        [
            whole(hat.shape),
            whole(gain.shape),
            per_step((2, rows, WIDE)),
            per_step((2, rows, WIDE)),
            whole(seg_col.shape),
            whole(keys_row.shape),
        ],
        [query_w, out_w],
        [shaped((steps, rows, WIDE), BF16), shaped((rows, width), BF16), shaped((rows, 1), F32)],
        [per_step((rows, WIDE)), whole((rows, width)), whole((rows, 1))],
        [(width, WIDE), (width, WIDE)],
        [
            pltpu.VMEM((rows, width), F32),
            pltpu.VMEM((rows, width), BF16),
            pltpu.VMEM((rows, 2 * rows), F32),
            pltpu.VMEM((rows, WIDE), F32),
            pltpu.VMEM((2 * rows, WIDE), BF16),
            pltpu.VMEM((2 * rows, WIDE), BF16),
        ],
        steps * (2 * rows * width * WIDE * 2 + 32 * rows * rows * WIDE),
    )


def cross_backward(grad, hat, inv, gain, saved_q, kv_own, kv_away, keys_col, seg_row, query_w, out_w):
    rows, width = grad.shape
    steps = len(query_w.parts) * query_w.count

    def body(ins, wrefs, outs, bufs, sems, extra):
        g_ref, hat_ref, inv_ref, gain_ref, q_ref, own_ref, away_ref, keysc_ref, segr_ref = ins
        dx_ref, own_grad_ref, away_grad_ref = outs
        acc, bias, dq, dk, dv, keys, values = extra
        step = pl.program_id(0)
        slot = advance((query_w, out_w), wrefs, bufs, sems, 1, step, steps)

        @pl.when(step == 0)
        def _():
            fill_bias(bias, keysc_ref[...], segr_ref[...], 0)
            acc[...] = g_ref[...].astype(F32)

        mixed_grad = dot_nn(g_ref[...], bufs[1][slot]).astype(BF16)
        keys[:rows] = own_ref[0, 0]
        keys[rows:] = away_ref[0, 0]
        values[:rows] = own_ref[0, 1]
        values[rows:] = away_ref[0, 1]
        attend_slope(q_ref[0], keys[...], values[...], mixed_grad, bias, dq, dk, dv, 256)
        own_grad_ref[0, 0] = dk[:rows].astype(BF16)
        own_grad_ref[0, 1] = dv[:rows].astype(BF16)
        away_grad_ref[0, 0] = dk[rows:].astype(BF16)
        away_grad_ref[0, 1] = dv[rows:].astype(BF16)
        acc[...] += dot_nt(dq[...].astype(BF16), bufs[0][slot])

        @pl.when(step == steps - 1)
        def _():
            dx_ref[...] = norm_slope(
                acc[...], hat_ref[...].astype(F32), inv_ref[...], gain_ref[...]
            ).astype(BF16)

    return call(
        body,
        steps,
        [grad, hat, inv, gain, saved_q, kv_own, kv_away, keys_col, seg_row],
        [
            whole(grad.shape),
            whole(hat.shape),
            whole(inv.shape),
            whole(gain.shape),
            per_step((rows, WIDE)),
            per_step((2, rows, WIDE)),
            per_step((2, rows, WIDE)),
            whole(keys_col.shape),
            whole(seg_row.shape),
        ],
        [query_w, out_w],
        [
            shaped((rows, width), BF16),
            shaped((steps, 2, rows, WIDE), BF16),
            shaped((steps, 2, rows, WIDE), BF16),
        ],
        [whole((rows, width)), per_step((2, rows, WIDE)), per_step((2, rows, WIDE))],
        [(width, WIDE), (width, WIDE)],
        [
            pltpu.VMEM((rows, width), F32),
            pltpu.VMEM((2 * rows, rows), F32),
            pltpu.VMEM((rows, WIDE), F32),
            pltpu.VMEM((2 * rows, WIDE), F32),
            pltpu.VMEM((2 * rows, WIDE), F32),
            pltpu.VMEM((2 * rows, WIDE), BF16),
            pltpu.VMEM((2 * rows, WIDE), BF16),
        ],
        steps * (2 * rows * width * WIDE * 2 + 80 * rows * rows * WIDE),
    )


def keys_forward(y, key_w, value_w):
    rows, width = y.shape
    steps = len(key_w.parts) * key_w.count

    def body(ins, wrefs, outs, bufs, sems, extra):
        (kv_ref,) = outs
        slot = advance((key_w, value_w), wrefs, bufs, sems, 0, pl.program_id(0), steps)
        kv_ref[0, 0] = dot_nn(ins[0][...], bufs[0][slot]).astype(BF16)
        kv_ref[0, 1] = dot_nn(ins[0][...], bufs[1][slot]).astype(BF16)

    return call(
        body,
        steps,
        [y],
        [whole(y.shape)],
        [key_w, value_w],
        [shaped((steps, 2, rows, WIDE), BF16)],
        [per_step((2, rows, WIDE))],
        [(width, WIDE), (width, WIDE)],
        [],
        steps * 4 * rows * width * WIDE,
    )[0]


def keys_backward(out_grad, kv_grad, kv_grad_away, key_w, value_w):
    rows, width = out_grad.shape
    steps = len(key_w.parts) * key_w.count

    def body(ins, wrefs, outs, bufs, sems, extra):
        g_ref, own_ref, away_ref = ins
        (sum_ref,) = outs
        (acc,) = extra
        step = pl.program_id(0)
        slot = advance((key_w, value_w), wrefs, bufs, sems, 0, step, steps)

        @pl.when(step == 0)
        def _():
            acc[...] = g_ref[...].astype(F32)

        both = (own_ref[0].astype(F32) + away_ref[0].astype(F32)).astype(BF16)
        acc[...] += dot_nt(both[0], bufs[0][slot]) + dot_nt(both[1], bufs[1][slot])

        @pl.when(step == steps - 1)
        def _():
            sum_ref[...] = acc[...].astype(BF16)

    return call(
        body,
        steps,
        [out_grad, kv_grad, kv_grad_away],
        [whole(out_grad.shape), per_step((2, rows, WIDE)), per_step((2, rows, WIDE))],
        [key_w, value_w],
        [shaped((rows, width), BF16)],
        [whole((rows, width))],
        [(width, WIDE), (width, WIDE)],
        [pltpu.VMEM((rows, width), F32)],
        steps * 4 * rows * width * WIDE,
    )[0]


def two_phase(layer, streams_a, refs_a, bufs_a, sems_a, streams_b, refs_b, bufs_b, sems_b, step, na, nb):
    slot = lax.rem(step, 2)

    def start_a(at, to):
        for s, r, b, m in zip(streams_a, refs_a, bufs_a, sems_a):
            issue(s, r, b, m, layer, at, to)

    def start_b(at, to):
        for s, r, b, m in zip(streams_b, refs_b, bufs_b, sems_b):
            issue(s, r, b, m, layer, at - na, to)

    @pl.when(step == 0)
    def _():
        start_a(0, 0)

    @pl.when(step + 1 < na)
    def _():
        start_a(step + 1, 1 - slot)

    @pl.when((step + 1 >= na) & (step + 1 < na + nb))
    def _():
        start_b(step + 1, 1 - slot)

    @pl.when(step < na)
    def _():
        for s, r, b, m in zip(streams_a, refs_a, bufs_a, sems_a):
            await_chunk(s, r, b, m, slot)

    @pl.when(step >= na)
    def _():
        for s, r, b, m in zip(streams_b, refs_b, bufs_b, sems_b):
            await_chunk(s, r, b, m, slot)

    return slot


def branch_forward(layer, hat, gain, out_gain, down_bias, up_bias, ffn, adapter):
    rows, width = hat.shape
    up_w, down_w = ffn
    adown, aup = adapter
    na = len(up_w.parts) * up_w.count
    nb = len(adown.parts) * adown.count
    units = down_bias.shape[-1]
    steps = na + nb

    def body(ins, wrefs, outs, bufs, sems, extra):
        hat_ref, gain_ref, ogain_ref, dbias_ref, ubias_ref = ins
        slope_ref, aslope_ref, aact_ref, nhat_ref, inv_ref, y_ref = outs
        acc, low = extra
        step = pl.program_id(0)
        slot = two_phase(
            layer, ffn, wrefs[:2], bufs[:2], sems[:2], adapter, wrefs[2:], bufs[2:], sems[2:],
            step, na, nb,
        )

        @pl.when(step == 0)
        def _():
            first = hat_ref[...].astype(F32) * gain_ref[...]
            low[...] = first.astype(BF16)
            acc[...] = first + 4.0 * ubias_ref[...]

        @pl.when(step < na)
        def _():
            for at in range(0, rows, 256):
                part = slice(at, at + 256)
                act, slope = gelu_pair(dot_nn(low[part, :], bufs[0][slot]))
                slope_ref[0, part, :] = slope.astype(BF16)
                acc[part, :] += dot_nn(act.astype(BF16), bufs[1][slot])

        @pl.when(step >= na)
        def _():
            act, slope = gelu_pair(dot_nn(low[...], bufs[2][slot]) + dbias_ref[0])
            low_act = act.astype(BF16)
            aslope_ref[0] = slope.astype(BF16)
            aact_ref[0] = low_act
            acc[...] += dot_nn(low_act * jnp.asarray(4.0, BF16), bufs[3][slot])

        @pl.when(step == steps - 1)
        def _():
            nhat, inverse = normalized(acc[...])
            nhat_ref[...] = nhat.astype(BF16)
            inv_ref[...] = inverse
            y_ref[...] = (nhat * ogain_ref[...]).astype(BF16)

    return call(
        body,
        steps,
        [hat, gain, out_gain, down_bias, up_bias],
        [
            whole(hat.shape),
            whole(gain.shape),
            whole(out_gain.shape),
            per_step((1, units), na),
            whole(up_bias.shape),
        ],
        [up_w, down_w, adown, aup],
        [
            shaped((na, rows, CHUNK), BF16),
            shaped((nb, rows, units), BF16),
            shaped((nb, rows, units), BF16),
            shaped((rows, width), BF16),
            shaped((rows, 1), F32),
            shaped((rows, width), BF16),
        ],
        [
            per_step((rows, CHUNK), 0, na - 1),
            per_step((rows, units), na),
            per_step((rows, units), na),
            whole((rows, width)),
            whole((rows, 1)),
            whole((rows, width)),
        ],
        [(width, CHUNK), (CHUNK, width), (width, units), (units, width)],
        [pltpu.VMEM((rows, width), F32), pltpu.VMEM((rows, width), BF16)],
        4 * rows * width * (na * CHUNK + nb * units),
    )


def branch_backward(layer, out_grad, nhat, ninv, out_gain, hat, inv, gain, slope, aslope, aact, ffn, adapter):
    rows, width = hat.shape
    up_w, down_w = ffn
    adown, aup = adapter
    na = len(up_w.parts) * up_w.count
    nb = len(adown.parts) * adown.count
    units = aact.shape[-1]
    steps = na + nb

    def body(ins, wrefs, outs, bufs, sems, extra):
        g_ref, nhat_ref, ninv_ref, ogain_ref, hat_ref, inv_ref, gain_ref, slope_ref, aslope_ref, aact_ref = ins
        dx_ref, down_ref, dbias_ref, up_ref, ubias_ref = outs
        acc, low, rows_low = extra
        step = pl.program_id(0)
        slot = two_phase(
            layer, ffn, wrefs[:2], bufs[:2], sems[:2], adapter, wrefs[2:], bufs[2:], sems[2:],
            step, na, nb,
        )

        @pl.when(step == 0)
        def _():
            grad = norm_slope(
                g_ref[...].astype(F32), nhat_ref[...].astype(F32), ninv_ref[...], ogain_ref[...]
            )
            acc[...] = grad
            small = grad.astype(BF16)
            low[...] = small
            ubias_ref[...] = 4.0 * jnp.sum(small.astype(F32), 0, keepdims=True)
            rows_low[...] = (hat_ref[...].astype(F32) * gain_ref[...]).astype(BF16)

        @pl.when(step < na)
        def _():
            for at in range(0, rows, 256):
                part = slice(at, at + 256)
                hidden = dot_nt(low[part, :], bufs[1][slot]) * slope_ref[0, part, :].astype(F32)
                acc[part, :] += dot_nt(hidden.astype(BF16), bufs[0][slot])

        @pl.when(step >= na)
        def _():
            hidden = 4.0 * dot_nt(low[...], bufs[3][slot]) * aslope_ref[0].astype(F32)
            small = hidden.astype(BF16)
            acc[...] += dot_nt(small, bufs[2][slot])
            down_ref[0] = dot_tn(rows_low[...], small)
            dbias_ref[0] = jnp.sum(small.astype(F32), 0, keepdims=True)
            up_ref[0] = 4.0 * dot_tn(aact_ref[0], low[...])

        @pl.when(step == steps - 1)
        def _():
            dx_ref[...] = norm_slope(
                acc[...], hat_ref[...].astype(F32), inv_ref[...], gain_ref[...]
            ).astype(BF16)

    return call(
        body,
        steps,
        [out_grad, nhat, ninv, out_gain, hat, inv, gain, slope, aslope, aact],
        [
            whole(out_grad.shape),
            whole(nhat.shape),
            whole(ninv.shape),
            whole(out_gain.shape),
            whole(hat.shape),
            whole(inv.shape),
            whole(gain.shape),
            per_step((rows, CHUNK), 0, na - 1),
            per_step((rows, units), na),
            per_step((rows, units), na),
        ],
        [up_w, down_w, adown, aup],
        [
            shaped((rows, width), BF16),
            shaped((nb, width, units), F32),
            shaped((nb, 1, units), F32),
            shaped((nb, units, width), F32),
            shaped((1, width), F32),
        ],
        [
            whole((rows, width)),
            per_step((width, units), na),
            per_step((1, units), na),
            per_step((units, width), na),
            whole((1, width)),
        ],
        [(width, CHUNK), (CHUNK, width), (width, units), (units, width)],
        [
            pltpu.VMEM((rows, width), F32),
            pltpu.VMEM((rows, width), BF16),
            pltpu.VMEM((rows, width), BF16),
        ],
        4 * rows * width * (na * CHUNK + nb * units),
    )


def swap(value, axis):
    return jax.tree.map(lambda a: lax.ppermute(a, axis, [(0, 1), (1, 0)]), value)


def rotated(pieces, start, count):
    return lax.dynamic_slice_in_dim(jnp.concatenate(pieces, 0), start, count, 0)


def per_device(
    inputs,
    segment_ids,
    cotangent,
    norm_gains,
    cross_gain,
    self_qkv,
    self_out,
    cross_kv,
    cross_vo,
    ffn_in,
    ffn_out,
    adapter_down,
    adapter_down_bias,
    adapter_up,
    adapter_up_bias,
):
    core = lax.axis_index("section")
    side = lax.axis_index("mp")
    first_core = core == 0
    seq = segment_ids.shape[2]
    half = seq // 2
    width = inputs.shape[3]
    units = adapter_down.shape[2]

    qkv = jnp.transpose(self_qkv[0], (1, 0, 2))
    near = (
        qkv, self_out[0], cross_kv[0], cross_vo[0], ffn_in[0], ffn_out[0],
        adapter_down[0], adapter_up[0],
    )
    far = swap(near, "mp")
    near_other = swap(near, "section")
    far_other = swap(far, "section")
    parts = [
        [(near[i], near_other[i]), (far[i], far_other[i])] for i in range(len(near))
    ]
    w_qkv = Stream(parts[0], stack_cut(WIDE), near[0].shape[2] // WIDE)
    w_out = Stream(parts[1], row_cut(WIDE), near[1].shape[0] // WIDE)
    w_ckv = Stream(parts[2], column_cut(WIDE), near[2].shape[1] // WIDE)
    w_cvo = Stream(parts[3], column_cut(WIDE), near[3].shape[1] // WIDE)
    w_up = Stream(parts[4], column_cut(CHUNK), near[4].shape[1] // CHUNK)
    w_down = Stream(parts[5], row_cut(CHUNK), near[5].shape[0] // CHUNK)
    w_adown = Stream(parts[6], column_cut(units), 1)
    w_aup = Stream(parts[7], row_cut(units), 1)
    ffn = (w_up, w_down)
    adapter = (w_adown, w_aup)

    bias_near = adapter_down_bias[0][None]
    bias_far = swap(bias_near, "mp")
    small = jnp.concatenate(
        [
            norm_gains[0],
            adapter_up_bias,
            jnp.concatenate([bias_near, bias_far, jnp.zeros((1, width - 2 * units), F32)], 1),
        ],
        0,
    )
    small_other = swap(small, "section")
    enc_small = jnp.where(first_core, small, small_other)
    dec_small = jnp.where(first_core, small_other, small)

    def small_of(s):
        down_bias = jnp.stack([s[3:4, :units], s[3:4, units : 2 * units]], 0)
        return s[0:1], s[1:2], s[2:3], down_bias

    enc_gain1, enc_gain2, enc_upb, enc_downb = small_of(enc_small)
    dec_gain1, dec_gain2, dec_upb, dec_downb = small_of(dec_small)
    mid_gain = cross_gain[None]

    segs = lax.dynamic_index_in_dim(segment_ids, side, 1, keepdims=False)
    docs = jnp.arange(seq)
    counts = jnp.sum(segs[:, :, None] == docs[None, None, :8], 1)
    largest = jnp.argmax(counts, 1)
    starts = jnp.sum(segs < largest[:, None], 1).astype(jnp.int32)

    def halves_of_seg(seg, start):
        twice = jnp.concatenate([seg, seg], 0)
        mine = lax.dynamic_slice_in_dim(twice, start + half * core, half, 0)
        away = lax.dynamic_slice_in_dim(twice, start + half * (1 - core), half, 0)
        return mine, away

    enc_seg, enc_seg_away = halves_of_seg(segs[0], starts[0])
    dec_seg, _ = halves_of_seg(segs[1], starts[1])
    own_start = jnp.where(first_core, starts[0], starts[1])

    def rows_here(value):
        keep = lax.dynamic_index_in_dim(value[0], side, 0, keepdims=False)
        give = lax.dynamic_index_in_dim(value[0], 1 - side, 0, keepdims=False)
        got = swap(give, "mp")
        at = lax.rem(own_start + seq - half * side, seq)
        ring = (keep, got, keep, got)
        mine = rotated(ring, at + half * core, half)
        away = rotated(ring, lax.rem(at + half * (1 - core), seq), half)
        other = swap(away, "section")
        return jnp.where(first_core, mine, other), jnp.where(first_core, other, mine)

    def rows_back(enc, dec):
        mine = jnp.where(first_core, enc, dec)
        away = jnp.where(first_core, dec, enc)
        other = swap(away, "section")
        big = jnp.where(first_core, mine, other)
        rest = jnp.where(first_core, other, mine)
        ring = (big, rest, big, rest)
        keep = rotated(ring, lax.rem(half * side + seq - own_start, seq), half)
        give = rotated(ring, lax.rem(half * (1 - side) + seq - own_start, seq), half)
        got = swap(give, "mp")
        return jnp.where(side == 0, jnp.stack([keep, got]), jnp.stack([got, keep]))

    x_enc, x_dec = rows_here(inputs)
    g_enc, g_dec = rows_here(cotangent)

    enc_col, enc_row = enc_seg[:, None], enc_seg[None, :]
    dec_col, dec_row = dec_seg[:, None], dec_seg[None, :]
    all_keys = jnp.concatenate([enc_seg, enc_seg_away], 0)

    e_qkv, e_hat1, e_inv1 = self_forward(0, x_enc, enc_col, enc_row, enc_gain1, w_qkv, w_out)
    e_slope, e_aslope, e_aact, e_hat2, e_inv2, y_enc = branch_forward(
        0, e_hat1, enc_gain1, enc_gain2, enc_downb, enc_upb, ffn, adapter
    )
    kv = keys_forward(y_enc, w_ckv, w_cvo)
    kv_away = swap(kv, "section")
    d_qkv, d_hat1, d_inv1 = self_forward(1, x_dec, dec_col, dec_row, dec_gain1, w_qkv, w_out)
    d_q, d_hat2, d_inv2 = cross_forward(
        d_hat1, dec_gain1, kv, kv_away, dec_col, all_keys[None, :], w_ckv, w_cvo
    )
    d_slope, d_aslope, d_aact, d_hat3, d_inv3, y_dec = branch_forward(
        1, d_hat2, mid_gain, dec_gain2, dec_downb, dec_upb, ffn, adapter
    )

    d_mid, d_down, d_dbias, d_up, d_ubias = branch_backward(
        1, g_dec, d_hat3, d_inv3, dec_gain2, d_hat2, d_inv2, mid_gain,
        d_slope, d_aslope, d_aact, ffn, adapter,
    )
    d_first, kv_grad, kv_grad_give = cross_backward(
        d_mid, d_hat1, d_inv1, dec_gain1, d_q, kv, kv_away, all_keys[:, None], dec_row, w_ckv, w_cvo
    )
    kv_grad_away = swap(kv_grad_give, "section")
    dx_dec = self_backward(1, d_first, d_qkv, dec_col, dec_row, w_qkv, w_out)
    e_out = keys_backward(g_enc, kv_grad, kv_grad_away, w_ckv, w_cvo)
    e_first, e_down, e_dbias, e_up, e_ubias = branch_backward(
        0, e_out, e_hat2, e_inv2, enc_gain2, e_hat1, e_inv1, enc_gain1,
        e_slope, e_aslope, e_aact, ffn, adapter,
    )
    dx_enc = self_backward(0, e_first, e_qkv, enc_col, enc_row, w_qkv, w_out)

    def gathered(enc, dec):
        mine = jnp.where(first_core, enc, dec).astype(BF16)
        away = jnp.where(first_core, dec, enc).astype(BF16)
        both = mine.astype(F32) + swap(away, "section").astype(F32)
        return both

    def to_side(both):
        return both[0] + swap(both[1].astype(BF16), "mp").astype(F32)

    def over_dp(value):
        return lax.psum(value.astype(BF16), "dp").astype(F32)

    down_total = over_dp(to_side(gathered(e_down, d_down)))
    up_total = over_dp(to_side(gathered(e_up, d_up)))
    dbias_total = over_dp(to_side(gathered(e_dbias, d_dbias)))
    ubias = gathered(e_ubias, d_ubias)
    ubias_total = over_dp(ubias + swap(ubias.astype(BF16), "mp").astype(F32))

    return (
        rows_back(y_enc, y_dec)[None],
        rows_back(dx_enc, dx_dec).astype(F32)[None],
        down_total[None],
        dbias_total,
        up_total[None],
        ubias_total,
    )


def solution(mesh):
    in_specs = (
        P("section", "dp", "mp", None),
        P(None, "dp", None),
        P("section", "dp", "mp", None),
        P("section", None, None),
        P(),
        P("section", None, None, "mp"),
        P("section", "mp", None),
        P("section", None, "mp"),
        P("section", None, "mp"),
        P("section", None, "mp"),
        P("section", "mp", None),
        P("section", None, "mp"),
        P("section", "mp"),
        P("section", "mp", None),
        P("section", None),
    )
    out_specs = (
        P("section", "dp", "mp", None),
        P("section", "dp", "mp", None),
        P("section", None, "mp"),
        P("section", "mp"),
        P("section", "mp", None),
        P("section", None),
    )
    return jax.shard_map(
        per_device, mesh=mesh, in_specs=in_specs, out_specs=out_specs, check_vma=False
    )
```

```python
import functools

import jax
import jax.numpy as jnp
from jax import lax
from jax.experimental import pallas as pl
from jax.experimental.pallas import tpu as pltpu
from jax.sharding import PartitionSpec as P

HEADDIM = 64
BUNCH = 4
WIDE = BUNCH * HEADDIM
CHUNK = 512
SCALE = HEADDIM**-0.5
LANES = 128
PART = 256
EXTRA = 16
HIDDEN_MASK = -1e30
VMEM_LIMIT = 60 * 1024 * 1024
BF16 = jnp.bfloat16
F32 = jnp.float32


def dot_nn(left, right):
    return lax.dot_general(left, right, (((1,), (0,)), ((), ())), preferred_element_type=F32)


def dot_nt(left, right):
    return lax.dot_general(left, right, (((1,), (1,)), ((), ())), preferred_element_type=F32)


def dot_tn(left, right):
    return lax.dot_general(left, right, (((0,), (0,)), ((), ())), preferred_element_type=F32)


class Plan:
    def __init__(self, bufs):
        self.pairs = []
        self.steps = []
        self.bufs = bufs

    def part(self, first, count):
        some = Plan(self.bufs)
        for copies in self.steps[first : first + count]:
            some.steps.append([(some.add(*self.pairs[c[0]]),) + tuple(c[1:]) for c in copies])
        return some

    def add(self, *arrays):
        for i, pair in enumerate(self.pairs):
            if pair[0] is arrays[0]:
                return i
        self.pairs.append(arrays)
        return len(self.pairs) - 1


def at(index):
    return lambda: index


def block(start, size):
    return pl.ds(start, size)


def advance(plan, refs, bufs, sems, layer, step):
    count = len(plan.steps)
    mine = lax.axis_index("section") == layer
    slot = lax.rem(step, 2)

    firsts = [sum(len(p) for p in plan.pairs[:i]) for i in range(len(plan.pairs))]

    def start(copies, side, to):
        for pair, source, buf, place in copies:
            src = refs[firsts[pair] + side].at[source()]
            dst = bufs[buf].at[(to,) + tuple(place())]
            pltpu.make_async_copy(src, dst, sems[buf].at[to]).start()

    def issue(which, to):
        start([c for c in plan.steps[which] if len(plan.pairs[c[0]]) == 1], 0, to)
        layered = [c for c in plan.steps[which] if len(plan.pairs[c[0]]) == 2]
        if layered:

            @pl.when(mine)
            def _():
                start(layered, 0, to)

            @pl.when(jnp.logical_not(mine))
            def _():
                start(layered, 1, to)

    @pl.when(step == 0)
    def _():
        issue(0, 0)

    for which in range(1, count):

        @pl.when(step + 1 == which)
        def _():
            issue(which, which % 2)

    used = [sorted({c[2] for c in copies}) for copies in plan.steps]

    def settle(buf):
        pltpu.make_async_copy(bufs[buf].at[slot], bufs[buf].at[slot], sems[buf].at[slot]).wait()

    first = 0
    for which in range(1, count + 1):
        if which == count or used[which] != used[first]:
            if first == 0 and which == count:
                for buf in used[first]:
                    settle(buf)
            else:

                @pl.when((step >= first) & (step < which))
                def _():
                    for buf in used[first]:
                        settle(buf)

            first = which
    return slot


def call(body, operands, in_blocks, plan, out_shapes, out_blocks, scratch, cost):
    arrays = [a for pair in plan.pairs for a in pair]
    n_ops, n_out, n_buf = len(operands), len(out_shapes), len(plan.bufs)

    def kernel(*refs):
        ins, rest = refs[:n_ops], refs[n_ops:]
        wrefs, rest = rest[: len(arrays)], rest[len(arrays) :]
        outs, rest = rest[:n_out], rest[n_out:]
        bufs, rest = rest[:n_buf], rest[n_buf:]
        sems, extra = rest[:n_buf], rest[n_buf:]
        body(ins, wrefs, outs, bufs, sems, extra)

    return pl.pallas_call(
        kernel,
        grid=(len(plan.steps),),
        in_specs=list(in_blocks) + [pl.BlockSpec(memory_space=pltpu.HBM)] * len(arrays),
        out_specs=tuple(out_blocks),
        out_shape=tuple(out_shapes),
        scratch_shapes=[pltpu.VMEM((2,) + tuple(b), BF16) for b in plan.bufs]
        + [pltpu.SemaphoreType.DMA((2,)) for _ in plan.bufs]
        + list(scratch),
        compiler_params=pltpu.CompilerParams(
            dimension_semantics=("arbitrary",), vmem_limit_bytes=VMEM_LIMIT
        ),
        cost_estimate=pl.CostEstimate(
            flops=int(3 * cost), bytes_accessed=int(cost // 200), transcendentals=0
        ),
    )(*operands, *arrays)


ALL = slice(None)
QUARTER = 128


def self_plan(near, far):
    width = near[0][0].shape[1]
    plan = Plan([(3, width, WIDE), (WIDE, width)])
    qkv, out = plan.add(*near[0]), plan.add(*near[1])
    for g in range(near[0][0].shape[2] // WIDE):
        cols = block(g * WIDE, WIDE)
        plan.steps.append(
            [(qkv, at((ALL, ALL, cols)), 0, at(())), (out, at((cols, ALL)), 1, at(()))]
        )
    for g in range(len(far) // 2):
        copies = []
        for j in range(2):
            first, second, base = far[2 * g + j]
            a, b = plan.add(*first), plan.add(*second)
            lanes = block(j * QUARTER, QUARTER)
            copies.append((a, at((block(0, 2),)), 0, at((block(0, 2), ALL, lanes))))
            copies.append((b, at((base,)), 0, at((2, ALL, lanes))))
            for k in range(width // QUARTER):
                here = block(k * QUARTER, QUARTER)
                copies.append((b, at((base + 1, here, ALL)), 1, at((lanes, here))))
        plan.steps.append(copies)
    return plan


def cross_plan(near, far):
    width = near[0][0].shape[0]
    plan = Plan([(width, WIDE), (width, WIDE)])
    ckv, cvo = plan.add(*near[0]), plan.add(*near[1])
    for g in range(near[0][0].shape[1] // WIDE):
        cols = block(g * WIDE, WIDE)
        plan.steps.append([(ckv, at((ALL, cols)), 0, at(())), (cvo, at((ALL, cols)), 1, at(()))])
    for g in range(len(far) // 2):
        copies = []
        for j in range(2):
            first, second, base = far[2 * g + j]
            a, b = plan.add(*first), plan.add(*second)
            lanes = block(j * QUARTER, QUARTER)
            copies.append((a, at((0,)), 0, at((ALL, lanes))))
            copies.append((b, at((base,)), 1, at((ALL, lanes))))
        plan.steps.append(copies)
    return plan


def branch_plan(near, far, stride):
    width, hidden = near[0][0].shape
    units = near[2][0].shape[1]
    piece = width // 8
    plan = Plan([(width, CHUNK), (CHUNK, width), (width, units), (units, width)])
    up, down, adown, aup = [plan.add(*pair) for pair in near]
    for g in range(hidden // CHUNK):
        cols = block(g * CHUNK, CHUNK)
        plan.steps.append([(up, at((ALL, cols)), 0, at(())), (down, at((cols, ALL)), 1, at(()))])
    adapter = []
    for j, both in enumerate(far):
        copies = []
        for k, (first, second, base) in enumerate(both):
            a, b = plan.add(first), plan.add(second)
            cols = block(k * WIDE, WIDE)
            copies.append((a, at((block(0, width), ALL)), 0, at((ALL, cols))))
            for n in range(width // WIDE):
                rows = block(base + n * WIDE, WIDE)
                copies.append((b, at((rows, ALL)), 1, at((cols, block(n * WIDE, WIDE)))))

            def spot(j=j, k=k):
                return block(pl.multiple_of(eighth_of(j, k, stride) * piece, piece), piece)

            rows = block(base + width, piece)
            adapter.append((b, at((rows, ALL)), 2, lambda spot=spot: (spot(), ALL)))
            for n in range(units // piece):
                rows = block(base + width + piece, piece)
                here = block(n * piece, piece)
                adapter.append(
                    (b, at((rows, here)), 3, lambda spot=spot, here=here: (here, spot()))
                )
        plan.steps.append(copies)
    plan.steps.append([(adown, at(()), 2, at(())), (aup, at(()), 3, at(()))])
    plan.steps.append(adapter)
    return plan


def share_of(j, stride):
    place = lax.axis_index("dp")
    x = lax.rem(place, 2)
    z = lax.rem(lax.div(place, stride), 2)
    x = 1 - x if j in (1, 3) else x
    z = 1 - z if j in (2, 3) else z
    return 2 * x + z


def eighth_of(j, k, stride):
    core = lax.axis_index("section")
    return 4 * (1 - core if k else core) + share_of(j, stride)


def cut_piece(pairs, layer, shape, moves):
    plan = Plan([])
    plan.pairs = pairs
    firsts = [sum(len(p) for p in pairs[:i]) for i in range(len(pairs))]
    arrays = [a for pair in pairs for a in pair]

    def kernel(*refs):
        ins, out, sem = refs[: len(arrays)], refs[-2], refs[-1]

        def start(side):
            for pair, index, place in moves:
                src = ins[firsts[pair] + side].at[index()]
                pltpu.make_async_copy(src, out.at[place()], sem).start()

        if layer is None:
            start(0)
        else:
            mine = lax.axis_index("section") == layer

            @pl.when(mine)
            def _():
                start(0)

            @pl.when(jnp.logical_not(mine))
            def _():
                start(1)

        pltpu.make_async_copy(out, out, sem).wait()

    return pl.pallas_call(
        kernel,
        in_specs=[pl.BlockSpec(memory_space=pltpu.HBM)] * len(arrays),
        out_specs=pl.BlockSpec(memory_space=pltpu.VMEM),
        out_shape=shaped(shape, BF16),
        scratch_shapes=[pltpu.SemaphoreType.DMA],
        compiler_params=pltpu.CompilerParams(vmem_limit_bytes=8 * 1024 * 1024),
    )(*arrays)


def whole(shape):
    zeros = (0,) * len(shape)
    return pl.BlockSpec(tuple(shape), lambda i: zeros)


def per_step(shape, first=0, last=None):
    def index(i):
        k = jnp.maximum(i - first, 0)
        if last is not None:
            k = jnp.minimum(k, last)
        return (k,) + (0,) * len(shape)

    return pl.BlockSpec((1,) + tuple(shape), index)


def shaped(shape, dtype):
    return jax.ShapeDtypeStruct(tuple(shape), dtype)


def normalized(value):
    center = value - jnp.mean(value, -1, keepdims=True)
    spread = jnp.mean(center * center, -1, keepdims=True)
    inverse = lax.rsqrt(spread + 1e-05)
    return center * inverse, inverse


def norm_slope(grad, hat, inverse, gain):
    scaled = grad * gain
    along = jnp.mean(scaled * hat, -1, keepdims=True)
    return inverse * (scaled - jnp.mean(scaled, -1, keepdims=True) - hat * along)


def gelu_pair(value):
    below = 0.5 + 0.5 * lax.erf(value * (0.5**0.5))
    density = jnp.exp(value * value * -0.5) * 0.3989422804014327
    return value * below, below + value * density


def lanes_of(head):
    first = head * HEADDIM // LANES * LANES
    return slice(first, first + LANES)


def only_head(value, head):
    lane = lax.broadcasted_iota(jnp.int32, (1, LANES), 1)
    inside = head * HEADDIM % LANES
    keep = (lane >= inside) & (lane < inside + HEADDIM)
    part = value[:, lanes_of(head)]
    return jnp.where(keep, part, jnp.zeros_like(part))


def attend(blocks, q_ref, k_ref, v_ref, bias_ref, valid_ref, lse_ref, out_ref):
    units = [(rows, keys, head) for rows, keys in blocks for head in range(BUNCH)]

    def scores_of(unit):
        rows, keys, head = unit
        q_head = only_head(q_ref[rows, :] * jnp.asarray(SCALE, BF16), head)
        return dot_nt(k_ref[keys, lanes_of(head)], q_head)

    ahead = scores_of(units[0])
    for i, (rows, keys, head) in enumerate(units):
        scores = ahead + bias_ref[keys, rows]
        if i + 1 < len(units):
            ahead = scores_of(units[i + 1])
        peak = jnp.max(scores, 0, keepdims=True)
        powers = jnp.exp(scores - peak)
        total = jnp.sum(powers, 0, keepdims=True)
        share = 1.0 / total
        lse = peak + jnp.log(total)
        if valid_ref is not None:
            valid = valid_ref[:, rows] > 0.0
            share = jnp.where(valid, share, 0.0)
            lse = jnp.where(valid, lse, -HIDDEN_MASK)
        lse_ref[head : head + 1, rows] = lse
        mixed = dot_tn((powers * share).astype(BF16), only_head(v_ref[keys, :], head))
        out_ref[rows, lanes_of(head)] += mixed


def attend_slope(blocks, q_ref, k_ref, v_ref, g_ref, bias_ref, lse_ref, dq_ref, dk_ref, dv_ref):
    units = [(rows, keys, head) for rows, keys in blocks for head in range(BUNCH)]

    def products_of(unit):
        rows, keys, head = unit
        q_head = only_head(q_ref[rows, :] * jnp.asarray(SCALE, BF16), head)
        g_head = only_head(g_ref[rows, :], head)
        lanes = lanes_of(head)
        return q_head, g_head, dot_nt(k_ref[keys, lanes], q_head), dot_nt(v_ref[keys, lanes], g_head)

    ahead = products_of(units[0])
    for i, (rows, keys, head) in enumerate(units):
        q_head, g_head, scores, prob_grad = ahead
        if i + 1 < len(units):
            ahead = products_of(units[i + 1])
        lanes = lanes_of(head)
        probs = jnp.exp(scores + bias_ref[keys, rows] - lse_ref[head : head + 1, rows])
        inner = jnp.sum(probs * prob_grad, 0, keepdims=True)
        score_grad = (probs * (prob_grad - inner)).astype(BF16)
        dv_ref[keys, lanes] += dot_nn(probs.astype(BF16), g_head)
        dk_ref[keys, lanes] += dot_nn(score_grad, q_head)
        dq_ref[rows, lanes] += dot_tn(score_grad, only_head(k_ref[keys, :], head))


def fill_bias(bias_ref, key_seg, row_seg, causal):
    seen = key_seg == row_seg
    if causal:
        key = lax.broadcasted_iota(jnp.int32, bias_ref.shape, 0)
        row = lax.broadcasted_iota(jnp.int32, bias_ref.shape, 1)
        seen = seen & (key <= row)
    bias_ref[...] = jnp.where(seen, 0.0, HIDDEN_MASK)


def self_blocks(rows, causal):
    count = rows // PART
    parts = [slice(i * PART, (i + 1) * PART) for i in range(count)]
    return [(part, slice(0, part.stop if causal else rows)) for part in parts]


def note_active(bias, valid, active, rows):
    for h in range(2):
        best = jnp.max(bias[h], 0, keepdims=True)
        valid[h] = jnp.where(best > 0.5 * HIDDEN_MASK, 1.0, 0.0)
        for i in range(rows // PART):
            some = jnp.max(valid[h, :, i * PART : (i + 1) * PART])
            active[h, i] = (some > 0.0).astype(jnp.int32)


def self_forward(layer, x, seg_col, seg_row, gain, plan):
    rows, width = x.shape
    steps = len(plan.steps)

    def body(ins, wrefs, outs, bufs, sems, extra):
        x_ref, segc_ref, segr_ref, gain_ref = ins
        qkv_ref, lse_ref, hat_ref, inv_ref = outs
        acc, bias, mixed = extra
        step = pl.program_id(0)
        slot = advance(plan, wrefs, bufs, sems, layer, step)

        @pl.when(step == 0)
        def _():
            fill_bias(bias, segc_ref[...], segr_ref[...], layer == 1)
            acc[...] = x_ref[...].astype(F32)

        x_rows = x_ref[...]
        w = bufs[0].at[slot]
        q = dot_nn(x_rows, w[0]).astype(BF16)
        k = dot_nn(x_rows, w[1]).astype(BF16)
        v = dot_nn(x_rows, w[2]).astype(BF16)
        qkv_ref[0, 0] = q
        qkv_ref[0, 1] = k
        qkv_ref[0, 2] = v
        mixed[...] = jnp.zeros_like(mixed)
        attend(
            self_blocks(rows, layer == 1), qkv_ref.at[0, 0], qkv_ref.at[0, 1], qkv_ref.at[0, 2],
            bias, None, lse_ref.at[0], mixed,
        )
        acc[...] += dot_nn(mixed[...].astype(BF16), bufs[1][slot])

        @pl.when(step == steps - 1)
        def _():
            hat, inverse = normalized(acc[...])
            hat_ref[...] = hat.astype(BF16)
            inv_ref[...] = inverse

    return call(
        body,
        [x, seg_col, seg_row, gain],
        [whole(x.shape), whole(seg_col.shape), whole(seg_row.shape), whole(gain.shape)],
        plan,
        [
            shaped((steps, 3, rows, WIDE), BF16),
            shaped((steps, BUNCH, rows), F32),
            shaped((rows, width), BF16),
            shaped((rows, 1), F32),
        ],
        [
            per_step((3, rows, WIDE)),
            per_step((BUNCH, rows)),
            whole((rows, width)),
            whole((rows, 1)),
        ],
        [
            pltpu.VMEM((rows, width), F32),
            pltpu.VMEM((rows, rows), F32),
            pltpu.VMEM((rows, WIDE), F32),
        ],
        steps * (2 * rows * width * WIDE * 4 + 16 * rows * rows * WIDE),
    )


def self_backward(layer, grad, base, saved, lse, seg_col, seg_row, plan, first, count):
    rows, width = grad.shape
    steps = count
    plan = plan.part(first, count)

    def body(ins, wrefs, outs, bufs, sems, extra):
        g_ref, base_ref, saved_ref, lse_ref, segc_ref, segr_ref = ins
        (dx_ref,) = outs
        acc, bias, mixed_grad, dq, dk, dv = extra
        step = pl.program_id(0)
        slot = advance(plan, wrefs, bufs, sems, layer, step)

        @pl.when(step == 0)
        def _():
            fill_bias(bias, segc_ref[...], segr_ref[...], layer == 1)
            acc[...] = base_ref[...].astype(F32)

        mixed_grad[...] = dot_nt(g_ref[...], bufs[1][slot]).astype(BF16)
        for ref in (dq, dk, dv):
            ref[...] = jnp.zeros_like(ref)
        attend_slope(
            self_blocks(rows, layer == 1), saved_ref.at[0, 0], saved_ref.at[0, 1],
            saved_ref.at[0, 2], mixed_grad, bias, lse_ref.at[0], dq, dk, dv,
        )
        w = bufs[0].at[slot]
        acc[...] += (
            dot_nt((dq[...] * SCALE).astype(BF16), w[0])
            + dot_nt(dk[...].astype(BF16), w[1])
            + dot_nt(dv[...].astype(BF16), w[2])
        )

        @pl.when(step == steps - 1)
        def _():
            dx_ref[...] = acc[...].astype(BF16)

    return call(
        body,
        [grad, base, saved, lse, seg_col, seg_row],
        [
            whole(grad.shape),
            whole(grad.shape),
            per_step((3, rows, WIDE), -first),
            per_step((BUNCH, rows), -first),
            whole(seg_col.shape),
            whole(seg_row.shape),
        ],
        plan,
        [shaped((rows, width), BF16)],
        [whole((rows, width))],
        [
            pltpu.VMEM((rows, width), F32),
            pltpu.VMEM((rows, rows), F32),
            pltpu.VMEM((rows, WIDE), BF16),
            pltpu.VMEM((rows, WIDE), F32),
            pltpu.VMEM((rows, WIDE), F32),
            pltpu.VMEM((rows, WIDE), F32),
        ],
        steps * (2 * rows * width * WIDE * 4 + 40 * rows * rows * WIDE),
    )[0]


def cross_forward(hat, gain, kv_own, kv_away, keys_col, seg_row, plan):
    rows, width = hat.shape
    steps = len(plan.steps)

    def body(ins, wrefs, outs, bufs, sems, extra):
        hat_ref, gain_ref, own_ref, away_ref, keysc_ref, segr_ref = ins
        q_ref, lse_ref, nhat_ref, inv_ref = outs
        acc, low, bias, mixed, valid, active = extra
        step = pl.program_id(0)
        slot = advance(plan, wrefs, bufs, sems, 1, step)

        @pl.when(step == 0)
        def _():
            for h in range(2):
                fill_bias(bias.at[h], keysc_ref[h], segr_ref[...], False)
            note_active(bias, valid, active, rows)
            first = hat_ref[...].astype(F32) * gain_ref[...]
            acc[...] = first
            low[...] = first.astype(BF16)

        q = dot_nn(low[...], bufs[0][slot]).astype(BF16)
        q_ref[0] = q
        mixed[...] = jnp.zeros_like(mixed)
        for h, kv_ref in enumerate((own_ref, away_ref)):
            for i, pair in enumerate(self_blocks(rows, False)):

                @pl.when(active[h, i] > 0)
                def _():
                    attend(
                        [pair], q_ref.at[0], kv_ref.at[0, 0], kv_ref.at[0, 1],
                        bias.at[h], valid.at[h], lse_ref.at[0, h], mixed,
                    )

        acc[...] += dot_nt(mixed[...].astype(BF16), bufs[1][slot])

        @pl.when(step == steps - 1)
        def _():
            nhat, inverse = normalized(acc[...])
            nhat_ref[...] = nhat.astype(BF16)
            inv_ref[...] = inverse

    return call(
        body,
        [hat, gain, kv_own, kv_away, keys_col, seg_row],
        [
            whole(hat.shape),
            whole(gain.shape),
            per_step((2, rows, WIDE)),
            per_step((2, rows, WIDE)),
            whole(keys_col.shape),
            whole(seg_row.shape),
        ],
        plan,
        [
            shaped((steps, rows, WIDE), BF16),
            shaped((steps, 2, BUNCH, rows), F32),
            shaped((rows, width), BF16),
            shaped((rows, 1), F32),
        ],
        [
            per_step((rows, WIDE)),
            per_step((2, BUNCH, rows)),
            whole((rows, width)),
            whole((rows, 1)),
        ],
        [
            pltpu.VMEM((rows, width), F32),
            pltpu.VMEM((rows, width), BF16),
            pltpu.VMEM((2, rows, rows), F32),
            pltpu.VMEM((rows, WIDE), F32),
            pltpu.VMEM((2, 1, rows), F32),
            pltpu.SMEM((2, rows // PART), jnp.int32),
        ],
        steps * (2 * rows * width * WIDE * 2 + 32 * rows * rows * WIDE),
    )


def cross_backward(grad, hat, inv, gain, saved_q, lse, kv_own, kv_away, keys_col, seg_row, plan):
    rows, width = grad.shape
    steps = len(plan.steps)

    def body(ins, wrefs, outs, bufs, sems, extra):
        g_ref, hat_ref, inv_ref, gain_ref, q_ref, lse_ref, own_ref, away_ref, keysc_ref, segr_ref = ins
        dx_ref, own_grad_ref, away_grad_ref = outs
        acc, bias, mixed_grad, dq, dk, dv, valid, active = extra
        step = pl.program_id(0)
        slot = advance(plan, wrefs, bufs, sems, 1, step)

        @pl.when(step == 0)
        def _():
            for h in range(2):
                fill_bias(bias.at[h], keysc_ref[h], segr_ref[...], False)
            note_active(bias, valid, active, rows)
            acc[...] = g_ref[...].astype(F32)

        mixed_grad[...] = dot_nn(g_ref[...], bufs[1][slot]).astype(BF16)
        for ref in (dq, dk, dv):
            ref[...] = jnp.zeros_like(ref)
        for h, kv_ref in enumerate((own_ref, away_ref)):
            for i, pair in enumerate(self_blocks(rows, False)):

                @pl.when(active[h, i] > 0)
                def _():
                    attend_slope(
                        [pair], q_ref.at[0], kv_ref.at[0, 0], kv_ref.at[0, 1], mixed_grad,
                        bias.at[h], lse_ref.at[0, h], dq, dk.at[h], dv.at[h],
                    )

        for h, out_ref in enumerate((own_grad_ref, away_grad_ref)):
            out_ref[0, 0] = dk[h].astype(BF16)
            out_ref[0, 1] = dv[h].astype(BF16)
        acc[...] += dot_nt((dq[...] * SCALE).astype(BF16), bufs[0][slot])

        @pl.when(step == steps - 1)
        def _():
            dx_ref[...] = norm_slope(
                acc[...], hat_ref[...].astype(F32), inv_ref[...], gain_ref[...]
            ).astype(BF16)

    return call(
        body,
        [grad, hat, inv, gain, saved_q, lse, kv_own, kv_away, keys_col, seg_row],
        [
            whole(grad.shape),
            whole(hat.shape),
            whole(inv.shape),
            whole(gain.shape),
            per_step((rows, WIDE)),
            per_step((2, BUNCH, rows)),
            per_step((2, rows, WIDE)),
            per_step((2, rows, WIDE)),
            whole(keys_col.shape),
            whole(seg_row.shape),
        ],
        plan,
        [
            shaped((rows, width), BF16),
            shaped((steps, 2, rows, WIDE), BF16),
            shaped((steps, 2, rows, WIDE), BF16),
        ],
        [whole((rows, width)), per_step((2, rows, WIDE)), per_step((2, rows, WIDE))],
        [
            pltpu.VMEM((rows, width), F32),
            pltpu.VMEM((2, rows, rows), F32),
            pltpu.VMEM((rows, WIDE), BF16),
            pltpu.VMEM((rows, WIDE), F32),
            pltpu.VMEM((2, rows, WIDE), F32),
            pltpu.VMEM((2, rows, WIDE), F32),
            pltpu.VMEM((2, 1, rows), F32),
            pltpu.SMEM((2, rows // PART), jnp.int32),
        ],
        steps * (2 * rows * width * WIDE * 2 + 80 * rows * rows * WIDE),
    )


def keys_forward(y, plan):
    rows, width = y.shape
    steps = len(plan.steps)

    def body(ins, wrefs, outs, bufs, sems, extra):
        (kv_ref,) = outs
        slot = advance(plan, wrefs, bufs, sems, 0, pl.program_id(0))
        kv_ref[0, 0] = dot_nn(ins[0][...], bufs[0][slot]).astype(BF16)
        kv_ref[0, 1] = dot_nn(ins[0][...], bufs[1][slot]).astype(BF16)

    return call(
        body,
        [y],
        [whole(y.shape)],
        plan,
        [shaped((steps, 2, rows, WIDE), BF16)],
        [per_step((2, rows, WIDE))],
        [],
        steps * 4 * rows * width * WIDE,
    )[0]


def keys_backward(out_grad, kv_grad, kv_grad_away, plan):
    rows, width = out_grad.shape
    steps = len(plan.steps)

    def body(ins, wrefs, outs, bufs, sems, extra):
        g_ref, own_ref, away_ref = ins
        (sum_ref,) = outs
        (acc,) = extra
        step = pl.program_id(0)
        slot = advance(plan, wrefs, bufs, sems, 0, step)

        @pl.when(step == 0)
        def _():
            acc[...] = g_ref[...].astype(F32)

        both = (own_ref[0].astype(F32) + away_ref[0].astype(F32)).astype(BF16)
        acc[...] += dot_nt(both[0], bufs[0][slot]) + dot_nt(both[1], bufs[1][slot])

        @pl.when(step == steps - 1)
        def _():
            sum_ref[...] = acc[...].astype(BF16)

    return call(
        body,
        [out_grad, kv_grad, kv_grad_away],
        [whole(out_grad.shape), per_step((2, rows, WIDE)), per_step((2, rows, WIDE))],
        plan,
        [shaped((rows, width), BF16)],
        [whole((rows, width))],
        [pltpu.VMEM((rows, width), F32)],
        steps * 4 * rows * width * WIDE,
    )[0]


def branch_forward(layer, hat, gain, out_gain, down_bias, up_bias, plan):
    rows, width = hat.shape
    nb = 2
    na = len(plan.steps) - nb
    units = down_bias.shape[-1]
    steps = na + nb

    def body(ins, wrefs, outs, bufs, sems, extra):
        hat_ref, gain_ref, ogain_ref, dbias_ref, ubias_ref = ins
        slope_ref, aslope_ref, aact_ref, nhat_ref, inv_ref, y_ref = outs
        acc, low = extra
        step = pl.program_id(0)
        slot = advance(plan, wrefs, bufs, sems, layer, step)

        @pl.when(step == 0)
        def _():
            first = hat_ref[...].astype(F32) * gain_ref[...]
            low[...] = first.astype(BF16)
            acc[...] = first + 4.0 * ubias_ref[...]

        @pl.when(step < na)
        def _():
            for at in range(0, rows, 256):
                part = slice(at, at + 256)
                act, slope = gelu_pair(dot_nn(low[part, :], bufs[0][slot]))
                slope_ref[0, part, :] = slope.astype(BF16)
                acc[part, :] += dot_nn(act.astype(BF16), bufs[1][slot])

        @pl.when(step >= na)
        def _():
            act, slope = gelu_pair(dot_nn(low[...], bufs[2][slot]) + dbias_ref[0])
            low_act = act.astype(BF16)
            aslope_ref[0] = slope.astype(BF16)
            aact_ref[0] = low_act
            acc[...] += dot_nn(low_act * jnp.asarray(4.0, BF16), bufs[3][slot])

        @pl.when(step == steps - 1)
        def _():
            nhat, inverse = normalized(acc[...])
            nhat_ref[...] = nhat.astype(BF16)
            inv_ref[...] = inverse
            y_ref[...] = (nhat * ogain_ref[...]).astype(BF16)

    return call(
        body,
        [hat, gain, out_gain, down_bias, up_bias],
        [
            whole(hat.shape),
            whole(gain.shape),
            whole(out_gain.shape),
            per_step((1, units), na),
            whole(up_bias.shape),
        ],
        plan,
        [
            shaped((na, rows, CHUNK), BF16),
            shaped((nb, rows, units), BF16),
            shaped((nb, rows, units), BF16),
            shaped((rows, width), BF16),
            shaped((rows, 1), F32),
            shaped((rows, width), BF16),
        ],
        [
            per_step((rows, CHUNK), 0, na - 1),
            per_step((rows, units), na),
            per_step((rows, units), na),
            whole((rows, width)),
            whole((rows, 1)),
            whole((rows, width)),
        ],
        [pltpu.VMEM((rows, width), F32), pltpu.VMEM((rows, width), BF16)],
        4 * rows * width * (na * CHUNK + nb * units),
    )


def branch_backward(layer, out_grad, nhat, ninv, out_gain, hat, inv, gain, slope, aslope, aact, plan):
    rows, width = hat.shape
    nb = 2
    na = len(plan.steps) - nb
    units = aact.shape[-1]
    steps = na + nb

    def body(ins, wrefs, outs, bufs, sems, extra):
        g_ref, nhat_ref, ninv_ref, ogain_ref, hat_ref, inv_ref, gain_ref, slope_ref, aslope_ref, aact_ref = ins
        dx_ref, packed_ref = outs
        acc, low, rows_low, up_bias = extra
        step = pl.program_id(0)
        slot = advance(plan, wrefs, bufs, sems, layer, step)

        @pl.when(step == 0)
        def _():
            grad = norm_slope(
                g_ref[...].astype(F32), nhat_ref[...].astype(F32), ninv_ref[...], ogain_ref[...]
            )
            acc[...] = grad
            small = grad.astype(BF16)
            low[...] = small
            up_bias[...] = 4.0 * jnp.sum(small.astype(F32), 0, keepdims=True)
            rows_low[...] = (hat_ref[...].astype(F32) * gain_ref[...]).astype(BF16)

        @pl.when(step < na)
        def _():
            for at in range(0, rows, 256):
                part = slice(at, at + 256)
                hidden = dot_nt(low[part, :], bufs[1][slot]) * slope_ref[0, part, :].astype(F32)
                acc[part, :] += dot_nt(hidden.astype(BF16), bufs[0][slot])

        @pl.when(step >= na)
        def _():
            hidden = 4.0 * dot_nt(low[...], bufs[3][slot]) * aslope_ref[0].astype(F32)
            small = hidden.astype(BF16)
            acc[...] += dot_nt(small, bufs[2][slot])
            down = dot_tn(rows_low[...], small).astype(BF16)
            for n in range(width // units):
                cols = slice(n * units, (n + 1) * units)
                packed_ref[0, 0, :units, cols] = down[cols]
            packed_ref[0, 1, :units] = (4.0 * dot_tn(aact_ref[0], low[...])).astype(BF16)
            bias = jnp.sum(small.astype(F32), 0, keepdims=True)
            bias = jnp.concatenate([bias] + [jnp.zeros_like(bias)] * (width // units - 1), 1)
            row = lax.broadcasted_iota(jnp.int32, (EXTRA, width), 0)
            last = jnp.where(row == 0, bias, jnp.where(row == 1, up_bias[...], 0.0))
            packed_ref[0, 0, units:] = jnp.zeros((EXTRA, width), BF16)
            packed_ref[0, 1, units:] = last.astype(BF16)

        @pl.when(step == steps - 1)
        def _():
            dx_ref[...] = norm_slope(
                acc[...], hat_ref[...].astype(F32), inv_ref[...], gain_ref[...]
            ).astype(BF16)

    return call(
        body,
        [out_grad, nhat, ninv, out_gain, hat, inv, gain, slope, aslope, aact],
        [
            whole(out_grad.shape),
            whole(nhat.shape),
            whole(ninv.shape),
            whole(out_gain.shape),
            whole(hat.shape),
            whole(inv.shape),
            whole(gain.shape),
            per_step((rows, CHUNK), 0, na - 1),
            per_step((rows, units), na),
            per_step((rows, units), na),
        ],
        plan,
        [
            shaped((rows, width), BF16),
            shaped((nb, 2, units + EXTRA, width), BF16),
        ],
        [
            whole((rows, width)),
            per_step((2, units + EXTRA, width), na),
        ],
        [
            pltpu.VMEM((rows, width), F32),
            pltpu.VMEM((rows, width), BF16),
            pltpu.VMEM((rows, width), BF16),
            pltpu.VMEM((1, width), F32),
        ],
        4 * rows * width * (na * CHUNK + nb * units),
    )


class Lane:
    def __init__(self, depth):
        self.depth = depth
        self.sent = []

    def send(self, value, axes, route):
        if len(self.sent) >= self.depth:
            value, _ = lax.optimization_barrier((value, self.sent[-self.depth]))
        got = lax.ppermute(value, axes, route)
        self.sent.append(got)
        return got


MESH_AXES = ("section", "mp", "dp")


def route(axis, flip, core=None):
    sizes = [lax.axis_size(a) for a in MESH_AXES]
    pairs = []
    for s in range(sizes[0]):
        for m in range(sizes[1]):
            for d in range(sizes[2]):
                if core is not None and s != core:
                    continue
                to = [s, m, d]
                to[MESH_AXES.index(axis)] ^= flip
                number = lambda p: (p[0] * sizes[1] + p[1]) * sizes[2] + p[2]
                pairs.append((number((s, m, d)), number(to)))
    return pairs


def after(value, token):
    return lax.optimization_barrier((value, token))[0]


def swap(value, axis):
    return jax.tree.map(lambda a: lax.ppermute(a, axis, [(0, 1), (1, 0)]), value)


def rotated(pieces, start, count):
    return lax.dynamic_slice_in_dim(jnp.concatenate(pieces, 0), start, count, 0)


def per_device(
    inputs,
    segment_ids,
    cotangent,
    norm_gains,
    cross_gain,
    self_qkv,
    self_out,
    cross_kv,
    cross_vo,
    ffn_in,
    ffn_out,
    adapter_down,
    adapter_down_bias,
    adapter_up,
    adapter_up_bias,
):
    core = lax.axis_index("section")
    side = lax.axis_index("mp")
    first_core = core == 0
    seq = segment_ids.shape[2]
    half = seq // 2
    width = inputs.shape[3]
    units = adapter_down.shape[2]

    stride = max(lax.axis_size("dp") // 4, 1)
    lane_y, lane_x, lane_z = Lane(1), Lane(2), Lane(2)

    def over_y(value):
        return lane_y.send(value, MESH_AXES, route("mp", 1))

    def over_x(value):
        return lane_x.send(value, MESH_AXES, route("dp", 1))

    def over_z(value):
        return lane_z.send(value, MESH_AXES, route("dp", stride))

    def near_pairs(*arrays):
        return [(a, swap(a, "section")) for a in arrays]

    def share(j, size):
        return block(pl.multiple_of(share_of(j, stride) * size, size), size)

    def eighth(j, size):
        return block(pl.multiple_of(eighth_of(j, 0, stride) * size, size), size)

    def columns(n, size):
        return block(n * size, size)

    qkv = jnp.transpose(self_qkv[0], (1, 0, 2))
    near_self = near_pairs(qkv, self_out[0])

    def self_piece(j):
        moves = [(0, lambda: (ALL, ALL, share(j, QUARTER)), at((block(0, 3),)))]
        moves += [
            (1, lambda n=n: (share(j, QUARTER), columns(n, QUARTER)), at((3, columns(n, QUARTER))))
            for n in range(width // QUARTER)
        ]
        return cut_piece([(qkv,), (self_out[0],)], None, (4, width, QUARTER), moves)

    piece = width // 8

    def ffn_piece(layer, j):
        moves = [(0, lambda: (ALL, eighth(j, WIDE)), at((block(0, width), ALL)))]
        moves += [
            (1, lambda n=n: (eighth(j, WIDE), columns(n, WIDE)), at((block(width + n * WIDE, WIDE), ALL)))
            for n in range(width // WIDE)
        ]
        moves += [(2, lambda: (eighth(j, piece), ALL), at((block(2 * width, piece), ALL)))]
        moves += [
            (
                3,
                lambda n=n: (columns(n, piece), eighth(j, piece)),
                at((block(2 * width + piece, piece), columns(n, piece))),
            )
            for n in range(units // piece)
        ]
        return cut_piece(near_ffn, layer, (2 * width + 2 * piece, WIDE), moves)

    def cross_piece(j):
        moves = [(n, lambda: (ALL, share(j, QUARTER)), at((n,))) for n in range(2)]
        return cut_piece([(cross_kv[0],), (cross_vo[0],)], None, (2, width, QUARTER), moves)

    def swapped(value):
        return swap(value, "section")

    def quarters(pieces, swaps, base):
        return [((p, q), (p, q), base) for p, q in zip(pieces, swaps)]

    def eighths(pieces, swaps, base):
        return [((p, p, base), (q, q, base)) for p, q in zip(pieces, swaps)]

    def swapped_after(pieces, token):
        return [swapped(after(p, token)) for p in pieces]

    bias_near = adapter_down_bias[0][None]
    bias_far = over_y(bias_near)
    small = jnp.concatenate(
        [
            norm_gains[0],
            adapter_up_bias,
            jnp.concatenate([bias_near, bias_far, jnp.zeros((1, width - 2 * units), F32)], 1),
        ],
        0,
    )
    small_other = swap(small, "section")
    enc_small = jnp.where(first_core, small, small_other)
    dec_small = jnp.where(first_core, small_other, small)

    def small_of(s):
        down_bias = jnp.stack([s[3:4, :units], s[3:4, units : 2 * units]], 0)
        return s[0:1], s[1:2], s[2:3], down_bias

    enc_gain1, enc_gain2, enc_upb, enc_downb = small_of(enc_small)
    dec_gain1, dec_gain2, dec_upb, dec_downb = small_of(dec_small)
    mid_gain = cross_gain[None]

    segs = lax.dynamic_index_in_dim(segment_ids, side, 1, keepdims=False)
    docs = jnp.arange(seq)
    counts = jnp.sum(segs[:, :, None] == docs[None, None, :8], 1)
    largest = jnp.argmax(counts, 1)
    starts = jnp.sum(segs < largest[:, None], 1).astype(jnp.int32)

    def halves_of_seg(seg, start):
        twice = jnp.concatenate([seg, seg], 0)
        mine = lax.dynamic_slice_in_dim(twice, start + half * core, half, 0)
        away = lax.dynamic_slice_in_dim(twice, start + half * (1 - core), half, 0)
        return mine, away

    enc_seg, enc_seg_away = halves_of_seg(segs[0], starts[0])
    dec_seg, _ = halves_of_seg(segs[1], starts[1])
    own_start = jnp.where(first_core, starts[0], starts[1])

    def rows_sent(value, token=None):
        keep = lax.dynamic_index_in_dim(value[0], side, 0, keepdims=False)
        give = lax.dynamic_index_in_dim(value[0], 1 - side, 0, keepdims=False)
        return keep, over_y(give if token is None else after(give, token))

    def rows_here(keep, got):
        start = lax.rem(own_start + seq - half * side, seq)
        ring = (keep, got, keep, got)
        mine = rotated(ring, start + half * core, half)
        away = rotated(ring, lax.rem(start + half * (1 - core), seq), half)
        other = swap(away, "section")
        return jnp.where(first_core, mine, other), jnp.where(first_core, other, mine)

    def slices_back(big, rest, start):
        ring = (big, rest, big, rest)
        keep = rotated(ring, lax.rem(half * side + seq - start, seq), half)
        give = rotated(ring, lax.rem(half * (1 - side) + seq - start, seq), half)
        return keep, give

    def by_row(keep, got):
        return jnp.where(side == 0, jnp.stack([keep, got]), jnp.stack([got, keep]))

    def rows_back(enc, dec):
        mine = jnp.where(first_core, enc, dec)
        away = jnp.where(first_core, dec, enc)
        other = swap(away, "section")
        big = jnp.where(first_core, mine, other)
        rest = jnp.where(first_core, other, mine)
        keep, give = slices_back(big, rest, own_start)
        return by_row(keep, swap(give, "mp"))

    def layer_back(layer, value):
        other = lax.ppermute(value, MESH_AXES, route("section", 1, 1 - layer))
        big, rest = (value, other) if layer == 0 else (other, value)
        keep, give = slices_back(big, rest, starts[layer])
        return by_row(keep, lax.ppermute(give, MESH_AXES, route("mp", 1, layer)))

    x_keep, x_got = rows_sent(inputs)
    near_ffn = near_pairs(ffn_in[0], ffn_out[0], adapter_down[0], adapter_up[0])
    near_cross = near_pairs(cross_kv[0], cross_vo[0])
    near_other = [pair[1] for pair in near_self + near_ffn + near_cross]
    self_0 = over_y(after(self_piece(0), near_other))
    self_3 = over_y(self_piece(3))
    self_1, self_2 = over_x(self_0), over_z(self_0)
    self_swaps = [swapped(p) for p in (self_0, self_1, self_2)]
    self_swaps.append(swapped(after(self_3, (self_1, self_2))))
    cross_0 = over_y(after(cross_piece(0), (self_1, self_2)))
    enc_0 = over_y(ffn_piece(0, 0))
    lane_y.depth = 2
    x_enc, x_dec = rows_here(x_keep, x_got)
    w_self = self_plan(near_self, quarters((self_0, self_1, self_2, self_3), self_swaps, 2))

    enc_col, enc_row = enc_seg[:, None], enc_seg[None, :]
    dec_col, dec_row = dec_seg[:, None], dec_seg[None, :]
    all_keys = jnp.stack([enc_seg, enc_seg_away], 0)[:, :, None]

    e_qkv, e_lse, e_hat1, e_inv1 = self_forward(0, x_enc, enc_col, enc_row, enc_gain1, w_self)
    enc_1, enc_2 = over_x(after(enc_0, e_inv1)), over_z(after(enc_0, e_inv1))
    enc_3 = over_y(after(ffn_piece(0, 3), e_inv1))
    d_qkv, d_lse, d_hat1, d_inv1 = self_forward(
        1, after(x_dec, e_inv1), dec_col, dec_row, dec_gain1, w_self
    )
    enc = (enc_0, enc_1, enc_2, enc_3)
    w_enc = branch_plan(near_ffn, eighths(enc, swapped_after(enc, d_inv1), width), stride)
    cross_1, cross_2 = over_x(after(cross_0, d_inv1)), over_z(after(cross_0, d_inv1))
    cross_3 = over_y(after(cross_piece(3), d_inv1))
    dec_0 = over_y(after(ffn_piece(1, 0), d_inv1))
    e_slope, e_aslope, e_aact, e_hat2, e_inv2, y_enc = branch_forward(
        0, after(e_hat1, d_inv1), enc_gain1, enc_gain2, enc_downb, enc_upb, w_enc
    )
    crosses = (cross_0, cross_1, cross_2, cross_3)
    cross_swaps = swapped_after(crosses, e_inv2)
    w_cross = cross_plan(near_cross, quarters(crosses, cross_swaps, 1))
    dec_3 = over_y(after(ffn_piece(1, 3), e_inv2))
    kv = keys_forward(y_enc, w_cross)
    kv_away = swap(kv, "section")
    dec_1, dec_2 = over_x(after(dec_0, kv)), over_z(after(dec_0, kv))
    d_q, c_lse, d_hat2, d_inv2 = cross_forward(
        d_hat1, dec_gain1, kv, kv_away, all_keys, dec_row, w_cross
    )
    dec = (dec_0, dec_1, dec_2, dec_3)
    w_dec = branch_plan(near_ffn, eighths(dec, swapped_after(dec, d_inv2), width), stride)
    g_keep, g_got = rows_sent(cotangent, d_inv2)
    d_slope, d_aslope, d_aact, d_hat3, d_inv3, y_dec = branch_forward(
        1, d_hat2, mid_gain, dec_gain2, dec_downb, dec_upb, w_dec
    )
    g_enc, g_dec = rows_here(g_keep, g_got)

    def summed_here(grads):
        keep = lax.dynamic_index_in_dim(grads, core, 1, keepdims=False)
        give = lax.dynamic_index_in_dim(grads, 1 - core, 1, keepdims=False)
        return (keep.astype(F32) + swap(give, "section").astype(F32)).astype(BF16)

    def summed_side(both, token):
        got = after(swap(both[1], "mp"), token)
        return (both[0].astype(F32) + got.astype(F32)).astype(BF16)

    def summed_rows(value, over, token):
        for flip in over:
            got = after(lax.ppermute(value, MESH_AXES, route("dp", flip)), token)
            value = (value.astype(F32) + got.astype(F32)).astype(BF16)
        return value

    flips = [1 << i for i in range(lax.axis_size("dp").bit_length() - 1)]
    d_mid, d_grads = branch_backward(
        1, g_dec, d_hat3, d_inv3, dec_gain2, d_hat2, d_inv2, mid_gain,
        d_slope, d_aslope, d_aact, w_dec,
    )
    d_both = summed_here(d_grads)
    d_first, kv_grad, kv_grad_give = cross_backward(
        after(d_mid, d_both), d_hat1, d_inv1, dec_gain1, d_q, c_lse, kv, kv_away, all_keys, dec_row,
        w_cross,
    )
    d_total = summed_side(d_both, d_first)
    kv_grad_away = swap(kv_grad_give, "section")
    e_out = keys_backward(after(g_enc, d_total), kv_grad, kv_grad_away, w_cross)
    e_first, e_grads = branch_backward(
        0, e_out, e_hat2, e_inv2, enc_gain2, e_hat1, e_inv1, enc_gain1,
        e_slope, e_aslope, e_aact, w_enc,
    )
    e_both = summed_here(e_grads)
    d_total = summed_rows(d_total, flips[:1], e_first)
    d_first = after(d_first, e_both)
    bunches = len(w_self.steps) // 2

    def self_part(layer, grad, base, saved, lse, col, row, n):
        return self_backward(
            layer, grad, base, saved, lse, col, row, w_self, n * bunches, bunches
        )

    dx_dec = self_part(1, d_first, d_first, d_qkv, d_lse, dec_col, dec_row, 0)
    e_total = summed_side(e_both, dx_dec)
    d_total = summed_rows(d_total, flips[1:2], dx_dec)
    outputs = rows_back(y_enc, y_dec)
    dx_dec = self_part(1, d_first, after(dx_dec, (e_total, outputs)), d_qkv, d_lse, dec_col, dec_row, 1)
    e_total = summed_rows(e_total, flips[:1], dx_dec)
    d_total = summed_rows(d_total, flips[2:], dx_dec)
    e_first = after(e_first, (dx_dec, e_total))
    dx_enc = self_part(0, e_first, e_first, e_qkv, e_lse, enc_col, enc_row, 0)
    e_total = summed_rows(e_total, flips[1:2], dx_enc)
    dx_dec_back = layer_back(1, dx_dec)
    dx_enc = self_part(
        0, e_first, after(dx_enc, (e_total, d_total, dx_dec_back)), e_qkv, e_lse, enc_col, enc_row, 1
    )
    e_total = summed_rows(e_total, flips[2:], dx_enc)
    dx = jnp.where(first_core, layer_back(0, dx_enc), dx_dec_back)
    mine = jnp.where(first_core, e_total, d_total)
    other = swap(jnp.where(first_core, d_total, e_total), "section")
    down_total = jnp.where(first_core, mine, other)[:units].astype(F32)
    down_total = jnp.transpose(down_total.reshape(units, -1, units), (1, 0, 2)).reshape(width, units)
    up_total = jnp.where(first_core, other, mine).astype(F32)
    dx = jnp.where(first_core, layer_back(0, dx_enc), dx_dec_back)

    return (
        outputs[None],
        dx.astype(F32)[None],
        down_total[None],
        up_total[units : units + 1, :units],
        up_total[:units][None],
        up_total[units + 1 : units + 2],
    )


def solution(mesh):
    in_specs = (
        P("section", "dp", "mp", None),
        P(None, "dp", None),
        P("section", "dp", "mp", None),
        P("section", None, None),
        P(),
        P("section", None, None, "mp"),
        P("section", "mp", None),
        P("section", None, "mp"),
        P("section", None, "mp"),
        P("section", None, "mp"),
        P("section", "mp", None),
        P("section", None, "mp"),
        P("section", "mp"),
        P("section", "mp", None),
        P("section", None),
    )
    out_specs = (
        P("section", "dp", "mp", None),
        P("section", "dp", "mp", None),
        P("section", None, "mp"),
        P("section", "mp"),
        P("section", "mp", None),
        P("section", None),
    )
    return jax.shard_map(
        per_device, mesh=mesh, in_specs=in_specs, out_specs=out_specs, check_vma=False
    )
```

```python
import functools

import jax
import jax.numpy as jnp
from jax import lax
from jax.experimental import pallas as pl
from jax.experimental.pallas import tpu as pltpu
from jax.sharding import PartitionSpec as P

HEADDIM = 64
BUNCH = 4
WIDE = BUNCH * HEADDIM
CHUNK = 1024
SCALE = HEADDIM**-0.5
LANES = 128
PART = 256
EXTRA = 16
HIDDEN_MASK = -1e30
VMEM_LIMIT = 60 * 1024 * 1024
BF16 = jnp.bfloat16
F32 = jnp.float32


def dot_nn(left, right):
    return lax.dot_general(left, right, (((1,), (0,)), ((), ())), preferred_element_type=F32)


def dot_nt(left, right):
    return lax.dot_general(left, right, (((1,), (1,)), ((), ())), preferred_element_type=F32)


def dot_tn(left, right):
    return lax.dot_general(left, right, (((0,), (0,)), ((), ())), preferred_element_type=F32)


class Plan:
    def __init__(self, bufs):
        self.pairs = []
        self.steps = []
        self.bufs = bufs

    def part(self, first, count):
        some = Plan(self.bufs)
        for copies in self.steps[first : first + count]:
            some.steps.append([(some.add(*self.pairs[c[0]]),) + tuple(c[1:]) for c in copies])
        return some

    def add(self, *arrays):
        for i, pair in enumerate(self.pairs):
            if pair[0] is arrays[0]:
                return i
        self.pairs.append(arrays)
        return len(self.pairs) - 1


def at(index):
    return lambda: index


def block(start, size):
    return pl.ds(start, size)


def advance(plan, refs, bufs, sems, layer, step):
    count = len(plan.steps)
    mine = lax.axis_index("section") == layer
    slot = lax.rem(step, 2)

    firsts = [sum(len(p) for p in plan.pairs[:i]) for i in range(len(plan.pairs))]

    def start(copies, side, to):
        for pair, source, buf, place in copies:
            src = refs[firsts[pair] + side].at[source()]
            dst = bufs[buf].at[(to,) + tuple(place())]
            pltpu.make_async_copy(src, dst, sems[buf].at[to]).start()

    def issue(which, to):
        start([c for c in plan.steps[which] if len(plan.pairs[c[0]]) == 1], 0, to)
        layered = [c for c in plan.steps[which] if len(plan.pairs[c[0]]) == 2]
        if layered:

            @pl.when(mine)
            def _():
                start(layered, 0, to)

            @pl.when(jnp.logical_not(mine))
            def _():
                start(layered, 1, to)

    @pl.when(step == 0)
    def _():
        issue(0, 0)

    for which in range(1, count):

        @pl.when(step + 1 == which)
        def _():
            issue(which, which % 2)

    used = [sorted({c[2] for c in copies}) for copies in plan.steps]

    def settle(buf):
        pltpu.make_async_copy(bufs[buf].at[slot], bufs[buf].at[slot], sems[buf].at[slot]).wait()

    first = 0
    for which in range(1, count + 1):
        if which == count or used[which] != used[first]:
            if first == 0 and which == count:
                for buf in used[first]:
                    settle(buf)
            else:

                @pl.when((step >= first) & (step < which))
                def _():
                    for buf in used[first]:
                        settle(buf)

            first = which
    return slot


def call(body, operands, in_blocks, plan, out_shapes, out_blocks, scratch, cost):
    arrays = [a for pair in plan.pairs for a in pair]
    n_ops, n_out, n_buf = len(operands), len(out_shapes), len(plan.bufs)

    def kernel(*refs):
        ins, rest = refs[:n_ops], refs[n_ops:]
        wrefs, rest = rest[: len(arrays)], rest[len(arrays) :]
        outs, rest = rest[:n_out], rest[n_out:]
        bufs, rest = rest[:n_buf], rest[n_buf:]
        sems, extra = rest[:n_buf], rest[n_buf:]
        body(ins, wrefs, outs, bufs, sems, extra)

    return pl.pallas_call(
        kernel,
        grid=(len(plan.steps),),
        in_specs=list(in_blocks) + [pl.BlockSpec(memory_space=pltpu.HBM)] * len(arrays),
        out_specs=tuple(out_blocks),
        out_shape=tuple(out_shapes),
        scratch_shapes=[pltpu.VMEM((2,) + tuple(b), BF16) for b in plan.bufs]
        + [pltpu.SemaphoreType.DMA((2,)) for _ in plan.bufs]
        + list(scratch),
        compiler_params=pltpu.CompilerParams(
            dimension_semantics=("arbitrary",), vmem_limit_bytes=VMEM_LIMIT
        ),
        cost_estimate=pl.CostEstimate(
            flops=int(3 * cost), bytes_accessed=int(cost // 200), transcendentals=0
        ),
    )(*operands, *arrays)


ALL = slice(None)
QUARTER = 128


def self_plan(near, far):
    width = near[0][0].shape[1]
    plan = Plan([(3, width, WIDE), (WIDE, width)])
    qkv, out = plan.add(*near[0]), plan.add(*near[1])
    for g in range(near[0][0].shape[2] // WIDE):
        cols = block(g * WIDE, WIDE)
        plan.steps.append(
            [(qkv, at((ALL, ALL, cols)), 0, at(())), (out, at((cols, ALL)), 1, at(()))]
        )
    for g in range(len(far) // 2):
        copies = []
        for j in range(2):
            first, second, base = far[2 * g + j]
            a, b = plan.add(*first), plan.add(*second)
            lanes = block(j * QUARTER, QUARTER)
            copies.append((a, at((block(0, 2),)), 0, at((block(0, 2), ALL, lanes))))
            copies.append((b, at((base,)), 0, at((2, ALL, lanes))))
            for k in range(width // QUARTER):
                here = block(k * QUARTER, QUARTER)
                copies.append((b, at((base + 1, here, ALL)), 1, at((lanes, here))))
        plan.steps.append(copies)
    return plan


def cross_plan(near, far):
    width = near[0][0].shape[0]
    plan = Plan([(width, WIDE), (width, WIDE)])
    ckv, cvo = plan.add(*near[0]), plan.add(*near[1])
    for g in range(near[0][0].shape[1] // WIDE):
        cols = block(g * WIDE, WIDE)
        plan.steps.append([(ckv, at((ALL, cols)), 0, at(())), (cvo, at((ALL, cols)), 1, at(()))])
    for g in range(len(far) // 2):
        copies = []
        for j in range(2):
            first, second, base = far[2 * g + j]
            a, b = plan.add(*first), plan.add(*second)
            lanes = block(j * QUARTER, QUARTER)
            copies.append((a, at((0,)), 0, at((ALL, lanes))))
            copies.append((b, at((base,)), 1, at((ALL, lanes))))
        plan.steps.append(copies)
    return plan


def branch_plan(near, far, stride):
    width, hidden = near[0][0].shape
    units = near[2][0].shape[1]
    piece = width // 8
    plan = Plan([(width, CHUNK), (CHUNK, width), (width, units), (units, width)])
    up, down, adown, aup = [plan.add(*pair) for pair in near]
    for g in range(hidden // CHUNK):
        cols = block(g * CHUNK, CHUNK)
        plan.steps.append([(up, at((ALL, cols)), 0, at(())), (down, at((cols, ALL)), 1, at(()))])
    adapter = []
    each = CHUNK // (2 * WIDE)
    for j, both in enumerate(far):
        copies = [] if j % each == 0 else copies
        for k, (first, second, base) in enumerate(both):
            a, b = plan.add(first), plan.add(second)
            cols = block((j % each * 2 + k) * WIDE, WIDE)
            copies.append((a, at((block(0, width), ALL)), 0, at((ALL, cols))))
            for n in range(width // WIDE):
                rows = block(base + n * WIDE, WIDE)
                copies.append((b, at((rows, ALL)), 1, at((cols, block(n * WIDE, WIDE)))))

            def spot(j=j, k=k):
                return block(pl.multiple_of(eighth_of(j, k, stride) * piece, piece), piece)

            rows = block(base + width, piece)
            adapter.append((b, at((rows, ALL)), 2, lambda spot=spot: (spot(), ALL)))
            for n in range(units // piece):
                rows = block(base + width + piece, piece)
                here = block(n * piece, piece)
                adapter.append(
                    (b, at((rows, here)), 3, lambda spot=spot, here=here: (here, spot()))
                )
        if j % each == each - 1:
            plan.steps.append(copies)
    plan.steps.append([(adown, at(()), 2, at(())), (aup, at(()), 3, at(()))])
    plan.steps.append(adapter)
    return plan


def share_of(j, stride):
    place = lax.axis_index("dp")
    x = lax.rem(place, 2)
    z = lax.rem(lax.div(place, stride), 2)
    x = 1 - x if j in (1, 3) else x
    z = 1 - z if j in (2, 3) else z
    return 2 * x + z


def eighth_of(j, k, stride):
    core = lax.axis_index("section")
    return 4 * (1 - core if k else core) + share_of(j, stride)


def cut_piece(pairs, layer, shape, moves):
    plan = Plan([])
    plan.pairs = pairs
    firsts = [sum(len(p) for p in pairs[:i]) for i in range(len(pairs))]
    arrays = [a for pair in pairs for a in pair]

    def kernel(*refs):
        ins, out, sem = refs[: len(arrays)], refs[-2], refs[-1]

        def start(side):
            for pair, index, place in moves:
                src = ins[firsts[pair] + side].at[index()]
                pltpu.make_async_copy(src, out.at[place()], sem).start()

        if layer is None:
            start(0)
        else:
            mine = lax.axis_index("section") == layer

            @pl.when(mine)
            def _():
                start(0)

            @pl.when(jnp.logical_not(mine))
            def _():
                start(1)

        pltpu.make_async_copy(out, out, sem).wait()

    return pl.pallas_call(
        kernel,
        in_specs=[pl.BlockSpec(memory_space=pltpu.HBM)] * len(arrays),
        out_specs=pl.BlockSpec(memory_space=pltpu.VMEM),
        out_shape=shaped(shape, BF16),
        scratch_shapes=[pltpu.SemaphoreType.DMA],
        compiler_params=pltpu.CompilerParams(vmem_limit_bytes=8 * 1024 * 1024),
    )(*arrays)


def whole(shape):
    zeros = (0,) * len(shape)
    return pl.BlockSpec(tuple(shape), lambda i: zeros)


def per_step(shape, first=0, last=None):
    def index(i):
        k = jnp.maximum(i - first, 0)
        if last is not None:
            k = jnp.minimum(k, last)
        return (k,) + (0,) * len(shape)

    return pl.BlockSpec((1,) + tuple(shape), index)


def shaped(shape, dtype):
    return jax.ShapeDtypeStruct(tuple(shape), dtype)


def normalized(value):
    center = value - jnp.mean(value, -1, keepdims=True)
    spread = jnp.mean(center * center, -1, keepdims=True)
    inverse = lax.rsqrt(spread + 1e-05)
    return center * inverse, inverse


def norm_slope(grad, hat, inverse, gain):
    scaled = grad * gain
    along = jnp.mean(scaled * hat, -1, keepdims=True)
    return inverse * (scaled - jnp.mean(scaled, -1, keepdims=True) - hat * along)


def gelu_pair(value):
    below = 0.5 + 0.5 * lax.erf(value * (0.5**0.5))
    density = jnp.exp(value * value * -0.5) * 0.3989422804014327
    return value * below, below + value * density


def lanes_of(head):
    first = head * HEADDIM // LANES * LANES
    return slice(first, first + LANES)


def only_head(value, head):
    lane = lax.broadcasted_iota(jnp.int32, (1, LANES), 1)
    inside = head * HEADDIM % LANES
    keep = (lane >= inside) & (lane < inside + HEADDIM)
    part = value[:, lanes_of(head)]
    return jnp.where(keep, part, jnp.zeros_like(part))


def attend(blocks, q_ref, k_ref, v_ref, bias_ref, valid_ref, lse_ref, out_ref):
    units = [(rows, keys, head) for rows, keys in blocks for head in range(BUNCH)]

    def scores_of(unit):
        rows, keys, head = unit
        q_head = only_head(q_ref[rows, :] * jnp.asarray(SCALE, BF16), head)
        return dot_nt(k_ref[keys, lanes_of(head)], q_head)

    ahead = scores_of(units[0])
    for i, (rows, keys, head) in enumerate(units):
        scores = ahead + bias_ref[keys, rows]
        if i + 1 < len(units):
            ahead = scores_of(units[i + 1])
        peak = jnp.max(scores, 0, keepdims=True)
        powers = jnp.exp(scores - peak)
        total = jnp.sum(powers, 0, keepdims=True)
        share = 1.0 / total
        lse = peak + jnp.log(total)
        if valid_ref is not None:
            valid = valid_ref[:, rows] > 0.0
            share = jnp.where(valid, share, 0.0)
            lse = jnp.where(valid, lse, -HIDDEN_MASK)
        lse_ref[head : head + 1, rows] = lse
        mixed = dot_tn((powers * share).astype(BF16), only_head(v_ref[keys, :], head))
        out_ref[rows, lanes_of(head)] += mixed


def attend_slope(blocks, q_ref, k_ref, v_ref, g_ref, bias_ref, lse_ref, dq_ref, dk_ref, dv_ref):
    units = [(rows, keys, head) for rows, keys in blocks for head in range(BUNCH)]

    def products_of(unit):
        rows, keys, head = unit
        q_head = only_head(q_ref[rows, :] * jnp.asarray(SCALE, BF16), head)
        g_head = only_head(g_ref[rows, :], head)
        lanes = lanes_of(head)
        return q_head, g_head, dot_nt(k_ref[keys, lanes], q_head), dot_nt(v_ref[keys, lanes], g_head)

    ahead = products_of(units[0])
    for i, (rows, keys, head) in enumerate(units):
        q_head, g_head, scores, prob_grad = ahead
        if i + 1 < len(units):
            ahead = products_of(units[i + 1])
        lanes = lanes_of(head)
        probs = jnp.exp(scores + bias_ref[keys, rows] - lse_ref[head : head + 1, rows])
        inner = jnp.sum(probs * prob_grad, 0, keepdims=True)
        score_grad = (probs * (prob_grad - inner)).astype(BF16)
        dv_ref[keys, lanes] += dot_nn(probs.astype(BF16), g_head)
        dk_ref[keys, lanes] += dot_nn(score_grad, q_head)
        dq_ref[rows, lanes] += dot_tn(score_grad, only_head(k_ref[keys, :], head))


def fill_bias(bias_ref, key_seg, row_seg, causal):
    seen = key_seg == row_seg
    if causal:
        key = lax.broadcasted_iota(jnp.int32, bias_ref.shape, 0)
        row = lax.broadcasted_iota(jnp.int32, bias_ref.shape, 1)
        seen = seen & (key <= row)
    bias_ref[...] = jnp.where(seen, 0.0, HIDDEN_MASK)


def self_blocks(rows, causal):
    if not causal:
        return [(slice(0, rows), slice(0, rows))]
    count = rows // PART
    parts = [slice(i * PART, (i + 1) * PART) for i in range(count)]
    return [(part, slice(0, part.stop)) for part in parts]


def cross_blocks(rows):
    return [(slice(i, i + PART), slice(0, rows)) for i in range(0, rows, PART)]


def note_active(bias, valid, active, rows):
    for h in range(2):
        best = jnp.max(bias[h], 0, keepdims=True)
        valid[h] = jnp.where(best > 0.5 * HIDDEN_MASK, 1.0, 0.0)
        for i in range(rows // PART):
            some = jnp.max(valid[h, :, i * PART : (i + 1) * PART])
            active[h, i] = (some > 0.0).astype(jnp.int32)


def self_forward(layer, x, seg_col, seg_row, gain, plan):
    rows, width = x.shape
    steps = len(plan.steps)

    def body(ins, wrefs, outs, bufs, sems, extra):
        x_ref, segc_ref, segr_ref, gain_ref = ins
        qkv_ref, lse_ref, hat_ref, inv_ref = outs
        acc, bias, mixed = extra
        step = pl.program_id(0)
        slot = advance(plan, wrefs, bufs, sems, layer, step)

        @pl.when(step == 0)
        def _():
            fill_bias(bias, segc_ref[...], segr_ref[...], layer == 1)
            acc[...] = x_ref[...].astype(F32)

        x_rows = x_ref[...]
        w = bufs[0].at[slot]
        q = dot_nn(x_rows, w[0]).astype(BF16)
        k = dot_nn(x_rows, w[1]).astype(BF16)
        v = dot_nn(x_rows, w[2]).astype(BF16)
        qkv_ref[0, 0] = q
        qkv_ref[0, 1] = k
        qkv_ref[0, 2] = v
        mixed[...] = jnp.zeros_like(mixed)
        attend(
            self_blocks(rows, layer == 1), qkv_ref.at[0, 0], qkv_ref.at[0, 1], qkv_ref.at[0, 2],
            bias, None, lse_ref.at[0], mixed,
        )
        acc[...] += dot_nn(mixed[...].astype(BF16), bufs[1][slot])

        @pl.when(step == steps - 1)
        def _():
            hat, inverse = normalized(acc[...])
            hat_ref[...] = hat.astype(BF16)
            inv_ref[...] = inverse

    return call(
        body,
        [x, seg_col, seg_row, gain],
        [whole(x.shape), whole(seg_col.shape), whole(seg_row.shape), whole(gain.shape)],
        plan,
        [
            shaped((steps, 3, rows, WIDE), BF16),
            shaped((steps, BUNCH, rows), F32),
            shaped((rows, width), BF16),
            shaped((rows, 1), F32),
        ],
        [
            per_step((3, rows, WIDE)),
            per_step((BUNCH, rows)),
            whole((rows, width)),
            whole((rows, 1)),
        ],
        [
            pltpu.VMEM((rows, width), F32),
            pltpu.VMEM((rows, rows), F32),
            pltpu.VMEM((rows, WIDE), F32),
        ],
        steps * (2 * rows * width * WIDE * 4 + 16 * rows * rows * WIDE),
    )


def self_backward(layer, grad, base, saved, lse, seg_col, seg_row, plan, first, count):
    rows, width = grad.shape
    steps = count
    plan = plan.part(first, count)

    def body(ins, wrefs, outs, bufs, sems, extra):
        g_ref, base_ref, saved_ref, lse_ref, segc_ref, segr_ref = ins
        (dx_ref,) = outs
        acc, bias, mixed_grad, dq, dk, dv = extra
        step = pl.program_id(0)
        slot = advance(plan, wrefs, bufs, sems, layer, step)

        @pl.when(step == 0)
        def _():
            fill_bias(bias, segc_ref[...], segr_ref[...], layer == 1)
            acc[...] = base_ref[...].astype(F32)

        mixed_grad[...] = dot_nt(g_ref[...], bufs[1][slot]).astype(BF16)
        for ref in (dq, dk, dv):
            ref[...] = jnp.zeros_like(ref)
        attend_slope(
            self_blocks(rows, layer == 1), saved_ref.at[0, 0], saved_ref.at[0, 1],
            saved_ref.at[0, 2], mixed_grad, bias, lse_ref.at[0], dq, dk, dv,
        )
        w = bufs[0].at[slot]
        acc[...] += (
            dot_nt((dq[...] * SCALE).astype(BF16), w[0])
            + dot_nt(dk[...].astype(BF16), w[1])
            + dot_nt(dv[...].astype(BF16), w[2])
        )

        @pl.when(step == steps - 1)
        def _():
            dx_ref[...] = acc[...].astype(BF16)

    return call(
        body,
        [grad, base, saved, lse, seg_col, seg_row],
        [
            whole(grad.shape),
            whole(grad.shape),
            per_step((3, rows, WIDE), -first),
            per_step((BUNCH, rows), -first),
            whole(seg_col.shape),
            whole(seg_row.shape),
        ],
        plan,
        [shaped((rows, width), BF16)],
        [whole((rows, width))],
        [
            pltpu.VMEM((rows, width), F32),
            pltpu.VMEM((rows, rows), F32),
            pltpu.VMEM((rows, WIDE), BF16),
            pltpu.VMEM((rows, WIDE), F32),
            pltpu.VMEM((rows, WIDE), F32),
            pltpu.VMEM((rows, WIDE), F32),
        ],
        steps * (2 * rows * width * WIDE * 4 + 40 * rows * rows * WIDE),
    )[0]


def cross_forward(hat, gain, kv_own, kv_away, keys_col, seg_row, plan):
    rows, width = hat.shape
    steps = len(plan.steps)

    def body(ins, wrefs, outs, bufs, sems, extra):
        hat_ref, gain_ref, own_ref, away_ref, keysc_ref, segr_ref = ins
        q_ref, lse_ref, nhat_ref, inv_ref = outs
        acc, low, bias, mixed, valid, active = extra
        step = pl.program_id(0)
        slot = advance(plan, wrefs, bufs, sems, 1, step)

        @pl.when(step == 0)
        def _():
            for h in range(2):
                fill_bias(bias.at[h], keysc_ref[h], segr_ref[...], False)
            note_active(bias, valid, active, rows)
            first = hat_ref[...].astype(F32) * gain_ref[...]
            acc[...] = first
            low[...] = first.astype(BF16)

        q = dot_nn(low[...], bufs[0][slot]).astype(BF16)
        q_ref[0] = q
        mixed[...] = jnp.zeros_like(mixed)
        for h, kv_ref in enumerate((own_ref, away_ref)):
            for i, pair in enumerate(cross_blocks(rows)):

                @pl.when(active[h, i] > 0)
                def _():
                    attend(
                        [pair], q_ref.at[0], kv_ref.at[0, 0], kv_ref.at[0, 1],
                        bias.at[h], valid.at[h], lse_ref.at[0, h], mixed,
                    )

        acc[...] += dot_nt(mixed[...].astype(BF16), bufs[1][slot])

        @pl.when(step == steps - 1)
        def _():
            nhat, inverse = normalized(acc[...])
            nhat_ref[...] = nhat.astype(BF16)
            inv_ref[...] = inverse

    return call(
        body,
        [hat, gain, kv_own, kv_away, keys_col, seg_row],
        [
            whole(hat.shape),
            whole(gain.shape),
            per_step((2, rows, WIDE)),
            per_step((2, rows, WIDE)),
            whole(keys_col.shape),
            whole(seg_row.shape),
        ],
        plan,
        [
            shaped((steps, rows, WIDE), BF16),
            shaped((steps, 2, BUNCH, rows), F32),
            shaped((rows, width), BF16),
            shaped((rows, 1), F32),
        ],
        [
            per_step((rows, WIDE)),
            per_step((2, BUNCH, rows)),
            whole((rows, width)),
            whole((rows, 1)),
        ],
        [
            pltpu.VMEM((rows, width), F32),
            pltpu.VMEM((rows, width), BF16),
            pltpu.VMEM((2, rows, rows), F32),
            pltpu.VMEM((rows, WIDE), F32),
            pltpu.VMEM((2, 1, rows), F32),
            pltpu.SMEM((2, rows // PART), jnp.int32),
        ],
        steps * (2 * rows * width * WIDE * 2 + 32 * rows * rows * WIDE),
    )


def cross_backward(grad, hat, inv, gain, saved_q, lse, kv_own, kv_away, keys_col, seg_row, plan):
    rows, width = grad.shape
    steps = len(plan.steps)

    def body(ins, wrefs, outs, bufs, sems, extra):
        g_ref, hat_ref, inv_ref, gain_ref, q_ref, lse_ref, own_ref, away_ref, keysc_ref, segr_ref = ins
        dx_ref, own_grad_ref, away_grad_ref = outs
        acc, bias, mixed_grad, dq, dk, dv, valid, active = extra
        step = pl.program_id(0)
        slot = advance(plan, wrefs, bufs, sems, 1, step)

        @pl.when(step == 0)
        def _():
            for h in range(2):
                fill_bias(bias.at[h], keysc_ref[h], segr_ref[...], False)
            note_active(bias, valid, active, rows)
            acc[...] = g_ref[...].astype(F32)

        mixed_grad[...] = dot_nn(g_ref[...], bufs[1][slot]).astype(BF16)
        for ref in (dq, dk, dv):
            ref[...] = jnp.zeros_like(ref)
        for h, kv_ref in enumerate((own_ref, away_ref)):
            for i, pair in enumerate(cross_blocks(rows)):

                @pl.when(active[h, i] > 0)
                def _():
                    attend_slope(
                        [pair], q_ref.at[0], kv_ref.at[0, 0], kv_ref.at[0, 1], mixed_grad,
                        bias.at[h], lse_ref.at[0, h], dq, dk.at[h], dv.at[h],
                    )

        for h, out_ref in enumerate((own_grad_ref, away_grad_ref)):
            out_ref[0, 0] = dk[h].astype(BF16)
            out_ref[0, 1] = dv[h].astype(BF16)
        acc[...] += dot_nt((dq[...] * SCALE).astype(BF16), bufs[0][slot])

        @pl.when(step == steps - 1)
        def _():
            dx_ref[...] = norm_slope(
                acc[...], hat_ref[...].astype(F32), inv_ref[...], gain_ref[...]
            ).astype(BF16)

    return call(
        body,
        [grad, hat, inv, gain, saved_q, lse, kv_own, kv_away, keys_col, seg_row],
        [
            whole(grad.shape),
            whole(hat.shape),
            whole(inv.shape),
            whole(gain.shape),
            per_step((rows, WIDE)),
            per_step((2, BUNCH, rows)),
            per_step((2, rows, WIDE)),
            per_step((2, rows, WIDE)),
            whole(keys_col.shape),
            whole(seg_row.shape),
        ],
        plan,
        [
            shaped((rows, width), BF16),
            shaped((steps, 2, rows, WIDE), BF16),
            shaped((steps, 2, rows, WIDE), BF16),
        ],
        [whole((rows, width)), per_step((2, rows, WIDE)), per_step((2, rows, WIDE))],
        [
            pltpu.VMEM((rows, width), F32),
            pltpu.VMEM((2, rows, rows), F32),
            pltpu.VMEM((rows, WIDE), BF16),
            pltpu.VMEM((rows, WIDE), F32),
            pltpu.VMEM((2, rows, WIDE), F32),
            pltpu.VMEM((2, rows, WIDE), F32),
            pltpu.VMEM((2, 1, rows), F32),
            pltpu.SMEM((2, rows // PART), jnp.int32),
        ],
        steps * (2 * rows * width * WIDE * 2 + 80 * rows * rows * WIDE),
    )


def keys_forward(y, plan):
    rows, width = y.shape
    steps = len(plan.steps)

    def body(ins, wrefs, outs, bufs, sems, extra):
        (kv_ref,) = outs
        slot = advance(plan, wrefs, bufs, sems, 0, pl.program_id(0))
        kv_ref[0, 0] = dot_nn(ins[0][...], bufs[0][slot]).astype(BF16)
        kv_ref[0, 1] = dot_nn(ins[0][...], bufs[1][slot]).astype(BF16)

    return call(
        body,
        [y],
        [whole(y.shape)],
        plan,
        [shaped((steps, 2, rows, WIDE), BF16)],
        [per_step((2, rows, WIDE))],
        [],
        steps * 4 * rows * width * WIDE,
    )[0]


def keys_backward(out_grad, kv_grad, kv_grad_away, plan):
    rows, width = out_grad.shape
    steps = len(plan.steps)

    def body(ins, wrefs, outs, bufs, sems, extra):
        g_ref, own_ref, away_ref = ins
        (sum_ref,) = outs
        (acc,) = extra
        step = pl.program_id(0)
        slot = advance(plan, wrefs, bufs, sems, 0, step)

        @pl.when(step == 0)
        def _():
            acc[...] = g_ref[...].astype(F32)

        both = (own_ref[0].astype(F32) + away_ref[0].astype(F32)).astype(BF16)
        acc[...] += dot_nt(both[0], bufs[0][slot]) + dot_nt(both[1], bufs[1][slot])

        @pl.when(step == steps - 1)
        def _():
            sum_ref[...] = acc[...].astype(BF16)

    return call(
        body,
        [out_grad, kv_grad, kv_grad_away],
        [whole(out_grad.shape), per_step((2, rows, WIDE)), per_step((2, rows, WIDE))],
        plan,
        [shaped((rows, width), BF16)],
        [whole((rows, width))],
        [pltpu.VMEM((rows, width), F32)],
        steps * 4 * rows * width * WIDE,
    )[0]


def branch_forward(layer, hat, gain, out_gain, down_bias, up_bias, plan):
    rows, width = hat.shape
    nb = 2
    na = len(plan.steps) - nb
    units = down_bias.shape[-1]
    steps = na + nb

    def body(ins, wrefs, outs, bufs, sems, extra):
        hat_ref, gain_ref, ogain_ref, dbias_ref, ubias_ref = ins
        slope_ref, aslope_ref, aact_ref, nhat_ref, inv_ref, y_ref = outs
        acc, low = extra
        step = pl.program_id(0)
        slot = advance(plan, wrefs, bufs, sems, layer, step)

        @pl.when(step == 0)
        def _():
            first = hat_ref[...].astype(F32) * gain_ref[...]
            low[...] = first.astype(BF16)
            acc[...] = first + 4.0 * ubias_ref[...]

        @pl.when(step < na)
        def _():
            for at in range(0, rows, 512):
                part = slice(at, at + 512)
                act, slope = gelu_pair(dot_nn(low[part, :], bufs[0][slot]))
                slope_ref[0, part, :] = slope.astype(BF16)
                acc[part, :] += dot_nn(act.astype(BF16), bufs[1][slot])

        @pl.when(step >= na)
        def _():
            act, slope = gelu_pair(dot_nn(low[...], bufs[2][slot]) + dbias_ref[0])
            low_act = act.astype(BF16)
            aslope_ref[0] = slope.astype(BF16)
            aact_ref[0] = low_act
            acc[...] += dot_nn(low_act * jnp.asarray(4.0, BF16), bufs[3][slot])

        @pl.when(step == steps - 1)
        def _():
            nhat, inverse = normalized(acc[...])
            nhat_ref[...] = nhat.astype(BF16)
            inv_ref[...] = inverse
            y_ref[...] = (nhat * ogain_ref[...]).astype(BF16)

    return call(
        body,
        [hat, gain, out_gain, down_bias, up_bias],
        [
            whole(hat.shape),
            whole(gain.shape),
            whole(out_gain.shape),
            per_step((1, units), na),
            whole(up_bias.shape),
        ],
        plan,
        [
            shaped((na, rows, CHUNK), BF16),
            shaped((nb, rows, units), BF16),
            shaped((nb, rows, units), BF16),
            shaped((rows, width), BF16),
            shaped((rows, 1), F32),
            shaped((rows, width), BF16),
        ],
        [
            per_step((rows, CHUNK), 0, na - 1),
            per_step((rows, units), na),
            per_step((rows, units), na),
            whole((rows, width)),
            whole((rows, 1)),
            whole((rows, width)),
        ],
        [pltpu.VMEM((rows, width), F32), pltpu.VMEM((rows, width), BF16)],
        4 * rows * width * (na * CHUNK + nb * units),
    )


def branch_backward(layer, out_grad, nhat, ninv, out_gain, hat, inv, gain, slope, aslope, aact, plan):
    rows, width = hat.shape
    nb = 2
    na = len(plan.steps) - nb
    units = aact.shape[-1]
    steps = na + nb

    def body(ins, wrefs, outs, bufs, sems, extra):
        g_ref, nhat_ref, ninv_ref, ogain_ref, hat_ref, inv_ref, gain_ref, slope_ref, aslope_ref, aact_ref = ins
        dx_ref, packed_ref = outs
        acc, low, rows_low, up_bias = extra
        step = pl.program_id(0)
        slot = advance(plan, wrefs, bufs, sems, layer, step)

        @pl.when(step == 0)
        def _():
            grad = norm_slope(
                g_ref[...].astype(F32), nhat_ref[...].astype(F32), ninv_ref[...], ogain_ref[...]
            )
            acc[...] = grad
            small = grad.astype(BF16)
            low[...] = small
            up_bias[...] = 4.0 * jnp.sum(small.astype(F32), 0, keepdims=True)
            rows_low[...] = (hat_ref[...].astype(F32) * gain_ref[...]).astype(BF16)

        @pl.when(step < na)
        def _():
            for at in range(0, rows, 512):
                part = slice(at, at + 512)
                hidden = dot_nt(low[part, :], bufs[1][slot]) * slope_ref[0, part, :].astype(F32)
                acc[part, :] += dot_nt(hidden.astype(BF16), bufs[0][slot])

        @pl.when(step >= na)
        def _():
            hidden = 4.0 * dot_nt(low[...], bufs[3][slot]) * aslope_ref[0].astype(F32)
            small = hidden.astype(BF16)
            acc[...] += dot_nt(small, bufs[2][slot])
            down = dot_tn(rows_low[...], small).astype(BF16)
            for n in range(width // units):
                cols = slice(n * units, (n + 1) * units)
                packed_ref[0, 0, :units, cols] = down[cols]
            packed_ref[0, 1, :units] = (4.0 * dot_tn(aact_ref[0], low[...])).astype(BF16)
            bias = jnp.sum(small.astype(F32), 0, keepdims=True)
            bias = jnp.concatenate([bias] + [jnp.zeros_like(bias)] * (width // units - 1), 1)
            row = lax.broadcasted_iota(jnp.int32, (EXTRA, width), 0)
            last = jnp.where(row == 0, bias, jnp.where(row == 1, up_bias[...], 0.0))
            packed_ref[0, 0, units:] = jnp.zeros((EXTRA, width), BF16)
            packed_ref[0, 1, units:] = last.astype(BF16)

        @pl.when(step == steps - 1)
        def _():
            dx_ref[...] = norm_slope(
                acc[...], hat_ref[...].astype(F32), inv_ref[...], gain_ref[...]
            ).astype(BF16)

    return call(
        body,
        [out_grad, nhat, ninv, out_gain, hat, inv, gain, slope, aslope, aact],
        [
            whole(out_grad.shape),
            whole(nhat.shape),
            whole(ninv.shape),
            whole(out_gain.shape),
            whole(hat.shape),
            whole(inv.shape),
            whole(gain.shape),
            per_step((rows, CHUNK), 0, na - 1),
            per_step((rows, units), na),
            per_step((rows, units), na),
        ],
        plan,
        [
            shaped((rows, width), BF16),
            shaped((nb, 2, units + EXTRA, width), BF16),
        ],
        [
            whole((rows, width)),
            per_step((2, units + EXTRA, width), na),
        ],
        [
            pltpu.VMEM((rows, width), F32),
            pltpu.VMEM((rows, width), BF16),
            pltpu.VMEM((rows, width), BF16),
            pltpu.VMEM((1, width), F32),
        ],
        4 * rows * width * (na * CHUNK + nb * units),
    )


class Lane:
    def __init__(self, depth):
        self.depth = depth
        self.sent = []

    def send(self, value, axes, route):
        if len(self.sent) >= self.depth:
            value, _ = lax.optimization_barrier((value, self.sent[-self.depth]))
        got = lax.ppermute(value, axes, route)
        self.sent.append(got)
        return got


MESH_AXES = ("section", "mp", "dp")


def route(axis, flip, core=None):
    sizes = [lax.axis_size(a) for a in MESH_AXES]
    pairs = []
    for s in range(sizes[0]):
        for m in range(sizes[1]):
            for d in range(sizes[2]):
                if core is not None and s != core:
                    continue
                to = [s, m, d]
                to[MESH_AXES.index(axis)] ^= flip
                number = lambda p: (p[0] * sizes[1] + p[1]) * sizes[2] + p[2]
                pairs.append((number((s, m, d)), number(to)))
    return pairs


def after(value, token):
    return lax.optimization_barrier((value, token))[0]


def swap(value, axis):
    return jax.tree.map(lambda a: lax.ppermute(a, axis, [(0, 1), (1, 0)]), value)


def rotated(pieces, start, count):
    return lax.dynamic_slice_in_dim(jnp.concatenate(pieces, 0), start, count, 0)


def per_device(
    inputs,
    segment_ids,
    cotangent,
    norm_gains,
    cross_gain,
    self_qkv,
    self_out,
    cross_kv,
    cross_vo,
    ffn_in,
    ffn_out,
    adapter_down,
    adapter_down_bias,
    adapter_up,
    adapter_up_bias,
):
    core = lax.axis_index("section")
    side = lax.axis_index("mp")
    first_core = core == 0
    seq = segment_ids.shape[2]
    half = seq // 2
    width = inputs.shape[3]
    units = adapter_down.shape[2]

    stride = max(lax.axis_size("dp") // 4, 1)
    lane_y, lane_x, lane_z, lane_core = Lane(1), Lane(2), Lane(2), Lane(3)

    def over_y(value):
        return lane_y.send(value, MESH_AXES, route("mp", 1))

    def over_x(value):
        return lane_x.send(value, MESH_AXES, route("dp", 1))

    def over_z(value):
        return lane_z.send(value, MESH_AXES, route("dp", stride))

    def near_pairs(*arrays):
        return [(a, lane_core.send(a, MESH_AXES, route("section", 1))) for a in arrays]

    def share(j, size):
        return block(pl.multiple_of(share_of(j, stride) * size, size), size)

    def eighth(j, size):
        return block(pl.multiple_of(eighth_of(j, 0, stride) * size, size), size)

    def columns(n, size):
        return block(n * size, size)

    qkv = jnp.transpose(self_qkv[0], (1, 0, 2))
    near_self = near_pairs(qkv, self_out[0])

    def self_piece(j):
        moves = [(0, lambda: (ALL, ALL, share(j, QUARTER)), at((block(0, 3),)))]
        moves += [
            (1, lambda n=n: (share(j, QUARTER), columns(n, QUARTER)), at((3, columns(n, QUARTER))))
            for n in range(width // QUARTER)
        ]
        return cut_piece([(qkv,), (self_out[0],)], None, (4, width, QUARTER), moves)

    piece = width // 8

    def ffn_piece(layer, j):
        moves = [(0, lambda: (ALL, eighth(j, WIDE)), at((block(0, width), ALL)))]
        moves += [
            (1, lambda n=n: (eighth(j, WIDE), columns(n, WIDE)), at((block(width + n * WIDE, WIDE), ALL)))
            for n in range(width // WIDE)
        ]
        moves += [(2, lambda: (eighth(j, piece), ALL), at((block(2 * width, piece), ALL)))]
        moves += [
            (
                3,
                lambda n=n: (columns(n, piece), eighth(j, piece)),
                at((block(2 * width + piece, piece), columns(n, piece))),
            )
            for n in range(units // piece)
        ]
        return cut_piece(near_ffn, layer, (2 * width + 2 * piece, WIDE), moves)

    def cross_piece(j):
        moves = [(n, lambda: (ALL, share(j, QUARTER)), at((n,))) for n in range(2)]
        return cut_piece([(cross_kv[0],), (cross_vo[0],)], None, (2, width, QUARTER), moves)

    def swapped(value):
        return swap(value, "section")

    def quarters(pieces, swaps, base):
        return [((p, q), (p, q), base) for p, q in zip(pieces, swaps)]

    def eighths(pieces, swaps, base):
        return [((p, p, base), (q, q, base)) for p, q in zip(pieces, swaps)]

    def swapped_after(pieces, token):
        return [swapped(after(p, token)) for p in pieces]

    bias_near = adapter_down_bias[0][None]
    bias_far = over_y(bias_near)
    small = jnp.concatenate(
        [
            norm_gains[0],
            adapter_up_bias,
            jnp.concatenate([bias_near, bias_far, jnp.zeros((1, width - 2 * units), F32)], 1),
        ],
        0,
    )
    small_other = swap(small, "section")
    enc_small = jnp.where(first_core, small, small_other)
    dec_small = jnp.where(first_core, small_other, small)

    def small_of(s):
        down_bias = jnp.stack([s[3:4, :units], s[3:4, units : 2 * units]], 0)
        return s[0:1], s[1:2], s[2:3], down_bias

    enc_gain1, enc_gain2, enc_upb, enc_downb = small_of(enc_small)
    dec_gain1, dec_gain2, dec_upb, dec_downb = small_of(dec_small)
    mid_gain = cross_gain[None]

    segs = lax.dynamic_index_in_dim(segment_ids, side, 1, keepdims=False)
    docs = jnp.arange(seq)
    counts = jnp.sum(segs[:, :, None] == docs[None, None, :8], 1)
    largest = jnp.argmax(counts, 1)
    starts = jnp.sum(segs < largest[:, None], 1).astype(jnp.int32)

    def halves_of_seg(seg, start):
        twice = jnp.concatenate([seg, seg], 0)
        mine = lax.dynamic_slice_in_dim(twice, start + half * core, half, 0)
        away = lax.dynamic_slice_in_dim(twice, start + half * (1 - core), half, 0)
        return mine, away

    enc_seg, enc_seg_away = halves_of_seg(segs[0], starts[0])
    dec_seg, _ = halves_of_seg(segs[1], starts[1])
    own_start = jnp.where(first_core, starts[0], starts[1])

    def rows_sent(value, token=None):
        keep = lax.dynamic_index_in_dim(value[0], side, 0, keepdims=False)
        give = lax.dynamic_index_in_dim(value[0], 1 - side, 0, keepdims=False)
        return keep, over_y(give if token is None else after(give, token))

    def rows_here(keep, got):
        start = lax.rem(own_start + seq - half * side, seq)
        ring = (keep, got, keep, got)
        mine = rotated(ring, start + half * core, half)
        away = rotated(ring, lax.rem(start + half * (1 - core), seq), half)
        other = swap(away, "section")
        return jnp.where(first_core, mine, other), jnp.where(first_core, other, mine)

    def slices_back(big, rest, start):
        ring = (big, rest, big, rest)
        keep = rotated(ring, lax.rem(half * side + seq - start, seq), half)
        give = rotated(ring, lax.rem(half * (1 - side) + seq - start, seq), half)
        return keep, give

    def by_row(keep, got):
        return jnp.where(side == 0, jnp.stack([keep, got]), jnp.stack([got, keep]))

    def rows_back(enc, dec):
        mine = jnp.where(first_core, enc, dec)
        away = jnp.where(first_core, dec, enc)
        other = swap(away, "section")
        big = jnp.where(first_core, mine, other)
        rest = jnp.where(first_core, other, mine)
        keep, give = slices_back(big, rest, own_start)
        return by_row(keep, swap(give, "mp"))

    def layer_back(layer, value):
        other = lax.ppermute(value, MESH_AXES, route("section", 1, 1 - layer))
        big, rest = (value, other) if layer == 0 else (other, value)
        keep, give = slices_back(big, rest, starts[layer])
        return by_row(keep, lax.ppermute(give, MESH_AXES, route("mp", 1, layer)))

    x_keep, x_got = rows_sent(inputs)
    near_ffn = near_pairs(ffn_in[0], ffn_out[0], adapter_down[0], adapter_up[0])
    near_cross = near_pairs(cross_kv[0], cross_vo[0])
    near_other = [pair[1] for pair in near_self + near_ffn + near_cross]
    self_0 = over_y(after(self_piece(0), near_other))
    self_3 = over_y(self_piece(3))
    self_1, self_2 = over_x(self_0), over_z(self_0)
    self_swaps = [swapped(p) for p in (self_0, self_1, self_2)]
    self_swaps.append(swapped(after(self_3, (self_1, self_2))))
    cross_0 = over_y(after(cross_piece(0), (self_1, self_2)))
    enc_0 = over_y(ffn_piece(0, 0))
    lane_y.depth = 2
    x_enc, x_dec = rows_here(x_keep, x_got)
    w_self = self_plan(near_self, quarters((self_0, self_1, self_2, self_3), self_swaps, 2))

    enc_col, enc_row = enc_seg[:, None], enc_seg[None, :]
    dec_col, dec_row = dec_seg[:, None], dec_seg[None, :]
    all_keys = jnp.stack([enc_seg, enc_seg_away], 0)[:, :, None]

    e_qkv, e_lse, e_hat1, e_inv1 = self_forward(0, x_enc, enc_col, enc_row, enc_gain1, w_self)
    enc_1, enc_2 = over_x(after(enc_0, e_inv1)), over_z(after(enc_0, e_inv1))
    enc_3 = over_y(after(ffn_piece(0, 3), e_inv1))
    d_qkv, d_lse, d_hat1, d_inv1 = self_forward(
        1, after(x_dec, e_inv1), dec_col, dec_row, dec_gain1, w_self
    )
    enc = (enc_0, enc_1, enc_2, enc_3)
    w_enc = branch_plan(near_ffn, eighths(enc, swapped_after(enc, d_inv1), width), stride)
    cross_1, cross_2 = over_x(after(cross_0, d_inv1)), over_z(after(cross_0, d_inv1))
    cross_3 = over_y(after(cross_piece(3), d_inv1))
    dec_0 = over_y(after(ffn_piece(1, 0), d_inv1))
    e_slope, e_aslope, e_aact, e_hat2, e_inv2, y_enc = branch_forward(
        0, after(e_hat1, d_inv1), enc_gain1, enc_gain2, enc_downb, enc_upb, w_enc
    )
    crosses = (cross_0, cross_1, cross_2, cross_3)
    cross_swaps = swapped_after(crosses, e_inv2)
    w_cross = cross_plan(near_cross, quarters(crosses, cross_swaps, 1))
    dec_3 = over_y(after(ffn_piece(1, 3), e_inv2))
    kv = keys_forward(after(y_enc, dec_0), w_cross)
    kv_away = swap(kv, "section")
    dec_1, dec_2 = over_x(after(dec_0, kv)), over_z(after(dec_0, kv))
    d_q, c_lse, d_hat2, d_inv2 = cross_forward(
        d_hat1, dec_gain1, kv, kv_away, all_keys, dec_row, w_cross
    )
    dec = (dec_0, dec_1, dec_2, dec_3)
    w_dec = branch_plan(near_ffn, eighths(dec, swapped_after(dec, d_inv2), width), stride)
    g_keep, g_got = rows_sent(cotangent, d_inv2)
    d_slope, d_aslope, d_aact, d_hat3, d_inv3, y_dec = branch_forward(
        1, d_hat2, mid_gain, dec_gain2, dec_downb, dec_upb, w_dec
    )
    g_enc, g_dec = rows_here(g_keep, g_got)

    def summed_here(grads):
        keep = lax.dynamic_index_in_dim(grads, core, 1, keepdims=False)
        give = lax.dynamic_index_in_dim(grads, 1 - core, 1, keepdims=False)
        return (keep.astype(F32) + swap(give, "section").astype(F32)).astype(BF16)

    def summed_side(both, token):
        got = after(swap(both[1], "mp"), token)
        return (both[0].astype(F32) + got.astype(F32)).astype(BF16)

    def summed_rows(value, over, token):
        for flip in over:
            got = after(lax.ppermute(value, MESH_AXES, route("dp", flip)), token)
            value = (value.astype(F32) + got.astype(F32)).astype(BF16)
        return value

    flips = [1 << i for i in range(lax.axis_size("dp").bit_length() - 1)]
    flips = flips[2:3] + flips[:2] + flips[3:]
    d_mid, d_grads = branch_backward(
        1, g_dec, d_hat3, d_inv3, dec_gain2, d_hat2, d_inv2, mid_gain,
        d_slope, d_aslope, d_aact, w_dec,
    )
    d_both = summed_here(d_grads)
    d_first, kv_grad, kv_grad_give = cross_backward(
        after(d_mid, d_both), d_hat1, d_inv1, dec_gain1, d_q, c_lse, kv, kv_away, all_keys, dec_row,
        w_cross,
    )
    d_total = summed_side(d_both, d_first)
    kv_grad_away = swap(kv_grad_give, "section")
    e_out = keys_backward(after(g_enc, d_total), kv_grad, kv_grad_away, w_cross)
    e_first, e_grads = branch_backward(
        0, e_out, e_hat2, e_inv2, enc_gain2, e_hat1, e_inv1, enc_gain1,
        e_slope, e_aslope, e_aact, w_enc,
    )
    e_both = summed_here(e_grads)
    d_total = summed_rows(d_total, flips[:1], e_first)
    d_first = after(d_first, e_both)
    bunches = len(w_self.steps) // 2

    def self_part(layer, grad, base, saved, lse, col, row, n):
        return self_backward(
            layer, grad, base, saved, lse, col, row, w_self, n * bunches, bunches
        )

    dx_dec = self_part(1, d_first, d_first, d_qkv, d_lse, dec_col, dec_row, 0)
    e_total = summed_side(e_both, dx_dec)
    d_total = summed_rows(d_total, flips[1:2], dx_dec)
    outputs = rows_back(y_enc, y_dec)
    dx_dec = self_part(1, d_first, after(dx_dec, (e_total, outputs)), d_qkv, d_lse, dec_col, dec_row, 1)
    e_total = summed_rows(e_total, flips[:1], dx_dec)
    d_total = summed_rows(d_total, flips[2:], dx_dec)
    e_first = after(e_first, (dx_dec, e_total))
    dx_enc = self_part(0, e_first, e_first, e_qkv, e_lse, enc_col, enc_row, 0)
    e_total = summed_rows(e_total, flips[1:2], dx_enc)
    dx_dec_back = layer_back(1, dx_dec)
    dx_enc = self_part(
        0, e_first, after(dx_enc, (e_total, d_total, dx_dec_back)), e_qkv, e_lse, enc_col, enc_row, 1
    )
    e_total = summed_rows(e_total, flips[2:], dx_enc)
    dx = jnp.where(first_core, layer_back(0, dx_enc), dx_dec_back)
    mine = jnp.where(first_core, e_total, d_total)
    other = swap(jnp.where(first_core, d_total, e_total), "section")
    down_total = jnp.where(first_core, mine, other)[:units].astype(F32)
    down_total = jnp.transpose(down_total.reshape(units, -1, units), (1, 0, 2)).reshape(width, units)
    up_total = jnp.where(first_core, other, mine).astype(F32)
    dx = jnp.where(first_core, layer_back(0, dx_enc), dx_dec_back)

    return (
        outputs[None],
        dx.astype(F32)[None],
        down_total[None],
        up_total[units : units + 1, :units],
        up_total[:units][None],
        up_total[units + 1 : units + 2],
    )


def solution(mesh):
    in_specs = (
        P("section", "dp", "mp", None),
        P(None, "dp", None),
        P("section", "dp", "mp", None),
        P("section", None, None),
        P(),
        P("section", None, None, "mp"),
        P("section", "mp", None),
        P("section", None, "mp"),
        P("section", None, "mp"),
        P("section", None, "mp"),
        P("section", "mp", None),
        P("section", None, "mp"),
        P("section", "mp"),
        P("section", "mp", None),
        P("section", None),
    )
    out_specs = (
        P("section", "dp", "mp", None),
        P("section", "dp", "mp", None),
        P("section", None, "mp"),
        P("section", "mp"),
        P("section", "mp", None),
        P("section", None),
    )
    return jax.shard_map(
        per_device, mesh=mesh, in_specs=in_specs, out_specs=out_specs, check_vma=False
    )
```

```python
import functools

import jax
import jax.numpy as jnp
from jax import lax
from jax.experimental import pallas as pl
from jax.experimental.pallas import tpu as pltpu
from jax.sharding import PartitionSpec as P

HEADDIM = 64
BUNCH = 4
WIDE = BUNCH * HEADDIM
CHUNK = 1024
SCALE = HEADDIM**-0.5
LANES = 128
PART = 256
EXTRA = 16
HIDDEN_MASK = -1e30
VMEM_LIMIT = 60 * 1024 * 1024
BF16 = jnp.bfloat16
F32 = jnp.float32


def dot_nn(left, right):
    return lax.dot_general(left, right, (((1,), (0,)), ((), ())), preferred_element_type=F32)


def dot_nt(left, right):
    return lax.dot_general(left, right, (((1,), (1,)), ((), ())), preferred_element_type=F32)


def dot_tn(left, right):
    return lax.dot_general(left, right, (((0,), (0,)), ((), ())), preferred_element_type=F32)


class Plan:
    def __init__(self, bufs):
        self.pairs = []
        self.steps = []
        self.bufs = bufs

    def part(self, first, count):
        some = Plan(self.bufs)
        for copies in self.steps[first : first + count]:
            some.steps.append([(some.add(*self.pairs[c[0]]),) + tuple(c[1:]) for c in copies])
        return some

    def add(self, *arrays):
        for i, pair in enumerate(self.pairs):
            if pair[0] is arrays[0]:
                return i
        self.pairs.append(arrays)
        return len(self.pairs) - 1


def at(index):
    return lambda: index


def block(start, size):
    return pl.ds(start, size)


def advance(plan, refs, bufs, sems, layer, step):
    count = len(plan.steps)
    mine = lax.axis_index("section") == layer
    slot = lax.rem(step, 2)

    firsts = [sum(len(p) for p in plan.pairs[:i]) for i in range(len(plan.pairs))]

    def start(copies, side, to):
        for pair, source, buf, place in copies:
            src = refs[firsts[pair] + side].at[source()]
            dst = bufs[buf].at[(to,) + tuple(place())]
            pltpu.make_async_copy(src, dst, sems[buf].at[to]).start()

    def issue(which, to):
        start([c for c in plan.steps[which] if len(plan.pairs[c[0]]) == 1], 0, to)
        layered = [c for c in plan.steps[which] if len(plan.pairs[c[0]]) == 2]
        if layered:

            @pl.when(mine)
            def _():
                start(layered, 0, to)

            @pl.when(jnp.logical_not(mine))
            def _():
                start(layered, 1, to)

    @pl.when(step == 0)
    def _():
        issue(0, 0)

    for which in range(1, count):

        @pl.when(step + 1 == which)
        def _():
            issue(which, which % 2)

    used = [sorted({c[2] for c in copies}) for copies in plan.steps]

    def settle(buf):
        pltpu.make_async_copy(bufs[buf].at[slot], bufs[buf].at[slot], sems[buf].at[slot]).wait()

    first = 0
    for which in range(1, count + 1):
        if which == count or used[which] != used[first]:
            if first == 0 and which == count:
                for buf in used[first]:
                    settle(buf)
            else:

                @pl.when((step >= first) & (step < which))
                def _():
                    for buf in used[first]:
                        settle(buf)

            first = which
    return slot


def call(body, operands, in_blocks, plan, out_shapes, out_blocks, scratch, cost):
    arrays = [a for pair in plan.pairs for a in pair]
    n_ops, n_out, n_buf = len(operands), len(out_shapes), len(plan.bufs)

    def kernel(*refs):
        ins, rest = refs[:n_ops], refs[n_ops:]
        wrefs, rest = rest[: len(arrays)], rest[len(arrays) :]
        outs, rest = rest[:n_out], rest[n_out:]
        bufs, rest = rest[:n_buf], rest[n_buf:]
        sems, extra = rest[:n_buf], rest[n_buf:]
        body(ins, wrefs, outs, bufs, sems, extra)

    return pl.pallas_call(
        kernel,
        grid=(len(plan.steps),),
        in_specs=list(in_blocks) + [pl.BlockSpec(memory_space=pltpu.HBM)] * len(arrays),
        out_specs=tuple(out_blocks),
        out_shape=tuple(out_shapes),
        scratch_shapes=[pltpu.VMEM((2,) + tuple(b), BF16) for b in plan.bufs]
        + [pltpu.SemaphoreType.DMA((2,)) for _ in plan.bufs]
        + list(scratch),
        compiler_params=pltpu.CompilerParams(
            dimension_semantics=("arbitrary",), vmem_limit_bytes=VMEM_LIMIT
        ),
        cost_estimate=pl.CostEstimate(
            flops=int(3 * cost), bytes_accessed=int(cost // 200), transcendentals=0
        ),
    )(*operands, *arrays)


ALL = slice(None)
QUARTER = 128


def self_plan(near, far):
    width = near[0][0].shape[1]
    plan = Plan([(3, width, WIDE), (WIDE, width)])
    qkv, out = plan.add(*near[0]), plan.add(*near[1])
    for g in range(near[0][0].shape[2] // WIDE):
        cols = block(g * WIDE, WIDE)
        plan.steps.append(
            [(qkv, at((ALL, ALL, cols)), 0, at(())), (out, at((cols, ALL)), 1, at(()))]
        )
    for g in range(len(far) // 2):
        copies = []
        for j in range(2):
            first, second, base = far[2 * g + j]
            a, b = plan.add(*first), plan.add(*second)
            lanes = block(j * QUARTER, QUARTER)
            copies.append((a, at((block(0, 2),)), 0, at((block(0, 2), ALL, lanes))))
            copies.append((b, at((base,)), 0, at((2, ALL, lanes))))
            for k in range(width // QUARTER):
                here = block(k * QUARTER, QUARTER)
                copies.append((b, at((base + 1, here, ALL)), 1, at((lanes, here))))
        plan.steps.append(copies)
    return plan


def cross_plan(near, far):
    width = near[0][0].shape[0]
    plan = Plan([(width, WIDE), (width, WIDE)])
    ckv, cvo = plan.add(*near[0]), plan.add(*near[1])
    for g in range(near[0][0].shape[1] // WIDE):
        cols = block(g * WIDE, WIDE)
        plan.steps.append([(ckv, at((ALL, cols)), 0, at(())), (cvo, at((ALL, cols)), 1, at(()))])
    for g in range(len(far) // 2):
        copies = []
        for j in range(2):
            first, second, base = far[2 * g + j]
            a, b = plan.add(*first), plan.add(*second)
            lanes = block(j * QUARTER, QUARTER)
            copies.append((a, at((0,)), 0, at((ALL, lanes))))
            copies.append((b, at((base,)), 1, at((ALL, lanes))))
        plan.steps.append(copies)
    return plan


def branch_plan(near, far, stride):
    width, hidden = near[0][0].shape
    units = near[2][0].shape[1]
    piece = width // 8
    plan = Plan([(width, CHUNK), (CHUNK, width), (width, units), (units, width)])
    up, down, adown, aup = [plan.add(*pair) for pair in near]
    for g in range(hidden // CHUNK):
        cols = block(g * CHUNK, CHUNK)
        plan.steps.append([(up, at((ALL, cols)), 0, at(())), (down, at((cols, ALL)), 1, at(()))])
    adapter = []
    each = CHUNK // (2 * WIDE)
    for j, both in enumerate(far):
        copies = [] if j % each == 0 else copies
        for k, (first, second, base) in enumerate(both):
            a, b = plan.add(first), plan.add(second)
            cols = block((j % each * 2 + k) * WIDE, WIDE)
            copies.append((a, at((block(0, width), ALL)), 0, at((ALL, cols))))
            for n in range(width // WIDE):
                rows = block(base + n * WIDE, WIDE)
                copies.append((b, at((rows, ALL)), 1, at((cols, block(n * WIDE, WIDE)))))

            def spot(j=j, k=k):
                return block(pl.multiple_of(eighth_of(j, k, stride) * piece, piece), piece)

            rows = block(base + width, piece)
            adapter.append((b, at((rows, ALL)), 2, lambda spot=spot: (spot(), ALL)))
            for n in range(units // piece):
                rows = block(base + width + piece, piece)
                here = block(n * piece, piece)
                adapter.append(
                    (b, at((rows, here)), 3, lambda spot=spot, here=here: (here, spot()))
                )
        if j % each == each - 1:
            plan.steps.append(copies)
    plan.steps.append([(adown, at(()), 2, at(())), (aup, at(()), 3, at(()))])
    plan.steps.append(adapter)
    return plan


def share_of(j, stride):
    place = lax.axis_index("dp")
    x = lax.rem(place, 2)
    z = lax.rem(lax.div(place, stride), 2)
    x = 1 - x if j in (1, 3) else x
    z = 1 - z if j in (2, 3) else z
    return 2 * x + z


def eighth_of(j, k, stride):
    core = lax.axis_index("section")
    return 4 * (1 - core if k else core) + share_of(j, stride)


def cut_piece(pairs, layer, shape, moves):
    plan = Plan([])
    plan.pairs = pairs
    firsts = [sum(len(p) for p in pairs[:i]) for i in range(len(pairs))]
    arrays = [a for pair in pairs for a in pair]

    def kernel(*refs):
        ins, out, sem = refs[: len(arrays)], refs[-2], refs[-1]

        def start(side):
            for pair, index, place in moves:
                src = ins[firsts[pair] + side].at[index()]
                pltpu.make_async_copy(src, out.at[place()], sem).start()

        if layer is None:
            start(0)
        else:
            mine = lax.axis_index("section") == layer

            @pl.when(mine)
            def _():
                start(0)

            @pl.when(jnp.logical_not(mine))
            def _():
                start(1)

        pltpu.make_async_copy(out, out, sem).wait()

    return pl.pallas_call(
        kernel,
        in_specs=[pl.BlockSpec(memory_space=pltpu.HBM)] * len(arrays),
        out_specs=pl.BlockSpec(memory_space=pltpu.VMEM),
        out_shape=shaped(shape, BF16),
        scratch_shapes=[pltpu.SemaphoreType.DMA],
        compiler_params=pltpu.CompilerParams(vmem_limit_bytes=8 * 1024 * 1024),
    )(*arrays)


def whole(shape):
    zeros = (0,) * len(shape)
    return pl.BlockSpec(tuple(shape), lambda i: zeros)


def per_step(shape, first=0, last=None):
    def index(i):
        k = jnp.maximum(i - first, 0)
        if last is not None:
            k = jnp.minimum(k, last)
        return (k,) + (0,) * len(shape)

    return pl.BlockSpec((1,) + tuple(shape), index)


def shaped(shape, dtype):
    return jax.ShapeDtypeStruct(tuple(shape), dtype)


def normalized(value):
    center = value - jnp.mean(value, -1, keepdims=True)
    spread = jnp.mean(center * center, -1, keepdims=True)
    inverse = lax.rsqrt(spread + 1e-05)
    return center * inverse, inverse


def norm_slope(grad, hat, inverse, gain):
    scaled = grad * gain
    along = jnp.mean(scaled * hat, -1, keepdims=True)
    return inverse * (scaled - jnp.mean(scaled, -1, keepdims=True) - hat * along)


def gelu_pair(value):
    below = 0.5 + 0.5 * lax.erf(value * (0.5**0.5))
    density = jnp.exp(value * value * -0.5) * 0.3989422804014327
    return value * below, below + value * density


def lanes_of(head):
    first = head * HEADDIM // LANES * LANES
    return slice(first, first + LANES)


def only_head(value, head):
    lane = lax.broadcasted_iota(jnp.int32, (1, LANES), 1)
    inside = head * HEADDIM % LANES
    keep = (lane >= inside) & (lane < inside + HEADDIM)
    part = value[:, lanes_of(head)]
    return jnp.where(keep, part, jnp.zeros_like(part))


def attend(blocks, q_ref, k_ref, v_ref, bias_ref, valid_ref, lse_ref, out_ref):
    units = [(rows, keys, head) for rows, keys in blocks for head in range(BUNCH)]

    def scores_of(unit):
        rows, keys, head = unit
        q_head = only_head(q_ref[rows, :] * jnp.asarray(SCALE, BF16), head)
        return dot_nt(k_ref[keys, lanes_of(head)], q_head)

    ahead = scores_of(units[0])
    for i, (rows, keys, head) in enumerate(units):
        scores = ahead + bias_ref[keys, rows]
        if i + 1 < len(units):
            ahead = scores_of(units[i + 1])
        peak = jnp.max(scores, 0, keepdims=True)
        powers = jnp.exp(scores - peak)
        total = jnp.sum(powers, 0, keepdims=True)
        share = 1.0 / total
        lse = peak + jnp.log(total)
        if valid_ref is not None:
            valid = valid_ref[:, rows] > 0.0
            share = jnp.where(valid, share, 0.0)
            lse = jnp.where(valid, lse, -HIDDEN_MASK)
        lse_ref[head : head + 1, rows] = lse
        mixed = dot_tn((powers * share).astype(BF16), only_head(v_ref[keys, :], head))
        out_ref[rows, lanes_of(head)] += mixed


def attend_slope(blocks, q_ref, k_ref, v_ref, g_ref, bias_ref, lse_ref, dq_ref, dk_ref, dv_ref):
    units = [(rows, keys, head) for rows, keys in blocks for head in range(BUNCH)]

    def products_of(unit):
        rows, keys, head = unit
        q_head = only_head(q_ref[rows, :] * jnp.asarray(SCALE, BF16), head)
        g_head = only_head(g_ref[rows, :], head)
        lanes = lanes_of(head)
        return q_head, g_head, dot_nt(k_ref[keys, lanes], q_head), dot_nt(v_ref[keys, lanes], g_head)

    ahead = products_of(units[0])
    for i, (rows, keys, head) in enumerate(units):
        q_head, g_head, scores, prob_grad = ahead
        if i + 1 < len(units):
            ahead = products_of(units[i + 1])
        lanes = lanes_of(head)
        probs = jnp.exp(scores + bias_ref[keys, rows] - lse_ref[head : head + 1, rows])
        inner = jnp.sum(probs * prob_grad, 0, keepdims=True)
        score_grad = (probs * (prob_grad - inner)).astype(BF16)
        dv_ref[keys, lanes] += dot_nn(probs.astype(BF16), g_head)
        dk_ref[keys, lanes] += dot_nn(score_grad, q_head)
        dq_ref[rows, lanes] += dot_tn(score_grad, only_head(k_ref[keys, :], head))


def fill_bias(bias_ref, key_seg, row_seg, causal):
    seen = key_seg == row_seg
    if causal:
        key = lax.broadcasted_iota(jnp.int32, bias_ref.shape, 0)
        row = lax.broadcasted_iota(jnp.int32, bias_ref.shape, 1)
        seen = seen & (key <= row)
    bias_ref[...] = jnp.where(seen, 0.0, HIDDEN_MASK)


def self_blocks(rows, causal):
    if not causal:
        return [(slice(0, rows), slice(0, rows))]
    count = rows // PART
    parts = [slice(i * PART, (i + 1) * PART) for i in range(count)]
    return [(part, slice(0, part.stop)) for part in parts]


def cross_blocks(rows):
    return [(slice(i, i + PART), slice(0, rows)) for i in range(0, rows, PART)]


def note_active(bias, valid, active, rows):
    for h in range(2):
        best = jnp.max(bias[h], 0, keepdims=True)
        valid[h] = jnp.where(best > 0.5 * HIDDEN_MASK, 1.0, 0.0)
        for i in range(rows // PART):
            some = jnp.max(valid[h, :, i * PART : (i + 1) * PART])
            active[h, i] = (some > 0.0).astype(jnp.int32)


def self_forward(layer, x, seg_col, seg_row, gain, plan):
    rows, width = x.shape
    steps = len(plan.steps)

    def body(ins, wrefs, outs, bufs, sems, extra):
        x_ref, segc_ref, segr_ref, gain_ref = ins
        qkv_ref, lse_ref, hat_ref, inv_ref = outs
        acc, bias, mixed = extra
        step = pl.program_id(0)
        slot = advance(plan, wrefs, bufs, sems, layer, step)

        @pl.when(step == 0)
        def _():
            fill_bias(bias, segc_ref[...], segr_ref[...], layer == 1)
            acc[...] = x_ref[...].astype(F32)

        x_rows = x_ref[...]
        w = bufs[0].at[slot]
        q = dot_nn(x_rows, w[0]).astype(BF16)
        k = dot_nn(x_rows, w[1]).astype(BF16)
        v = dot_nn(x_rows, w[2]).astype(BF16)
        qkv_ref[0, 0] = q
        qkv_ref[0, 1] = k
        qkv_ref[0, 2] = v
        mixed[...] = jnp.zeros_like(mixed)
        attend(
            self_blocks(rows, layer == 1), qkv_ref.at[0, 0], qkv_ref.at[0, 1], qkv_ref.at[0, 2],
            bias, None, lse_ref.at[0], mixed,
        )
        acc[...] += dot_nn(mixed[...].astype(BF16), bufs[1][slot])

        @pl.when(step == steps - 1)
        def _():
            hat, inverse = normalized(acc[...])
            hat_ref[...] = hat.astype(BF16)
            inv_ref[...] = inverse

    return call(
        body,
        [x, seg_col, seg_row, gain],
        [whole(x.shape), whole(seg_col.shape), whole(seg_row.shape), whole(gain.shape)],
        plan,
        [
            shaped((steps, 3, rows, WIDE), BF16),
            shaped((steps, BUNCH, rows), F32),
            shaped((rows, width), BF16),
            shaped((rows, 1), F32),
        ],
        [
            per_step((3, rows, WIDE)),
            per_step((BUNCH, rows)),
            whole((rows, width)),
            whole((rows, 1)),
        ],
        [
            pltpu.VMEM((rows, width), F32),
            pltpu.VMEM((rows, rows), F32),
            pltpu.VMEM((rows, WIDE), F32),
        ],
        steps * (2 * rows * width * WIDE * 4 + 16 * rows * rows * WIDE),
    )


def self_backward(layer, grad, base, saved, lse, seg_col, seg_row, plan, first, count):
    rows, width = grad.shape
    steps = count
    plan = plan.part(first, count)

    def body(ins, wrefs, outs, bufs, sems, extra):
        g_ref, base_ref, saved_ref, lse_ref, segc_ref, segr_ref = ins
        (dx_ref,) = outs
        acc, bias, mixed_grad, dq, dk, dv = extra
        step = pl.program_id(0)
        slot = advance(plan, wrefs, bufs, sems, layer, step)

        @pl.when(step == 0)
        def _():
            fill_bias(bias, segc_ref[...], segr_ref[...], layer == 1)
            acc[...] = base_ref[...].astype(F32)

        mixed_grad[...] = dot_nt(g_ref[...], bufs[1][slot]).astype(BF16)
        for ref in (dq, dk, dv):
            ref[...] = jnp.zeros_like(ref)
        attend_slope(
            self_blocks(rows, layer == 1), saved_ref.at[0, 0], saved_ref.at[0, 1],
            saved_ref.at[0, 2], mixed_grad, bias, lse_ref.at[0], dq, dk, dv,
        )
        w = bufs[0].at[slot]
        acc[...] += (
            dot_nt((dq[...] * SCALE).astype(BF16), w[0])
            + dot_nt(dk[...].astype(BF16), w[1])
            + dot_nt(dv[...].astype(BF16), w[2])
        )

        @pl.when(step == steps - 1)
        def _():
            dx_ref[...] = acc[...].astype(BF16)

    return call(
        body,
        [grad, base, saved, lse, seg_col, seg_row],
        [
            whole(grad.shape),
            whole(grad.shape),
            per_step((3, rows, WIDE), -first),
            per_step((BUNCH, rows), -first),
            whole(seg_col.shape),
            whole(seg_row.shape),
        ],
        plan,
        [shaped((rows, width), BF16)],
        [whole((rows, width))],
        [
            pltpu.VMEM((rows, width), F32),
            pltpu.VMEM((rows, rows), F32),
            pltpu.VMEM((rows, WIDE), BF16),
            pltpu.VMEM((rows, WIDE), F32),
            pltpu.VMEM((rows, WIDE), F32),
            pltpu.VMEM((rows, WIDE), F32),
        ],
        steps * (2 * rows * width * WIDE * 4 + 40 * rows * rows * WIDE),
    )[0]


def cross_forward(hat, gain, kv_own, kv_away, keys_col, seg_row, plan):
    rows, width = hat.shape
    steps = len(plan.steps)

    def body(ins, wrefs, outs, bufs, sems, extra):
        hat_ref, gain_ref, own_ref, away_ref, keysc_ref, segr_ref = ins
        q_ref, lse_ref, nhat_ref, inv_ref = outs
        acc, low, bias, mixed, valid, active = extra
        step = pl.program_id(0)
        slot = advance(plan, wrefs, bufs, sems, 1, step)

        @pl.when(step == 0)
        def _():
            for h in range(2):
                fill_bias(bias.at[h], keysc_ref[h], segr_ref[...], False)
            note_active(bias, valid, active, rows)
            first = hat_ref[...].astype(F32) * gain_ref[...]
            acc[...] = first
            low[...] = first.astype(BF16)

        q = dot_nn(low[...], bufs[0][slot]).astype(BF16)
        q_ref[0] = q
        mixed[...] = jnp.zeros_like(mixed)
        for h, kv_ref in enumerate((own_ref, away_ref)):
            for i, pair in enumerate(cross_blocks(rows)):

                @pl.when(active[h, i] > 0)
                def _():
                    attend(
                        [pair], q_ref.at[0], kv_ref.at[0, 0], kv_ref.at[0, 1],
                        bias.at[h], valid.at[h], lse_ref.at[0, h], mixed,
                    )

        acc[...] += dot_nt(mixed[...].astype(BF16), bufs[1][slot])

        @pl.when(step == steps - 1)
        def _():
            nhat, inverse = normalized(acc[...])
            nhat_ref[...] = nhat.astype(BF16)
            inv_ref[...] = inverse

    return call(
        body,
        [hat, gain, kv_own, kv_away, keys_col, seg_row],
        [
            whole(hat.shape),
            whole(gain.shape),
            per_step((2, rows, WIDE)),
            per_step((2, rows, WIDE)),
            whole(keys_col.shape),
            whole(seg_row.shape),
        ],
        plan,
        [
            shaped((steps, rows, WIDE), BF16),
            shaped((steps, 2, BUNCH, rows), F32),
            shaped((rows, width), BF16),
            shaped((rows, 1), F32),
        ],
        [
            per_step((rows, WIDE)),
            per_step((2, BUNCH, rows)),
            whole((rows, width)),
            whole((rows, 1)),
        ],
        [
            pltpu.VMEM((rows, width), F32),
            pltpu.VMEM((rows, width), BF16),
            pltpu.VMEM((2, rows, rows), F32),
            pltpu.VMEM((rows, WIDE), F32),
            pltpu.VMEM((2, 1, rows), F32),
            pltpu.SMEM((2, rows // PART), jnp.int32),
        ],
        steps * (2 * rows * width * WIDE * 2 + 32 * rows * rows * WIDE),
    )


def cross_backward(grad, hat, inv, gain, saved_q, lse, kv_own, kv_away, keys_col, seg_row, plan):
    rows, width = grad.shape
    steps = len(plan.steps)

    def body(ins, wrefs, outs, bufs, sems, extra):
        g_ref, hat_ref, inv_ref, gain_ref, q_ref, lse_ref, own_ref, away_ref, keysc_ref, segr_ref = ins
        dx_ref, own_grad_ref, away_grad_ref = outs
        acc, bias, mixed_grad, dq, dk, dv, valid, active = extra
        step = pl.program_id(0)
        slot = advance(plan, wrefs, bufs, sems, 1, step)

        @pl.when(step == 0)
        def _():
            for h in range(2):
                fill_bias(bias.at[h], keysc_ref[h], segr_ref[...], False)
            note_active(bias, valid, active, rows)
            acc[...] = g_ref[...].astype(F32)

        mixed_grad[...] = dot_nn(g_ref[...], bufs[1][slot]).astype(BF16)
        for ref in (dq, dk, dv):
            ref[...] = jnp.zeros_like(ref)
        for h, kv_ref in enumerate((own_ref, away_ref)):
            for i, pair in enumerate(cross_blocks(rows)):

                @pl.when(active[h, i] > 0)
                def _():
                    attend_slope(
                        [pair], q_ref.at[0], kv_ref.at[0, 0], kv_ref.at[0, 1], mixed_grad,
                        bias.at[h], lse_ref.at[0, h], dq, dk.at[h], dv.at[h],
                    )

        for h, out_ref in enumerate((own_grad_ref, away_grad_ref)):
            out_ref[0, 0] = dk[h].astype(BF16)
            out_ref[0, 1] = dv[h].astype(BF16)
        acc[...] += dot_nt((dq[...] * SCALE).astype(BF16), bufs[0][slot])

        @pl.when(step == steps - 1)
        def _():
            dx_ref[...] = norm_slope(
                acc[...], hat_ref[...].astype(F32), inv_ref[...], gain_ref[...]
            ).astype(BF16)

    return call(
        body,
        [grad, hat, inv, gain, saved_q, lse, kv_own, kv_away, keys_col, seg_row],
        [
            whole(grad.shape),
            whole(hat.shape),
            whole(inv.shape),
            whole(gain.shape),
            per_step((rows, WIDE)),
            per_step((2, BUNCH, rows)),
            per_step((2, rows, WIDE)),
            per_step((2, rows, WIDE)),
            whole(keys_col.shape),
            whole(seg_row.shape),
        ],
        plan,
        [
            shaped((rows, width), BF16),
            shaped((steps, 2, rows, WIDE), BF16),
            shaped((steps, 2, rows, WIDE), BF16),
        ],
        [whole((rows, width)), per_step((2, rows, WIDE)), per_step((2, rows, WIDE))],
        [
            pltpu.VMEM((rows, width), F32),
            pltpu.VMEM((2, rows, rows), F32),
            pltpu.VMEM((rows, WIDE), BF16),
            pltpu.VMEM((rows, WIDE), F32),
            pltpu.VMEM((2, rows, WIDE), F32),
            pltpu.VMEM((2, rows, WIDE), F32),
            pltpu.VMEM((2, 1, rows), F32),
            pltpu.SMEM((2, rows // PART), jnp.int32),
        ],
        steps * (2 * rows * width * WIDE * 2 + 80 * rows * rows * WIDE),
    )


def keys_forward(y, plan):
    rows, width = y.shape
    steps = len(plan.steps)

    def body(ins, wrefs, outs, bufs, sems, extra):
        (kv_ref,) = outs
        slot = advance(plan, wrefs, bufs, sems, 0, pl.program_id(0))
        kv_ref[0, 0] = dot_nn(ins[0][...], bufs[0][slot]).astype(BF16)
        kv_ref[0, 1] = dot_nn(ins[0][...], bufs[1][slot]).astype(BF16)

    return call(
        body,
        [y],
        [whole(y.shape)],
        plan,
        [shaped((steps, 2, rows, WIDE), BF16)],
        [per_step((2, rows, WIDE))],
        [],
        steps * 4 * rows * width * WIDE,
    )[0]


def keys_backward(out_grad, kv_grad, kv_grad_away, plan):
    rows, width = out_grad.shape
    steps = len(plan.steps)

    def body(ins, wrefs, outs, bufs, sems, extra):
        g_ref, own_ref, away_ref = ins
        (sum_ref,) = outs
        (acc,) = extra
        step = pl.program_id(0)
        slot = advance(plan, wrefs, bufs, sems, 0, step)

        @pl.when(step == 0)
        def _():
            acc[...] = g_ref[...].astype(F32)

        both = (own_ref[0].astype(F32) + away_ref[0].astype(F32)).astype(BF16)
        acc[...] += dot_nt(both[0], bufs[0][slot]) + dot_nt(both[1], bufs[1][slot])

        @pl.when(step == steps - 1)
        def _():
            sum_ref[...] = acc[...].astype(BF16)

    return call(
        body,
        [out_grad, kv_grad, kv_grad_away],
        [whole(out_grad.shape), per_step((2, rows, WIDE)), per_step((2, rows, WIDE))],
        plan,
        [shaped((rows, width), BF16)],
        [whole((rows, width))],
        [pltpu.VMEM((rows, width), F32)],
        steps * 4 * rows * width * WIDE,
    )[0]


def branch_forward(layer, hat, gain, out_gain, down_bias, up_bias, plan):
    rows, width = hat.shape
    nb = 2
    na = len(plan.steps) - nb
    units = down_bias.shape[-1]
    steps = na + nb

    def body(ins, wrefs, outs, bufs, sems, extra):
        hat_ref, gain_ref, ogain_ref, dbias_ref, ubias_ref = ins
        slope_ref, aslope_ref, aact_ref, nhat_ref, inv_ref, y_ref = outs
        acc, low = extra
        step = pl.program_id(0)
        slot = advance(plan, wrefs, bufs, sems, layer, step)

        @pl.when(step == 0)
        def _():
            first = hat_ref[...].astype(F32) * gain_ref[...]
            low[...] = first.astype(BF16)
            acc[...] = first + 4.0 * ubias_ref[...]

        @pl.when(step < na)
        def _():
            for at in range(0, rows, 512):
                part = slice(at, at + 512)
                act, slope = gelu_pair(dot_nn(low[part, :], bufs[0][slot]))
                slope_ref[0, part, :] = slope.astype(BF16)
                acc[part, :] += dot_nn(act.astype(BF16), bufs[1][slot])

        @pl.when(step >= na)
        def _():
            act, slope = gelu_pair(dot_nn(low[...], bufs[2][slot]) + dbias_ref[0])
            low_act = act.astype(BF16)
            aslope_ref[0] = slope.astype(BF16)
            aact_ref[0] = low_act
            acc[...] += dot_nn(low_act * jnp.asarray(4.0, BF16), bufs[3][slot])

        @pl.when(step == steps - 1)
        def _():
            nhat, inverse = normalized(acc[...])
            nhat_ref[...] = nhat.astype(BF16)
            inv_ref[...] = inverse
            y_ref[...] = (nhat * ogain_ref[...]).astype(BF16)

    return call(
        body,
        [hat, gain, out_gain, down_bias, up_bias],
        [
            whole(hat.shape),
            whole(gain.shape),
            whole(out_gain.shape),
            per_step((1, units), na),
            whole(up_bias.shape),
        ],
        plan,
        [
            shaped((na, rows, CHUNK), BF16),
            shaped((nb, rows, units), BF16),
            shaped((nb, rows, units), BF16),
            shaped((rows, width), BF16),
            shaped((rows, 1), F32),
            shaped((rows, width), BF16),
        ],
        [
            per_step((rows, CHUNK), 0, na - 1),
            per_step((rows, units), na),
            per_step((rows, units), na),
            whole((rows, width)),
            whole((rows, 1)),
            whole((rows, width)),
        ],
        [pltpu.VMEM((rows, width), F32), pltpu.VMEM((rows, width), BF16)],
        4 * rows * width * (na * CHUNK + nb * units),
    )


def branch_backward(layer, out_grad, nhat, ninv, out_gain, hat, inv, gain, slope, aslope, aact, plan):
    rows, width = hat.shape
    nb = 2
    na = len(plan.steps) - nb
    units = aact.shape[-1]
    steps = na + nb

    def body(ins, wrefs, outs, bufs, sems, extra):
        g_ref, nhat_ref, ninv_ref, ogain_ref, hat_ref, inv_ref, gain_ref, slope_ref, aslope_ref, aact_ref = ins
        dx_ref, packed_ref = outs
        acc, low, rows_low, up_bias = extra
        step = pl.program_id(0)
        slot = advance(plan, wrefs, bufs, sems, layer, step)

        @pl.when(step == 0)
        def _():
            grad = norm_slope(
                g_ref[...].astype(F32), nhat_ref[...].astype(F32), ninv_ref[...], ogain_ref[...]
            )
            acc[...] = grad
            small = grad.astype(BF16)
            low[...] = small
            up_bias[...] = 4.0 * jnp.sum(small.astype(F32), 0, keepdims=True)
            rows_low[...] = (hat_ref[...].astype(F32) * gain_ref[...]).astype(BF16)

        @pl.when(step < na)
        def _():
            for at in range(0, rows, 512):
                part = slice(at, at + 512)
                hidden = dot_nt(low[part, :], bufs[1][slot]) * slope_ref[0, part, :].astype(F32)
                acc[part, :] += dot_nt(hidden.astype(BF16), bufs[0][slot])

        @pl.when(step >= na)
        def _():
            hidden = 4.0 * dot_nt(low[...], bufs[3][slot]) * aslope_ref[0].astype(F32)
            small = hidden.astype(BF16)
            acc[...] += dot_nt(small, bufs[2][slot])
            down = dot_tn(rows_low[...], small).astype(BF16)
            for n in range(width // units):
                cols = slice(n * units, (n + 1) * units)
                packed_ref[0, 0, :units, cols] = down[cols]
            packed_ref[0, 1, :units] = (4.0 * dot_tn(aact_ref[0], low[...])).astype(BF16)
            bias = jnp.sum(small.astype(F32), 0, keepdims=True)
            bias = jnp.concatenate([bias] + [jnp.zeros_like(bias)] * (width // units - 1), 1)
            row = lax.broadcasted_iota(jnp.int32, (EXTRA, width), 0)
            last = jnp.where(row == 0, bias, jnp.where(row == 1, up_bias[...], 0.0))
            packed_ref[0, 0, units:] = jnp.zeros((EXTRA, width), BF16)
            packed_ref[0, 1, units:] = last.astype(BF16)

        @pl.when(step == steps - 1)
        def _():
            dx_ref[...] = norm_slope(
                acc[...], hat_ref[...].astype(F32), inv_ref[...], gain_ref[...]
            ).astype(BF16)

    return call(
        body,
        [out_grad, nhat, ninv, out_gain, hat, inv, gain, slope, aslope, aact],
        [
            whole(out_grad.shape),
            whole(nhat.shape),
            whole(ninv.shape),
            whole(out_gain.shape),
            whole(hat.shape),
            whole(inv.shape),
            whole(gain.shape),
            per_step((rows, CHUNK), 0, na - 1),
            per_step((rows, units), na),
            per_step((rows, units), na),
        ],
        plan,
        [
            shaped((rows, width), BF16),
            shaped((nb, 2, units + EXTRA, width), BF16),
        ],
        [
            whole((rows, width)),
            per_step((2, units + EXTRA, width), na),
        ],
        [
            pltpu.VMEM((rows, width), F32),
            pltpu.VMEM((rows, width), BF16),
            pltpu.VMEM((rows, width), BF16),
            pltpu.VMEM((1, width), F32),
        ],
        4 * rows * width * (na * CHUNK + nb * units),
    )


class Lane:
    def __init__(self, depth):
        self.depth = depth
        self.sent = []

    def send(self, value, axes, route):
        if len(self.sent) >= self.depth:
            value, _ = lax.optimization_barrier((value, self.sent[-self.depth]))
        got = lax.ppermute(value, axes, route)
        self.sent.append(got)
        return got


MESH_AXES = ("section", "mp", "dp")


def route(axis, flip, core=None):
    sizes = [lax.axis_size(a) for a in MESH_AXES]
    pairs = []
    for s in range(sizes[0]):
        for m in range(sizes[1]):
            for d in range(sizes[2]):
                if core is not None and s != core:
                    continue
                to = [s, m, d]
                to[MESH_AXES.index(axis)] ^= flip
                number = lambda p: (p[0] * sizes[1] + p[1]) * sizes[2] + p[2]
                pairs.append((number((s, m, d)), number(to)))
    return pairs


def after(value, token):
    return lax.optimization_barrier((value, token))[0]


def swap(value, axis):
    return jax.tree.map(lambda a: lax.ppermute(a, axis, [(0, 1), (1, 0)]), value)


def rotated(pieces, start, count):
    return lax.dynamic_slice_in_dim(jnp.concatenate(pieces, 0), start, count, 0)


def per_device(
    inputs,
    segment_ids,
    cotangent,
    norm_gains,
    cross_gain,
    self_qkv,
    self_out,
    cross_kv,
    cross_vo,
    ffn_in,
    ffn_out,
    adapter_down,
    adapter_down_bias,
    adapter_up,
    adapter_up_bias,
):
    core = lax.axis_index("section")
    side = lax.axis_index("mp")
    first_core = core == 0
    seq = segment_ids.shape[2]
    half = seq // 2
    width = inputs.shape[3]
    units = adapter_down.shape[2]

    stride = max(lax.axis_size("dp") // 4, 1)
    lane_y, lane_x, lane_z, lane_core = Lane(1), Lane(2), Lane(2), Lane(3)

    def over_y(value):
        return lane_y.send(value, MESH_AXES, route("mp", 1))

    def over_x(value):
        return lane_x.send(value, MESH_AXES, route("dp", 1))

    def over_z(value):
        return lane_z.send(value, MESH_AXES, route("dp", stride))

    def near_pairs(*arrays):
        return [(a, lane_core.send(a, MESH_AXES, route("section", 1))) for a in arrays]

    def share(j, size):
        return block(pl.multiple_of(share_of(j, stride) * size, size), size)

    def eighth(j, size):
        return block(pl.multiple_of(eighth_of(j, 0, stride) * size, size), size)

    def columns(n, size):
        return block(n * size, size)

    qkv = jnp.transpose(self_qkv[0], (1, 0, 2))
    near_self = near_pairs(qkv, self_out[0])

    def self_piece(j):
        moves = [(0, lambda: (ALL, ALL, share(j, QUARTER)), at((block(0, 3),)))]
        moves += [
            (1, lambda n=n: (share(j, QUARTER), columns(n, QUARTER)), at((3, columns(n, QUARTER))))
            for n in range(width // QUARTER)
        ]
        return cut_piece([(qkv,), (self_out[0],)], None, (4, width, QUARTER), moves)

    piece = width // 8

    def ffn_piece(layer, j):
        moves = [(0, lambda: (ALL, eighth(j, WIDE)), at((block(0, width), ALL)))]
        moves += [
            (1, lambda n=n: (eighth(j, WIDE), columns(n, WIDE)), at((block(width + n * WIDE, WIDE), ALL)))
            for n in range(width // WIDE)
        ]
        moves += [(2, lambda: (eighth(j, piece), ALL), at((block(2 * width, piece), ALL)))]
        moves += [
            (
                3,
                lambda n=n: (columns(n, piece), eighth(j, piece)),
                at((block(2 * width + piece, piece), columns(n, piece))),
            )
            for n in range(units // piece)
        ]
        return cut_piece(near_ffn, layer, (2 * width + 2 * piece, WIDE), moves)

    def cross_piece(j):
        moves = [(n, lambda: (ALL, share(j, QUARTER)), at((n,))) for n in range(2)]
        return cut_piece([(cross_kv[0],), (cross_vo[0],)], None, (2, width, QUARTER), moves)

    def swapped(value):
        return swap(value, "section")

    def quarters(pieces, swaps, base):
        return [((p, q), (p, q), base) for p, q in zip(pieces, swaps)]

    def eighths(pieces, swaps, base):
        return [((p, p, base), (q, q, base)) for p, q in zip(pieces, swaps)]

    def swapped_after(pieces, token):
        return [swapped(after(p, token)) for p in pieces]

    bias_near = adapter_down_bias[0][None]
    bias_far = over_y(bias_near)
    small = jnp.concatenate(
        [
            norm_gains[0],
            adapter_up_bias,
            jnp.concatenate([bias_near, bias_far, jnp.zeros((1, width - 2 * units), F32)], 1),
        ],
        0,
    )
    small_other = swap(small, "section")
    enc_small = jnp.where(first_core, small, small_other)
    dec_small = jnp.where(first_core, small_other, small)

    def small_of(s):
        down_bias = jnp.stack([s[3:4, :units], s[3:4, units : 2 * units]], 0)
        return s[0:1], s[1:2], s[2:3], down_bias

    enc_gain1, enc_gain2, enc_upb, enc_downb = small_of(enc_small)
    dec_gain1, dec_gain2, dec_upb, dec_downb = small_of(dec_small)
    mid_gain = cross_gain[None]

    segs = lax.dynamic_index_in_dim(segment_ids, side, 1, keepdims=False)
    docs = jnp.arange(seq)
    counts = jnp.sum(segs[:, :, None] == docs[None, None, :8], 1)
    largest = jnp.argmax(counts, 1)
    starts = jnp.sum(segs < largest[:, None], 1).astype(jnp.int32)

    def halves_of_seg(seg, start):
        twice = jnp.concatenate([seg, seg], 0)
        mine = lax.dynamic_slice_in_dim(twice, start + half * core, half, 0)
        away = lax.dynamic_slice_in_dim(twice, start + half * (1 - core), half, 0)
        return mine, away

    enc_seg, enc_seg_away = halves_of_seg(segs[0], starts[0])
    dec_seg, _ = halves_of_seg(segs[1], starts[1])
    own_start = jnp.where(first_core, starts[0], starts[1])

    def rows_sent(value, token=None):
        keep = lax.dynamic_index_in_dim(value[0], side, 0, keepdims=False)
        give = lax.dynamic_index_in_dim(value[0], 1 - side, 0, keepdims=False)
        return keep, over_y(give if token is None else after(give, token))

    def rows_here(keep, got):
        start = lax.rem(own_start + seq - half * side, seq)
        ring = (keep, got, keep, got)
        mine = rotated(ring, start + half * core, half)
        away = rotated(ring, lax.rem(start + half * (1 - core), seq), half)
        other = swap(away, "section")
        return jnp.where(first_core, mine, other), jnp.where(first_core, other, mine)

    def slices_back(big, rest, start):
        ring = (big, rest, big, rest)
        keep = rotated(ring, lax.rem(half * side + seq - start, seq), half)
        give = rotated(ring, lax.rem(half * (1 - side) + seq - start, seq), half)
        return keep, give

    def by_row(keep, got):
        return jnp.where(side == 0, jnp.stack([keep, got]), jnp.stack([got, keep]))

    def rows_back(enc, dec):
        mine = jnp.where(first_core, enc, dec)
        away = jnp.where(first_core, dec, enc)
        other = swap(away, "section")
        big = jnp.where(first_core, mine, other)
        rest = jnp.where(first_core, other, mine)
        keep, give = slices_back(big, rest, own_start)
        return by_row(keep, swap(give, "mp"))

    def layer_back(layer, value):
        other = lax.ppermute(value, MESH_AXES, route("section", 1, 1 - layer))
        big, rest = (value, other) if layer == 0 else (other, value)
        keep, give = slices_back(big, rest, starts[layer])
        return by_row(keep, lax.ppermute(give, MESH_AXES, route("mp", 1, layer)))

    x_keep, x_got = rows_sent(inputs)
    near_ffn = near_pairs(ffn_in[0], ffn_out[0], adapter_down[0], adapter_up[0])
    near_cross = near_pairs(cross_kv[0], cross_vo[0])
    near_other = [pair[1] for pair in near_self + near_ffn + near_cross]
    self_0 = over_y(self_piece(0))
    self_3 = over_y(self_piece(3))
    self_1, self_2 = over_x(after(self_0, near_other)), over_z(after(self_0, near_other))
    self_swaps = [swapped(p) for p in (self_0, self_1, self_2)]
    self_swaps.append(swapped(after(self_3, (self_1, self_2))))
    cross_0 = over_y(after(cross_piece(0), (self_1, self_2)))
    enc_0 = over_y(ffn_piece(0, 0))
    lane_y.depth = 2
    x_enc, x_dec = rows_here(x_keep, x_got)
    w_self = self_plan(near_self, quarters((self_0, self_1, self_2, self_3), self_swaps, 2))

    enc_col, enc_row = enc_seg[:, None], enc_seg[None, :]
    dec_col, dec_row = dec_seg[:, None], dec_seg[None, :]
    all_keys = jnp.stack([enc_seg, enc_seg_away], 0)[:, :, None]

    e_qkv, e_lse, e_hat1, e_inv1 = self_forward(0, x_enc, enc_col, enc_row, enc_gain1, w_self)
    enc_1, enc_2 = over_x(after(enc_0, e_inv1)), over_z(after(enc_0, e_inv1))
    enc_3 = over_y(after(ffn_piece(0, 3), e_inv1))
    d_qkv, d_lse, d_hat1, d_inv1 = self_forward(
        1, after(x_dec, e_inv1), dec_col, dec_row, dec_gain1, w_self
    )
    enc = (enc_0, enc_1, enc_2, enc_3)
    w_enc = branch_plan(near_ffn, eighths(enc, swapped_after(enc, d_inv1), width), stride)
    cross_1, cross_2 = over_x(after(cross_0, d_inv1)), over_z(after(cross_0, d_inv1))
    cross_3 = over_y(after(cross_piece(3), d_inv1))
    dec_0 = over_y(after(ffn_piece(1, 0), d_inv1))
    e_slope, e_aslope, e_aact, e_hat2, e_inv2, y_enc = branch_forward(
        0, after(e_hat1, d_inv1), enc_gain1, enc_gain2, enc_downb, enc_upb, w_enc
    )
    crosses = (cross_0, cross_1, cross_2, cross_3)
    cross_swaps = swapped_after(crosses, e_inv2)
    w_cross = cross_plan(near_cross, quarters(crosses, cross_swaps, 1))
    dec_3 = over_y(after(ffn_piece(1, 3), e_inv2))
    kv = keys_forward(after(y_enc, dec_0), w_cross)
    kv_away = swap(kv, "section")
    dec_1, dec_2 = over_x(after(dec_0, kv)), over_z(after(dec_0, kv))
    d_q, c_lse, d_hat2, d_inv2 = cross_forward(
        d_hat1, dec_gain1, kv, kv_away, all_keys, dec_row, w_cross
    )
    dec = (dec_0, dec_1, dec_2, dec_3)
    w_dec = branch_plan(near_ffn, eighths(dec, swapped_after(dec, d_inv2), width), stride)
    g_keep, g_got = rows_sent(cotangent, kv)
    d_slope, d_aslope, d_aact, d_hat3, d_inv3, y_dec = branch_forward(
        1, d_hat2, mid_gain, dec_gain2, dec_downb, dec_upb, w_dec
    )
    g_enc, g_dec = rows_here(g_keep, g_got)

    def summed_here(grads):
        keep = lax.dynamic_index_in_dim(grads, core, 1, keepdims=False)
        give = lax.dynamic_index_in_dim(grads, 1 - core, 1, keepdims=False)
        return (keep.astype(F32) + swap(give, "section").astype(F32)).astype(BF16)

    def summed_side(both, token):
        got = after(swap(both[1], "mp"), token)
        return (both[0].astype(F32) + got.astype(F32)).astype(BF16)

    def summed_rows(value, over, token):
        for flip in over:
            got = after(lax.ppermute(value, MESH_AXES, route("dp", flip)), token)
            value = (value.astype(F32) + got.astype(F32)).astype(BF16)
        return value

    flips = [1 << i for i in range(lax.axis_size("dp").bit_length() - 1)]
    flips = flips[2:3] + flips[:2] + flips[3:]
    d_mid, d_grads = branch_backward(
        1, g_dec, d_hat3, d_inv3, dec_gain2, d_hat2, d_inv2, mid_gain,
        d_slope, d_aslope, d_aact, w_dec,
    )
    d_both = summed_here(d_grads)
    d_first, kv_grad, kv_grad_give = cross_backward(
        after(d_mid, d_both), d_hat1, d_inv1, dec_gain1, d_q, c_lse, kv, kv_away, all_keys, dec_row,
        w_cross,
    )
    kv_grad_away = swap(kv_grad_give, "section")
    e_out = keys_backward(g_enc, kv_grad, kv_grad_away, w_cross)
    e_first, e_grads = branch_backward(
        0, e_out, e_hat2, e_inv2, enc_gain2, e_hat1, e_inv1, enc_gain1,
        e_slope, e_aslope, e_aact, w_enc,
    )
    e_both = summed_here(e_grads)
    d_total = summed_side(d_both, e_first)
    d_first = after(d_first, e_both)
    bunches = len(w_self.steps) // 2

    def self_part(layer, grad, base, saved, lse, col, row, n):
        return self_backward(
            layer, grad, base, saved, lse, col, row, w_self, n * bunches, bunches
        )

    dx_dec = self_part(1, d_first, d_first, d_qkv, d_lse, dec_col, dec_row, 0)
    e_total = summed_side(e_both, dx_dec)
    d_total = summed_rows(d_total, flips[:1], dx_dec)
    outputs = rows_back(y_enc, y_dec)
    dx_dec = self_part(1, d_first, after(dx_dec, (e_total, outputs)), d_qkv, d_lse, dec_col, dec_row, 1)
    e_total = summed_rows(e_total, flips[:1], dx_dec)
    d_total = summed_rows(d_total, flips[1:2], dx_dec)
    e_first = after(e_first, (dx_dec, e_total))
    dx_enc = self_part(0, e_first, e_first, e_qkv, e_lse, enc_col, enc_row, 0)
    e_total = summed_rows(e_total, flips[1:2], dx_enc)
    d_total = summed_rows(d_total, flips[2:], dx_enc)
    dx_dec_back = layer_back(1, dx_dec)
    dx_enc = self_part(
        0, e_first, after(dx_enc, (e_total, d_total, dx_dec_back)), e_qkv, e_lse, enc_col, enc_row, 1
    )
    e_total = summed_rows(e_total, flips[2:], dx_enc)
    dx = jnp.where(first_core, layer_back(0, dx_enc), dx_dec_back)
    mine = jnp.where(first_core, e_total, d_total)
    other = swap(jnp.where(first_core, d_total, e_total), "section")
    down_total = jnp.where(first_core, mine, other)[:units].astype(F32)
    down_total = jnp.transpose(down_total.reshape(units, -1, units), (1, 0, 2)).reshape(width, units)
    up_total = jnp.where(first_core, other, mine).astype(F32)
    dx = jnp.where(first_core, layer_back(0, dx_enc), dx_dec_back)

    return (
        outputs[None],
        dx.astype(F32)[None],
        down_total[None],
        up_total[units : units + 1, :units],
        up_total[:units][None],
        up_total[units + 1 : units + 2],
    )


def solution(mesh):
    in_specs = (
        P("section", "dp", "mp", None),
        P(None, "dp", None),
        P("section", "dp", "mp", None),
        P("section", None, None),
        P(),
        P("section", None, None, "mp"),
        P("section", "mp", None),
        P("section", None, "mp"),
        P("section", None, "mp"),
        P("section", None, "mp"),
        P("section", "mp", None),
        P("section", None, "mp"),
        P("section", "mp"),
        P("section", "mp", None),
        P("section", None),
    )
    out_specs = (
        P("section", "dp", "mp", None),
        P("section", "dp", "mp", None),
        P("section", None, "mp"),
        P("section", "mp"),
        P("section", "mp", None),
        P("section", None),
    )
    return jax.shard_map(
        per_device, mesh=mesh, in_specs=in_specs, out_specs=out_specs, check_vma=False
    )
```

```python
import functools

import jax
import jax.numpy as jnp
from jax import lax
from jax.experimental import pallas as pl
from jax.experimental.pallas import tpu as pltpu
from jax.sharding import PartitionSpec as P

HEADDIM = 64
BUNCH = 4
WIDE = BUNCH * HEADDIM
CHUNK = 1024
SCALE = HEADDIM**-0.5
LANES = 128
PART = 256
EXTRA = 16
HIDDEN_MASK = -1e30
VMEM_LIMIT = 60 * 1024 * 1024
BF16 = jnp.bfloat16
F32 = jnp.float32


def dot_nn(left, right):
    return lax.dot_general(left, right, (((1,), (0,)), ((), ())), preferred_element_type=F32)


def dot_nt(left, right):
    return lax.dot_general(left, right, (((1,), (1,)), ((), ())), preferred_element_type=F32)


def dot_tn(left, right):
    return lax.dot_general(left, right, (((0,), (0,)), ((), ())), preferred_element_type=F32)


class Plan:
    def __init__(self, bufs):
        self.pairs = []
        self.steps = []
        self.bufs = bufs

    def part(self, first, count):
        some = Plan(self.bufs)
        for copies in self.steps[first : first + count]:
            some.steps.append([(some.add(*self.pairs[c[0]]),) + tuple(c[1:]) for c in copies])
        return some

    def add(self, *arrays):
        for i, pair in enumerate(self.pairs):
            if pair[0] is arrays[0]:
                return i
        self.pairs.append(arrays)
        return len(self.pairs) - 1


def at(index):
    return lambda: index


def block(start, size):
    return pl.ds(start, size)


def advance(plan, refs, bufs, sems, layer, step):
    count = len(plan.steps)
    mine = lax.axis_index("section") == layer
    slot = lax.rem(step, 2)

    firsts = [sum(len(p) for p in plan.pairs[:i]) for i in range(len(plan.pairs))]

    def start(copies, side, to):
        for pair, source, buf, place in copies:
            src = refs[firsts[pair] + side].at[source()]
            dst = bufs[buf].at[(to,) + tuple(place())]
            pltpu.make_async_copy(src, dst, sems[buf].at[to]).start()

    def issue(which, to):
        start([c for c in plan.steps[which] if len(plan.pairs[c[0]]) == 1], 0, to)
        layered = [c for c in plan.steps[which] if len(plan.pairs[c[0]]) == 2]
        if layered:

            @pl.when(mine)
            def _():
                start(layered, 0, to)

            @pl.when(jnp.logical_not(mine))
            def _():
                start(layered, 1, to)

    @pl.when(step == 0)
    def _():
        issue(0, 0)

    for which in range(1, count):

        @pl.when(step + 1 == which)
        def _():
            issue(which, which % 2)

    used = [sorted({c[2] for c in copies}) for copies in plan.steps]

    def settle(buf):
        pltpu.make_async_copy(bufs[buf].at[slot], bufs[buf].at[slot], sems[buf].at[slot]).wait()

    first = 0
    for which in range(1, count + 1):
        if which == count or used[which] != used[first]:
            if first == 0 and which == count:
                for buf in used[first]:
                    settle(buf)
            else:

                @pl.when((step >= first) & (step < which))
                def _():
                    for buf in used[first]:
                        settle(buf)

            first = which
    return slot


def call(body, operands, in_blocks, plan, out_shapes, out_blocks, scratch, cost):
    arrays = [a for pair in plan.pairs for a in pair]
    n_ops, n_out, n_buf = len(operands), len(out_shapes), len(plan.bufs)

    def kernel(*refs):
        ins, rest = refs[:n_ops], refs[n_ops:]
        wrefs, rest = rest[: len(arrays)], rest[len(arrays) :]
        outs, rest = rest[:n_out], rest[n_out:]
        bufs, rest = rest[:n_buf], rest[n_buf:]
        sems, extra = rest[:n_buf], rest[n_buf:]
        body(ins, wrefs, outs, bufs, sems, extra)

    return pl.pallas_call(
        kernel,
        grid=(len(plan.steps),),
        in_specs=list(in_blocks) + [pl.BlockSpec(memory_space=pltpu.HBM)] * len(arrays),
        out_specs=tuple(out_blocks),
        out_shape=tuple(out_shapes),
        scratch_shapes=[pltpu.VMEM((2,) + tuple(b), BF16) for b in plan.bufs]
        + [pltpu.SemaphoreType.DMA((2,)) for _ in plan.bufs]
        + list(scratch),
        compiler_params=pltpu.CompilerParams(
            dimension_semantics=("arbitrary",), vmem_limit_bytes=VMEM_LIMIT
        ),
        cost_estimate=pl.CostEstimate(
            flops=int(3 * cost), bytes_accessed=int(cost // 200), transcendentals=0
        ),
    )(*operands, *arrays)


ALL = slice(None)
QUARTER = 128


def self_plan(near, far):
    width = near[0][0].shape[1]
    plan = Plan([(3, width, WIDE), (WIDE, width)])
    qkv, out = plan.add(*near[0]), plan.add(*near[1])
    for g in range(near[0][0].shape[2] // WIDE):
        cols = block(g * WIDE, WIDE)
        plan.steps.append(
            [(qkv, at((ALL, ALL, cols)), 0, at(())), (out, at((cols, ALL)), 1, at(()))]
        )
    for g in range(len(far) // 2):
        copies = []
        for j in range(2):
            first, second, base = far[2 * g + j]
            a, b = plan.add(*first), plan.add(*second)
            lanes = block(j * QUARTER, QUARTER)
            copies.append((a, at((block(0, 2),)), 0, at((block(0, 2), ALL, lanes))))
            copies.append((b, at((base,)), 0, at((2, ALL, lanes))))
            for k in range(width // QUARTER):
                here = block(k * QUARTER, QUARTER)
                copies.append((b, at((base + 1, here, ALL)), 1, at((lanes, here))))
        plan.steps.append(copies)
    return plan


def cross_plan(near, far):
    width = near[0][0].shape[0]
    plan = Plan([(width, WIDE), (width, WIDE)])
    ckv, cvo = plan.add(*near[0]), plan.add(*near[1])
    for g in range(near[0][0].shape[1] // WIDE):
        cols = block(g * WIDE, WIDE)
        plan.steps.append([(ckv, at((ALL, cols)), 0, at(())), (cvo, at((ALL, cols)), 1, at(()))])
    for g in range(len(far) // 2):
        copies = []
        for j in range(2):
            first, second, base = far[2 * g + j]
            a, b = plan.add(*first), plan.add(*second)
            lanes = block(j * QUARTER, QUARTER)
            copies.append((a, at((0,)), 0, at((ALL, lanes))))
            copies.append((b, at((base,)), 1, at((ALL, lanes))))
        plan.steps.append(copies)
    return plan


def branch_plan(near, far, stride):
    width, hidden = near[0][0].shape
    units = near[2][0].shape[1]
    piece = width // 8
    plan = Plan([(width, CHUNK), (CHUNK, width), (width, units), (units, width)])
    up, down, adown, aup = [plan.add(*pair) for pair in near]
    for g in range(hidden // CHUNK):
        cols = block(g * CHUNK, CHUNK)
        plan.steps.append([(up, at((ALL, cols)), 0, at(())), (down, at((cols, ALL)), 1, at(()))])
    adapter = []
    each = CHUNK // (2 * WIDE)
    for j, both in enumerate(far):
        copies = [] if j % each == 0 else copies
        for k, (first, second, base) in enumerate(both):
            a, b = plan.add(first), plan.add(second)
            cols = block((j % each * 2 + k) * WIDE, WIDE)
            copies.append((a, at((block(0, width), ALL)), 0, at((ALL, cols))))
            for n in range(width // WIDE):
                rows = block(base + n * WIDE, WIDE)
                copies.append((b, at((rows, ALL)), 1, at((cols, block(n * WIDE, WIDE)))))

            def spot(j=j, k=k):
                return block(pl.multiple_of(eighth_of(j, k, stride) * piece, piece), piece)

            rows = block(base + width, piece)
            adapter.append((b, at((rows, ALL)), 2, lambda spot=spot: (spot(), ALL)))
            for n in range(units // piece):
                rows = block(base + width + piece, piece)
                here = block(n * piece, piece)
                adapter.append(
                    (b, at((rows, here)), 3, lambda spot=spot, here=here: (here, spot()))
                )
        if j % each == each - 1:
            plan.steps.append(copies)
    plan.steps.append([(adown, at(()), 2, at(())), (aup, at(()), 3, at(()))])
    plan.steps.append(adapter)
    return plan


def share_of(j, stride):
    place = lax.axis_index("dp")
    x = lax.rem(place, 2)
    z = lax.rem(lax.div(place, stride), 2)
    x = 1 - x if j in (1, 3) else x
    z = 1 - z if j in (2, 3) else z
    return 2 * x + z


def eighth_of(j, k, stride):
    core = lax.axis_index("section")
    return 4 * (1 - core if k else core) + share_of(j, stride)


def cut_piece(pairs, layer, shape, moves):
    plan = Plan([])
    plan.pairs = pairs
    firsts = [sum(len(p) for p in pairs[:i]) for i in range(len(pairs))]
    arrays = [a for pair in pairs for a in pair]

    def kernel(*refs):
        ins, out, sem = refs[: len(arrays)], refs[-2], refs[-1]

        def start(side):
            for pair, index, place in moves:
                src = ins[firsts[pair] + side].at[index()]
                pltpu.make_async_copy(src, out.at[place()], sem).start()

        if layer is None:
            start(0)
        else:
            mine = lax.axis_index("section") == layer

            @pl.when(mine)
            def _():
                start(0)

            @pl.when(jnp.logical_not(mine))
            def _():
                start(1)

        pltpu.make_async_copy(out, out, sem).wait()

    return pl.pallas_call(
        kernel,
        in_specs=[pl.BlockSpec(memory_space=pltpu.HBM)] * len(arrays),
        out_specs=pl.BlockSpec(memory_space=pltpu.VMEM),
        out_shape=shaped(shape, BF16),
        scratch_shapes=[pltpu.SemaphoreType.DMA],
        compiler_params=pltpu.CompilerParams(vmem_limit_bytes=8 * 1024 * 1024),
    )(*arrays)


def whole(shape):
    zeros = (0,) * len(shape)
    return pl.BlockSpec(tuple(shape), lambda i: zeros)


def per_step(shape, first=0, last=None):
    def index(i):
        k = jnp.maximum(i - first, 0)
        if last is not None:
            k = jnp.minimum(k, last)
        return (k,) + (0,) * len(shape)

    return pl.BlockSpec((1,) + tuple(shape), index)


def shaped(shape, dtype):
    return jax.ShapeDtypeStruct(tuple(shape), dtype)


def normalized(value):
    center = value - jnp.mean(value, -1, keepdims=True)
    spread = jnp.mean(center * center, -1, keepdims=True)
    inverse = lax.rsqrt(spread + 1e-05)
    return center * inverse, inverse


def norm_slope(grad, hat, inverse, gain):
    scaled = grad * gain
    along = jnp.mean(scaled * hat, -1, keepdims=True)
    return inverse * (scaled - jnp.mean(scaled, -1, keepdims=True) - hat * along)


def gelu_pair(value):
    below = 0.5 + 0.5 * lax.erf(value * (0.5**0.5))
    density = jnp.exp(value * value * -0.5) * 0.3989422804014327
    return value * below, below + value * density


def lanes_of(head):
    first = head * HEADDIM // LANES * LANES
    return slice(first, first + LANES)


def only_head(value, head):
    lane = lax.broadcasted_iota(jnp.int32, (1, LANES), 1)
    inside = head * HEADDIM % LANES
    keep = (lane >= inside) & (lane < inside + HEADDIM)
    part = value[:, lanes_of(head)]
    return jnp.where(keep, part, jnp.zeros_like(part))


def attend(blocks, q_ref, k_ref, v_ref, bias_ref, valid_ref, lse_ref, out_ref):
    units = [(rows, keys, head) for rows, keys in blocks for head in range(BUNCH)]

    def scores_of(unit):
        rows, keys, head = unit
        q_head = only_head(q_ref[rows, :] * jnp.asarray(SCALE, BF16), head)
        return dot_nt(k_ref[keys, lanes_of(head)], q_head)

    ahead = scores_of(units[0])
    for i, (rows, keys, head) in enumerate(units):
        scores = ahead + bias_ref[keys, rows]
        if i + 1 < len(units):
            ahead = scores_of(units[i + 1])
        peak = jnp.max(scores, 0, keepdims=True)
        powers = jnp.exp(scores - peak)
        total = jnp.sum(powers, 0, keepdims=True)
        share = 1.0 / total
        lse = peak + jnp.log(total)
        if valid_ref is not None:
            valid = valid_ref[:, rows] > 0.0
            share = jnp.where(valid, share, 0.0)
            lse = jnp.where(valid, lse, -HIDDEN_MASK)
        lse_ref[head : head + 1, rows] = lse
        mixed = dot_tn((powers * share).astype(BF16), only_head(v_ref[keys, :], head))
        out_ref[rows, lanes_of(head)] += mixed


def attend_slope(blocks, q_ref, k_ref, v_ref, g_ref, bias_ref, lse_ref, dq_ref, dk_ref, dv_ref):
    units = [(rows, keys, head) for rows, keys in blocks for head in range(BUNCH)]

    def products_of(unit):
        rows, keys, head = unit
        q_head = only_head(q_ref[rows, :] * jnp.asarray(SCALE, BF16), head)
        g_head = only_head(g_ref[rows, :], head)
        lanes = lanes_of(head)
        return q_head, g_head, dot_nt(k_ref[keys, lanes], q_head), dot_nt(v_ref[keys, lanes], g_head)

    ahead = products_of(units[0])
    for i, (rows, keys, head) in enumerate(units):
        q_head, g_head, scores, prob_grad = ahead
        if i + 1 < len(units):
            ahead = products_of(units[i + 1])
        lanes = lanes_of(head)
        probs = jnp.exp(scores + bias_ref[keys, rows] - lse_ref[head : head + 1, rows])
        inner = jnp.sum(probs * prob_grad, 0, keepdims=True)
        score_grad = (probs * (prob_grad - inner)).astype(BF16)
        dv_ref[keys, lanes] += dot_nn(probs.astype(BF16), g_head)
        dk_ref[keys, lanes] += dot_nn(score_grad, q_head)
        dq_ref[rows, lanes] += dot_tn(score_grad, only_head(k_ref[keys, :], head))


def fill_bias(bias_ref, key_seg, row_seg, causal):
    seen = key_seg == row_seg
    if causal:
        key = lax.broadcasted_iota(jnp.int32, bias_ref.shape, 0)
        row = lax.broadcasted_iota(jnp.int32, bias_ref.shape, 1)
        seen = seen & (key <= row)
    bias_ref[...] = jnp.where(seen, 0.0, HIDDEN_MASK)


def self_blocks(rows, causal):
    if not causal:
        return [(slice(0, rows), slice(0, rows))]
    count = rows // PART
    parts = [slice(i * PART, (i + 1) * PART) for i in range(count)]
    return [(part, slice(0, part.stop)) for part in parts]


def cross_blocks(rows):
    return [(slice(i, i + PART), slice(0, rows)) for i in range(0, rows, PART)]


def note_active(bias, valid, active, rows):
    for h in range(2):
        best = jnp.max(bias[h], 0, keepdims=True)
        valid[h] = jnp.where(best > 0.5 * HIDDEN_MASK, 1.0, 0.0)
        for i in range(rows // PART):
            some = jnp.max(valid[h, :, i * PART : (i + 1) * PART])
            active[h, i] = (some > 0.0).astype(jnp.int32)


def self_forward(layer, x, seg_col, seg_row, gain, plan):
    rows, width = x.shape
    steps = len(plan.steps)

    def body(ins, wrefs, outs, bufs, sems, extra):
        x_ref, segc_ref, segr_ref, gain_ref = ins
        qkv_ref, lse_ref, hat_ref, inv_ref = outs
        acc, bias, mixed = extra
        step = pl.program_id(0)
        slot = advance(plan, wrefs, bufs, sems, layer, step)

        @pl.when(step == 0)
        def _():
            fill_bias(bias, segc_ref[...], segr_ref[...], layer == 1)
            acc[...] = x_ref[...].astype(F32)

        x_rows = x_ref[...]
        w = bufs[0].at[slot]
        q = dot_nn(x_rows, w[0]).astype(BF16)
        k = dot_nn(x_rows, w[1]).astype(BF16)
        v = dot_nn(x_rows, w[2]).astype(BF16)
        qkv_ref[0, 0] = q
        qkv_ref[0, 1] = k
        qkv_ref[0, 2] = v
        mixed[...] = jnp.zeros_like(mixed)
        attend(
            self_blocks(rows, layer == 1), qkv_ref.at[0, 0], qkv_ref.at[0, 1], qkv_ref.at[0, 2],
            bias, None, lse_ref.at[0], mixed,
        )
        acc[...] += dot_nn(mixed[...].astype(BF16), bufs[1][slot])

        @pl.when(step == steps - 1)
        def _():
            hat, inverse = normalized(acc[...])
            hat_ref[...] = hat.astype(BF16)
            inv_ref[...] = inverse

    return call(
        body,
        [x, seg_col, seg_row, gain],
        [whole(x.shape), whole(seg_col.shape), whole(seg_row.shape), whole(gain.shape)],
        plan,
        [
            shaped((steps, 3, rows, WIDE), BF16),
            shaped((steps, BUNCH, rows), F32),
            shaped((rows, width), BF16),
            shaped((rows, 1), F32),
        ],
        [
            per_step((3, rows, WIDE)),
            per_step((BUNCH, rows)),
            whole((rows, width)),
            whole((rows, 1)),
        ],
        [
            pltpu.VMEM((rows, width), F32),
            pltpu.VMEM((rows, rows), F32),
            pltpu.VMEM((rows, WIDE), F32),
        ],
        steps * (2 * rows * width * WIDE * 4 + 16 * rows * rows * WIDE),
    )


def self_backward(layer, grad, base, saved, lse, seg_col, seg_row, plan, first, count):
    rows, width = grad.shape
    steps = count
    plan = plan.part(first, count)

    def body(ins, wrefs, outs, bufs, sems, extra):
        g_ref, base_ref, saved_ref, lse_ref, segc_ref, segr_ref = ins
        (dx_ref,) = outs
        acc, bias, mixed_grad, dq, dk, dv = extra
        step = pl.program_id(0)
        slot = advance(plan, wrefs, bufs, sems, layer, step)

        @pl.when(step == 0)
        def _():
            fill_bias(bias, segc_ref[...], segr_ref[...], layer == 1)
            acc[...] = base_ref[...].astype(F32)

        mixed_grad[...] = dot_nt(g_ref[...], bufs[1][slot]).astype(BF16)
        for ref in (dq, dk, dv):
            ref[...] = jnp.zeros_like(ref)
        attend_slope(
            self_blocks(rows, layer == 1), saved_ref.at[0, 0], saved_ref.at[0, 1],
            saved_ref.at[0, 2], mixed_grad, bias, lse_ref.at[0], dq, dk, dv,
        )
        w = bufs[0].at[slot]
        acc[...] += (
            dot_nt((dq[...] * SCALE).astype(BF16), w[0])
            + dot_nt(dk[...].astype(BF16), w[1])
            + dot_nt(dv[...].astype(BF16), w[2])
        )

        @pl.when(step == steps - 1)
        def _():
            dx_ref[...] = acc[...].astype(BF16)

    return call(
        body,
        [grad, base, saved, lse, seg_col, seg_row],
        [
            whole(grad.shape),
            whole(grad.shape),
            per_step((3, rows, WIDE), -first),
            per_step((BUNCH, rows), -first),
            whole(seg_col.shape),
            whole(seg_row.shape),
        ],
        plan,
        [shaped((rows, width), BF16)],
        [whole((rows, width))],
        [
            pltpu.VMEM((rows, width), F32),
            pltpu.VMEM((rows, rows), F32),
            pltpu.VMEM((rows, WIDE), BF16),
            pltpu.VMEM((rows, WIDE), F32),
            pltpu.VMEM((rows, WIDE), F32),
            pltpu.VMEM((rows, WIDE), F32),
        ],
        steps * (2 * rows * width * WIDE * 4 + 40 * rows * rows * WIDE),
    )[0]


def cross_forward(hat, gain, kv_own, kv_away, keys_col, seg_row, plan):
    rows, width = hat.shape
    steps = len(plan.steps)

    def body(ins, wrefs, outs, bufs, sems, extra):
        hat_ref, gain_ref, own_ref, away_ref, keysc_ref, segr_ref = ins
        q_ref, lse_ref, nhat_ref, inv_ref = outs
        acc, low, bias, mixed, valid, active = extra
        step = pl.program_id(0)
        slot = advance(plan, wrefs, bufs, sems, 1, step)

        @pl.when(step == 0)
        def _():
            for h in range(2):
                fill_bias(bias.at[h], keysc_ref[h], segr_ref[...], False)
            note_active(bias, valid, active, rows)
            first = hat_ref[...].astype(F32) * gain_ref[...]
            acc[...] = first
            low[...] = first.astype(BF16)

        q = dot_nn(low[...], bufs[0][slot]).astype(BF16)
        q_ref[0] = q
        mixed[...] = jnp.zeros_like(mixed)
        for h, kv_ref in enumerate((own_ref, away_ref)):
            for i, pair in enumerate(cross_blocks(rows)):

                @pl.when(active[h, i] > 0)
                def _():
                    attend(
                        [pair], q_ref.at[0], kv_ref.at[0, 0], kv_ref.at[0, 1],
                        bias.at[h], valid.at[h], lse_ref.at[0, h], mixed,
                    )

        acc[...] += dot_nt(mixed[...].astype(BF16), bufs[1][slot])

        @pl.when(step == steps - 1)
        def _():
            nhat, inverse = normalized(acc[...])
            nhat_ref[...] = nhat.astype(BF16)
            inv_ref[...] = inverse

    return call(
        body,
        [hat, gain, kv_own, kv_away, keys_col, seg_row],
        [
            whole(hat.shape),
            whole(gain.shape),
            per_step((2, rows, WIDE)),
            per_step((2, rows, WIDE)),
            whole(keys_col.shape),
            whole(seg_row.shape),
        ],
        plan,
        [
            shaped((steps, rows, WIDE), BF16),
            shaped((steps, 2, BUNCH, rows), F32),
            shaped((rows, width), BF16),
            shaped((rows, 1), F32),
        ],
        [
            per_step((rows, WIDE)),
            per_step((2, BUNCH, rows)),
            whole((rows, width)),
            whole((rows, 1)),
        ],
        [
            pltpu.VMEM((rows, width), F32),
            pltpu.VMEM((rows, width), BF16),
            pltpu.VMEM((2, rows, rows), F32),
            pltpu.VMEM((rows, WIDE), F32),
            pltpu.VMEM((2, 1, rows), F32),
            pltpu.SMEM((2, rows // PART), jnp.int32),
        ],
        steps * (2 * rows * width * WIDE * 2 + 32 * rows * rows * WIDE),
    )


def cross_backward(grad, hat, inv, gain, saved_q, lse, kv_own, kv_away, keys_col, seg_row, plan):
    rows, width = grad.shape
    steps = len(plan.steps)

    def body(ins, wrefs, outs, bufs, sems, extra):
        g_ref, hat_ref, inv_ref, gain_ref, q_ref, lse_ref, own_ref, away_ref, keysc_ref, segr_ref = ins
        dx_ref, own_grad_ref, away_grad_ref = outs
        acc, bias, mixed_grad, dq, dk, dv, valid, active = extra
        step = pl.program_id(0)
        slot = advance(plan, wrefs, bufs, sems, 1, step)

        @pl.when(step == 0)
        def _():
            for h in range(2):
                fill_bias(bias.at[h], keysc_ref[h], segr_ref[...], False)
            note_active(bias, valid, active, rows)
            acc[...] = g_ref[...].astype(F32)

        mixed_grad[...] = dot_nn(g_ref[...], bufs[1][slot]).astype(BF16)
        for ref in (dq, dk, dv):
            ref[...] = jnp.zeros_like(ref)
        for h, kv_ref in enumerate((own_ref, away_ref)):
            for i, pair in enumerate(cross_blocks(rows)):

                @pl.when(active[h, i] > 0)
                def _():
                    attend_slope(
                        [pair], q_ref.at[0], kv_ref.at[0, 0], kv_ref.at[0, 1], mixed_grad,
                        bias.at[h], lse_ref.at[0, h], dq, dk.at[h], dv.at[h],
                    )

        for h, out_ref in enumerate((own_grad_ref, away_grad_ref)):
            out_ref[0, 0] = dk[h].astype(BF16)
            out_ref[0, 1] = dv[h].astype(BF16)
        acc[...] += dot_nt((dq[...] * SCALE).astype(BF16), bufs[0][slot])

        @pl.when(step == steps - 1)
        def _():
            dx_ref[...] = norm_slope(
                acc[...], hat_ref[...].astype(F32), inv_ref[...], gain_ref[...]
            ).astype(BF16)

    return call(
        body,
        [grad, hat, inv, gain, saved_q, lse, kv_own, kv_away, keys_col, seg_row],
        [
            whole(grad.shape),
            whole(hat.shape),
            whole(inv.shape),
            whole(gain.shape),
            per_step((rows, WIDE)),
            per_step((2, BUNCH, rows)),
            per_step((2, rows, WIDE)),
            per_step((2, rows, WIDE)),
            whole(keys_col.shape),
            whole(seg_row.shape),
        ],
        plan,
        [
            shaped((rows, width), BF16),
            shaped((steps, 2, rows, WIDE), BF16),
            shaped((steps, 2, rows, WIDE), BF16),
        ],
        [whole((rows, width)), per_step((2, rows, WIDE)), per_step((2, rows, WIDE))],
        [
            pltpu.VMEM((rows, width), F32),
            pltpu.VMEM((2, rows, rows), F32),
            pltpu.VMEM((rows, WIDE), BF16),
            pltpu.VMEM((rows, WIDE), F32),
            pltpu.VMEM((2, rows, WIDE), F32),
            pltpu.VMEM((2, rows, WIDE), F32),
            pltpu.VMEM((2, 1, rows), F32),
            pltpu.SMEM((2, rows // PART), jnp.int32),
        ],
        steps * (2 * rows * width * WIDE * 2 + 80 * rows * rows * WIDE),
    )


def keys_forward(y, plan):
    rows, width = y.shape
    steps = len(plan.steps)

    def body(ins, wrefs, outs, bufs, sems, extra):
        (kv_ref,) = outs
        slot = advance(plan, wrefs, bufs, sems, 0, pl.program_id(0))
        kv_ref[0, 0] = dot_nn(ins[0][...], bufs[0][slot]).astype(BF16)
        kv_ref[0, 1] = dot_nn(ins[0][...], bufs[1][slot]).astype(BF16)

    return call(
        body,
        [y],
        [whole(y.shape)],
        plan,
        [shaped((steps, 2, rows, WIDE), BF16)],
        [per_step((2, rows, WIDE))],
        [],
        steps * 4 * rows * width * WIDE,
    )[0]


def keys_backward(out_grad, kv_grad, kv_grad_away, plan):
    rows, width = out_grad.shape
    steps = len(plan.steps)

    def body(ins, wrefs, outs, bufs, sems, extra):
        g_ref, own_ref, away_ref = ins
        (sum_ref,) = outs
        (acc,) = extra
        step = pl.program_id(0)
        slot = advance(plan, wrefs, bufs, sems, 0, step)

        @pl.when(step == 0)
        def _():
            acc[...] = g_ref[...].astype(F32)

        both = (own_ref[0].astype(F32) + away_ref[0].astype(F32)).astype(BF16)
        acc[...] += dot_nt(both[0], bufs[0][slot]) + dot_nt(both[1], bufs[1][slot])

        @pl.when(step == steps - 1)
        def _():
            sum_ref[...] = acc[...].astype(BF16)

    return call(
        body,
        [out_grad, kv_grad, kv_grad_away],
        [whole(out_grad.shape), per_step((2, rows, WIDE)), per_step((2, rows, WIDE))],
        plan,
        [shaped((rows, width), BF16)],
        [whole((rows, width))],
        [pltpu.VMEM((rows, width), F32)],
        steps * 4 * rows * width * WIDE,
    )[0]


def branch_forward(layer, hat, gain, out_gain, down_bias, up_bias, plan):
    rows, width = hat.shape
    nb = 2
    na = len(plan.steps) - nb
    units = down_bias.shape[-1]
    steps = na + nb

    def body(ins, wrefs, outs, bufs, sems, extra):
        hat_ref, gain_ref, ogain_ref, dbias_ref, ubias_ref = ins
        slope_ref, aslope_ref, aact_ref, nhat_ref, inv_ref, y_ref = outs
        acc, low = extra
        step = pl.program_id(0)
        slot = advance(plan, wrefs, bufs, sems, layer, step)

        @pl.when(step == 0)
        def _():
            first = hat_ref[...].astype(F32) * gain_ref[...]
            low[...] = first.astype(BF16)
            acc[...] = first + 4.0 * ubias_ref[...]

        @pl.when(step < na)
        def _():
            for at in range(0, rows, 512):
                part = slice(at, at + 512)
                act, slope = gelu_pair(dot_nn(low[part, :], bufs[0][slot]))
                slope_ref[0, part, :] = slope.astype(BF16)
                acc[part, :] += dot_nn(act.astype(BF16), bufs[1][slot])

        @pl.when(step >= na)
        def _():
            act, slope = gelu_pair(dot_nn(low[...], bufs[2][slot]) + dbias_ref[0])
            low_act = act.astype(BF16)
            aslope_ref[0] = slope.astype(BF16)
            aact_ref[0] = low_act
            acc[...] += dot_nn(low_act * jnp.asarray(4.0, BF16), bufs[3][slot])

        @pl.when(step == steps - 1)
        def _():
            nhat, inverse = normalized(acc[...])
            nhat_ref[...] = nhat.astype(BF16)
            inv_ref[...] = inverse
            y_ref[...] = (nhat * ogain_ref[...]).astype(BF16)

    return call(
        body,
        [hat, gain, out_gain, down_bias, up_bias],
        [
            whole(hat.shape),
            whole(gain.shape),
            whole(out_gain.shape),
            per_step((1, units), na),
            whole(up_bias.shape),
        ],
        plan,
        [
            shaped((na, rows, CHUNK), BF16),
            shaped((nb, rows, units), BF16),
            shaped((nb, rows, units), BF16),
            shaped((rows, width), BF16),
            shaped((rows, 1), F32),
            shaped((rows, width), BF16),
        ],
        [
            per_step((rows, CHUNK), 0, na - 1),
            per_step((rows, units), na),
            per_step((rows, units), na),
            whole((rows, width)),
            whole((rows, 1)),
            whole((rows, width)),
        ],
        [pltpu.VMEM((rows, width), F32), pltpu.VMEM((rows, width), BF16)],
        4 * rows * width * (na * CHUNK + nb * units),
    )


def branch_backward(layer, out_grad, nhat, ninv, out_gain, hat, inv, gain, slope, aslope, aact, plan):
    rows, width = hat.shape
    nb = 2
    na = len(plan.steps) - nb
    units = aact.shape[-1]
    steps = na + nb

    def body(ins, wrefs, outs, bufs, sems, extra):
        g_ref, nhat_ref, ninv_ref, ogain_ref, hat_ref, inv_ref, gain_ref, slope_ref, aslope_ref, aact_ref = ins
        dx_ref, packed_ref = outs
        acc, low, rows_low, up_bias = extra
        step = pl.program_id(0)
        slot = advance(plan, wrefs, bufs, sems, layer, step)

        @pl.when(step == 0)
        def _():
            grad = norm_slope(
                g_ref[...].astype(F32), nhat_ref[...].astype(F32), ninv_ref[...], ogain_ref[...]
            )
            acc[...] = grad
            small = grad.astype(BF16)
            low[...] = small
            up_bias[...] = 4.0 * jnp.sum(small.astype(F32), 0, keepdims=True)
            rows_low[...] = (hat_ref[...].astype(F32) * gain_ref[...]).astype(BF16)

        @pl.when(step < na)
        def _():
            for at in range(0, rows, 512):
                part = slice(at, at + 512)
                hidden = dot_nt(low[part, :], bufs[1][slot]) * slope_ref[0, part, :].astype(F32)
                acc[part, :] += dot_nt(hidden.astype(BF16), bufs[0][slot])

        @pl.when(step >= na)
        def _():
            hidden = 4.0 * dot_nt(low[...], bufs[3][slot]) * aslope_ref[0].astype(F32)
            small = hidden.astype(BF16)
            acc[...] += dot_nt(small, bufs[2][slot])
            down = dot_tn(rows_low[...], small).astype(BF16)
            for n in range(width // units):
                cols = slice(n * units, (n + 1) * units)
                packed_ref[0, 0, :units, cols] = down[cols]
            packed_ref[0, 1, :units] = (4.0 * dot_tn(aact_ref[0], low[...])).astype(BF16)
            bias = jnp.sum(small.astype(F32), 0, keepdims=True)
            bias = jnp.concatenate([bias] + [jnp.zeros_like(bias)] * (width // units - 1), 1)
            row = lax.broadcasted_iota(jnp.int32, (EXTRA, width), 0)
            last = jnp.where(row == 0, bias, jnp.where(row == 1, up_bias[...], 0.0))
            packed_ref[0, 0, units:] = jnp.zeros((EXTRA, width), BF16)
            packed_ref[0, 1, units:] = last.astype(BF16)

        @pl.when(step == steps - 1)
        def _():
            dx_ref[...] = norm_slope(
                acc[...], hat_ref[...].astype(F32), inv_ref[...], gain_ref[...]
            ).astype(BF16)

    return call(
        body,
        [out_grad, nhat, ninv, out_gain, hat, inv, gain, slope, aslope, aact],
        [
            whole(out_grad.shape),
            whole(nhat.shape),
            whole(ninv.shape),
            whole(out_gain.shape),
            whole(hat.shape),
            whole(inv.shape),
            whole(gain.shape),
            per_step((rows, CHUNK), 0, na - 1),
            per_step((rows, units), na),
            per_step((rows, units), na),
        ],
        plan,
        [
            shaped((rows, width), BF16),
            shaped((nb, 2, units + EXTRA, width), BF16),
        ],
        [
            whole((rows, width)),
            per_step((2, units + EXTRA, width), na),
        ],
        [
            pltpu.VMEM((rows, width), F32),
            pltpu.VMEM((rows, width), BF16),
            pltpu.VMEM((rows, width), BF16),
            pltpu.VMEM((1, width), F32),
        ],
        4 * rows * width * (na * CHUNK + nb * units),
    )


class Lane:
    def __init__(self, depth):
        self.depth = depth
        self.sent = []

    def send(self, value, axes, route):
        if len(self.sent) >= self.depth:
            value, _ = lax.optimization_barrier((value, self.sent[-self.depth]))
        got = lax.ppermute(value, axes, route)
        self.sent.append(got)
        return got


MESH_AXES = ("section", "mp", "dp")


def route(axis, flip, core=None):
    sizes = [lax.axis_size(a) for a in MESH_AXES]
    pairs = []
    for s in range(sizes[0]):
        for m in range(sizes[1]):
            for d in range(sizes[2]):
                if core is not None and s != core:
                    continue
                to = [s, m, d]
                to[MESH_AXES.index(axis)] ^= flip
                number = lambda p: (p[0] * sizes[1] + p[1]) * sizes[2] + p[2]
                pairs.append((number((s, m, d)), number(to)))
    return pairs


def after(value, token):
    return lax.optimization_barrier((value, token))[0]


def swap(value, axis):
    return jax.tree.map(lambda a: lax.ppermute(a, axis, [(0, 1), (1, 0)]), value)


def rotated(pieces, start, count):
    return lax.dynamic_slice_in_dim(jnp.concatenate(pieces, 0), start, count, 0)


def per_device(
    inputs,
    segment_ids,
    cotangent,
    norm_gains,
    cross_gain,
    self_qkv,
    self_out,
    cross_kv,
    cross_vo,
    ffn_in,
    ffn_out,
    adapter_down,
    adapter_down_bias,
    adapter_up,
    adapter_up_bias,
):
    core = lax.axis_index("section")
    side = lax.axis_index("mp")
    first_core = core == 0
    seq = segment_ids.shape[2]
    half = seq // 2
    width = inputs.shape[3]
    units = adapter_down.shape[2]

    stride = max(lax.axis_size("dp") // 4, 1)
    lane_y, lane_x, lane_z, lane_core = Lane(1), Lane(2), Lane(2), Lane(3)

    def over_y(value):
        return lane_y.send(value, MESH_AXES, route("mp", 1))

    def over_x(value):
        return lane_x.send(value, MESH_AXES, route("dp", 1))

    def over_z(value):
        return lane_z.send(value, MESH_AXES, route("dp", stride))

    def near_pairs(*arrays):
        return [(a, lane_core.send(a, MESH_AXES, route("section", 1))) for a in arrays]

    def share(j, size):
        return block(pl.multiple_of(share_of(j, stride) * size, size), size)

    def eighth(j, size):
        return block(pl.multiple_of(eighth_of(j, 0, stride) * size, size), size)

    def columns(n, size):
        return block(n * size, size)

    qkv = jnp.transpose(self_qkv[0], (1, 0, 2))
    near_self = near_pairs(qkv, self_out[0])

    def self_piece(j):
        moves = [(0, lambda: (ALL, ALL, share(j, QUARTER)), at((block(0, 3),)))]
        moves += [
            (1, lambda n=n: (share(j, QUARTER), columns(n, QUARTER)), at((3, columns(n, QUARTER))))
            for n in range(width // QUARTER)
        ]
        return cut_piece([(qkv,), (self_out[0],)], None, (4, width, QUARTER), moves)

    piece = width // 8

    def ffn_piece(layer, j):
        moves = [(0, lambda: (ALL, eighth(j, WIDE)), at((block(0, width), ALL)))]
        moves += [
            (1, lambda n=n: (eighth(j, WIDE), columns(n, WIDE)), at((block(width + n * WIDE, WIDE), ALL)))
            for n in range(width // WIDE)
        ]
        moves += [(2, lambda: (eighth(j, piece), ALL), at((block(2 * width, piece), ALL)))]
        moves += [
            (
                3,
                lambda n=n: (columns(n, piece), eighth(j, piece)),
                at((block(2 * width + piece, piece), columns(n, piece))),
            )
            for n in range(units // piece)
        ]
        return cut_piece(near_ffn, layer, (2 * width + 2 * piece, WIDE), moves)

    def cross_piece(j):
        moves = [(n, lambda: (ALL, share(j, QUARTER)), at((n,))) for n in range(2)]
        return cut_piece([(cross_kv[0],), (cross_vo[0],)], None, (2, width, QUARTER), moves)

    def swapped(value):
        return swap(value, "section")

    def quarters(pieces, swaps, base):
        return [((p, q), (p, q), base) for p, q in zip(pieces, swaps)]

    def eighths(pieces, swaps, base):
        return [((p, p, base), (q, q, base)) for p, q in zip(pieces, swaps)]

    def swapped_after(pieces, token):
        return [swapped(after(p, token)) for p in pieces]

    bias_near = adapter_down_bias[0][None]
    bias_far = over_y(bias_near)
    small = jnp.concatenate(
        [
            norm_gains[0],
            adapter_up_bias,
            jnp.concatenate([bias_near, bias_far, jnp.zeros((1, width - 2 * units), F32)], 1),
        ],
        0,
    )
    small_other = swap(small, "section")
    enc_small = jnp.where(first_core, small, small_other)
    dec_small = jnp.where(first_core, small_other, small)

    def small_of(s):
        down_bias = jnp.stack([s[3:4, :units], s[3:4, units : 2 * units]], 0)
        return s[0:1], s[1:2], s[2:3], down_bias

    enc_gain1, enc_gain2, enc_upb, enc_downb = small_of(enc_small)
    dec_gain1, dec_gain2, dec_upb, dec_downb = small_of(dec_small)
    mid_gain = cross_gain[None]

    segs = lax.dynamic_index_in_dim(segment_ids, side, 1, keepdims=False)
    docs = jnp.arange(seq)
    counts = jnp.sum(segs[:, :, None] == docs[None, None, :8], 1)
    largest = jnp.argmax(counts, 1)
    starts = jnp.sum(segs < largest[:, None], 1).astype(jnp.int32)

    def halves_of_seg(seg, start):
        twice = jnp.concatenate([seg, seg], 0)
        mine = lax.dynamic_slice_in_dim(twice, start + half * core, half, 0)
        away = lax.dynamic_slice_in_dim(twice, start + half * (1 - core), half, 0)
        return mine, away

    enc_seg, enc_seg_away = halves_of_seg(segs[0], starts[0])
    dec_seg, _ = halves_of_seg(segs[1], starts[1])
    own_start = jnp.where(first_core, starts[0], starts[1])

    def rows_sent(value, token=None):
        keep = lax.dynamic_index_in_dim(value[0], side, 0, keepdims=False)
        give = lax.dynamic_index_in_dim(value[0], 1 - side, 0, keepdims=False)
        return keep, over_y(give if token is None else after(give, token))

    def rows_here(keep, got):
        start = lax.rem(own_start + seq - half * side, seq)
        ring = (keep, got, keep, got)
        mine = rotated(ring, start + half * core, half)
        away = rotated(ring, lax.rem(start + half * (1 - core), seq), half)
        other = swap(away, "section")
        return jnp.where(first_core, mine, other), jnp.where(first_core, other, mine)

    def slices_back(big, rest, start):
        ring = (big, rest, big, rest)
        keep = rotated(ring, lax.rem(half * side + seq - start, seq), half)
        give = rotated(ring, lax.rem(half * (1 - side) + seq - start, seq), half)
        return keep, give

    def by_row(keep, got):
        return jnp.where(side == 0, jnp.stack([keep, got]), jnp.stack([got, keep]))

    def rows_back(enc, dec):
        mine = jnp.where(first_core, enc, dec)
        away = jnp.where(first_core, dec, enc)
        other = swap(away, "section")
        big = jnp.where(first_core, mine, other)
        rest = jnp.where(first_core, other, mine)
        keep, give = slices_back(big, rest, own_start)
        return by_row(keep, swap(give, "mp"))

    def layer_back(layer, value):
        other = lax.ppermute(value, MESH_AXES, route("section", 1, 1 - layer))
        big, rest = (value, other) if layer == 0 else (other, value)
        keep, give = slices_back(big, rest, starts[layer])
        return by_row(keep, lax.ppermute(give, MESH_AXES, route("mp", 1, layer)))

    x_keep, x_got = rows_sent(inputs)
    near_ffn = near_pairs(ffn_in[0], ffn_out[0], adapter_down[0], adapter_up[0])
    near_cross = near_pairs(cross_kv[0], cross_vo[0])
    near_other = [pair[1] for pair in near_self + near_ffn + near_cross]
    self_0 = over_y(self_piece(0))
    self_3 = over_y(self_piece(3))
    self_1, self_2 = over_x(after(self_0, near_other)), over_z(after(self_0, near_other))
    self_swaps = [swapped(p) for p in (self_0, self_1, self_2)]
    self_swaps.append(swapped(after(self_3, (self_1, self_2))))
    cross_0 = over_y(after(cross_piece(0), (self_1, self_2)))
    enc_0 = over_y(ffn_piece(0, 0))
    lane_y.depth = 2
    x_enc, x_dec = rows_here(x_keep, x_got)
    w_self = self_plan(near_self, quarters((self_0, self_1, self_2, self_3), self_swaps, 2))

    enc_col, enc_row = enc_seg[:, None], enc_seg[None, :]
    dec_col, dec_row = dec_seg[:, None], dec_seg[None, :]
    all_keys = jnp.stack([enc_seg, enc_seg_away], 0)[:, :, None]

    e_qkv, e_lse, e_hat1, e_inv1 = self_forward(0, x_enc, enc_col, enc_row, enc_gain1, w_self)
    enc_1, enc_2 = over_x(after(enc_0, e_inv1)), over_z(after(enc_0, e_inv1))
    enc_3 = over_y(after(ffn_piece(0, 3), e_inv1))
    d_qkv, d_lse, d_hat1, d_inv1 = self_forward(
        1, after(x_dec, e_inv1), dec_col, dec_row, dec_gain1, w_self
    )
    enc = (enc_0, enc_1, enc_2, enc_3)
    w_enc = branch_plan(near_ffn, eighths(enc, swapped_after(enc, d_inv1), width), stride)
    cross_1, cross_2 = over_x(after(cross_0, d_inv1)), over_z(after(cross_0, d_inv1))
    cross_3 = over_y(after(cross_piece(3), d_inv1))
    dec_0 = over_y(after(ffn_piece(1, 0), d_inv1))
    e_slope, e_aslope, e_aact, e_hat2, e_inv2, y_enc = branch_forward(
        0, after(e_hat1, d_inv1), enc_gain1, enc_gain2, enc_downb, enc_upb, w_enc
    )
    crosses = (cross_0, cross_1, cross_2, cross_3)
    cross_swaps = swapped_after(crosses, e_inv2)
    w_cross = cross_plan(near_cross, quarters(crosses, cross_swaps, 1))
    dec_3 = over_y(after(ffn_piece(1, 3), e_inv2))
    kv = keys_forward(after(y_enc, dec_0), w_cross)
    kv_away = swap(kv, "section")
    dec_1, dec_2 = over_x(after(dec_0, kv)), over_z(after(dec_0, kv))
    d_q, c_lse, d_hat2, d_inv2 = cross_forward(
        d_hat1, dec_gain1, kv, kv_away, all_keys, dec_row, w_cross
    )
    dec = (dec_0, dec_1, dec_2, dec_3)
    w_dec = branch_plan(near_ffn, eighths(dec, swapped_after(dec, d_inv2), width), stride)
    g_keep, g_got = rows_sent(cotangent, kv)
    d_slope, d_aslope, d_aact, d_hat3, d_inv3, y_dec = branch_forward(
        1, d_hat2, mid_gain, dec_gain2, dec_downb, dec_upb, w_dec
    )
    g_enc, g_dec = rows_here(g_keep, g_got)

    def summed_here(grads):
        keep = lax.dynamic_index_in_dim(grads, core, 1, keepdims=False)
        give = lax.dynamic_index_in_dim(grads, 1 - core, 1, keepdims=False)
        return (keep.astype(F32) + swap(give, "section").astype(F32)).astype(BF16)

    def summed_side(both, token):
        got = after(swap(both[1], "mp"), token)
        return (both[0].astype(F32) + got.astype(F32)).astype(BF16)

    def summed_rows(value, over, token):
        for flip in over:
            got = after(lax.ppermute(value, MESH_AXES, route("dp", flip)), token)
            value = (value.astype(F32) + got.astype(F32)).astype(BF16)
        return value

    flips = [1 << i for i in range(lax.axis_size("dp").bit_length() - 1)]
    flips = flips[2:3] + flips[:2] + flips[3:]
    d_mid, d_grads = branch_backward(
        1, g_dec, d_hat3, d_inv3, dec_gain2, d_hat2, d_inv2, mid_gain,
        d_slope, d_aslope, d_aact, w_dec,
    )
    d_both = summed_here(d_grads)
    d_first, kv_grad, kv_grad_give = cross_backward(
        after(d_mid, d_both), d_hat1, d_inv1, dec_gain1, d_q, c_lse, kv, kv_away, all_keys, dec_row,
        w_cross,
    )
    kv_grad_away = swap(kv_grad_give, "section")
    e_out = keys_backward(g_enc, kv_grad, kv_grad_away, w_cross)
    e_first, e_grads = branch_backward(
        0, e_out, e_hat2, e_inv2, enc_gain2, e_hat1, e_inv1, enc_gain1,
        e_slope, e_aslope, e_aact, w_enc,
    )
    e_both = summed_here(e_grads)
    d_total = summed_side(d_both, e_first)
    d_first = after(d_first, e_both)
    bunches = len(w_self.steps)

    def self_part(layer, grad, base, saved, lse, col, row, first, count):
        return self_backward(layer, grad, base, saved, lse, col, row, w_self, first, count)

    outputs = rows_back(y_enc, y_dec)
    dx_dec = self_part(1, d_first, d_first, d_qkv, d_lse, dec_col, dec_row, 0, bunches)
    e_total = summed_side(e_both, dx_dec)
    d_total = summed_rows(d_total, flips[:1], dx_dec)
    e_first = after(e_first, (dx_dec, e_total, outputs))
    dx_enc = self_part(0, e_first, e_first, e_qkv, e_lse, enc_col, enc_row, 0, bunches // 2)
    e_total = summed_rows(e_total, flips[:1], dx_enc)
    d_total = summed_rows(d_total, flips[1:2], dx_enc)
    dx_dec_back = layer_back(1, dx_dec)
    dx_enc = self_part(
        0, e_first, after(dx_enc, (e_total, d_total, dx_dec_back)), e_qkv, e_lse, enc_col, enc_row,
        bunches // 2, bunches // 2,
    )
    e_total = summed_rows(e_total, flips[1:2], dx_enc)
    d_total = summed_rows(d_total, flips[2:], dx_enc)
    e_total = summed_rows(e_total, flips[2:], dx_enc)
    dx = jnp.where(first_core, layer_back(0, dx_enc), dx_dec_back)
    mine = jnp.where(first_core, e_total, d_total)
    other = swap(jnp.where(first_core, d_total, e_total), "section")
    down_total = jnp.where(first_core, mine, other)[:units].astype(F32)
    down_total = jnp.transpose(down_total.reshape(units, -1, units), (1, 0, 2)).reshape(width, units)
    up_total = jnp.where(first_core, other, mine).astype(F32)
    dx = jnp.where(first_core, layer_back(0, dx_enc), dx_dec_back)

    return (
        outputs[None],
        dx.astype(F32)[None],
        down_total[None],
        up_total[units : units + 1, :units],
        up_total[:units][None],
        up_total[units + 1 : units + 2],
    )


def solution(mesh):
    in_specs = (
        P("section", "dp", "mp", None),
        P(None, "dp", None),
        P("section", "dp", "mp", None),
        P("section", None, None),
        P(),
        P("section", None, None, "mp"),
        P("section", "mp", None),
        P("section", None, "mp"),
        P("section", None, "mp"),
        P("section", None, "mp"),
        P("section", "mp", None),
        P("section", None, "mp"),
        P("section", "mp"),
        P("section", "mp", None),
        P("section", None),
    )
    out_specs = (
        P("section", "dp", "mp", None),
        P("section", "dp", "mp", None),
        P("section", None, "mp"),
        P("section", "mp"),
        P("section", "mp", None),
        P("section", None),
    )
    return jax.shard_map(
        per_device, mesh=mesh, in_specs=in_specs, out_specs=out_specs, check_vma=False
    )
```

```python
import functools

import jax
import jax.numpy as jnp
from jax import lax
from jax.experimental import pallas as pl
from jax.experimental.pallas import tpu as pltpu
from jax.sharding import PartitionSpec as P

HEADDIM = 64
BUNCH = 4
WIDE = BUNCH * HEADDIM
CHUNK = 1024
SCALE = HEADDIM**-0.5
LANES = 128
PART = 256
EXTRA = 16
HIDDEN_MASK = -1e30
VMEM_LIMIT = 60 * 1024 * 1024
BF16 = jnp.bfloat16
F32 = jnp.float32


def dot_nn(left, right):
    return lax.dot_general(left, right, (((1,), (0,)), ((), ())), preferred_element_type=F32)


def dot_nt(left, right):
    return lax.dot_general(left, right, (((1,), (1,)), ((), ())), preferred_element_type=F32)


def dot_tn(left, right):
    return lax.dot_general(left, right, (((0,), (0,)), ((), ())), preferred_element_type=F32)


class Plan:
    def __init__(self, bufs):
        self.pairs = []
        self.steps = []
        self.bufs = bufs

    def part(self, first, count):
        some = Plan(self.bufs)
        for copies in self.steps[first : first + count]:
            some.steps.append([(some.add(*self.pairs[c[0]]),) + tuple(c[1:]) for c in copies])
        return some

    def add(self, *arrays):
        for i, pair in enumerate(self.pairs):
            if pair[0] is arrays[0]:
                return i
        self.pairs.append(arrays)
        return len(self.pairs) - 1


def at(index):
    return lambda: index


def block(start, size):
    return pl.ds(start, size)


def advance(plan, refs, bufs, sems, layer, step):
    count = len(plan.steps)
    mine = lax.axis_index("section") == layer
    slot = lax.rem(step, 2)

    firsts = [sum(len(p) for p in plan.pairs[:i]) for i in range(len(plan.pairs))]

    def start(copies, side, to):
        for pair, source, buf, place in copies:
            src = refs[firsts[pair] + side].at[source()]
            dst = bufs[buf].at[(to,) + tuple(place())]
            pltpu.make_async_copy(src, dst, sems[buf].at[to]).start()

    def issue(which, to):
        start([c for c in plan.steps[which] if len(plan.pairs[c[0]]) == 1], 0, to)
        layered = [c for c in plan.steps[which] if len(plan.pairs[c[0]]) == 2]
        if layered:

            @pl.when(mine)
            def _():
                start(layered, 0, to)

            @pl.when(jnp.logical_not(mine))
            def _():
                start(layered, 1, to)

    @pl.when(step == 0)
    def _():
        issue(0, 0)

    for which in range(1, count):

        @pl.when(step + 1 == which)
        def _():
            issue(which, which % 2)

    used = [sorted({c[2] for c in copies}) for copies in plan.steps]

    def settle(buf):
        pltpu.make_async_copy(bufs[buf].at[slot], bufs[buf].at[slot], sems[buf].at[slot]).wait()

    first = 0
    for which in range(1, count + 1):
        if which == count or used[which] != used[first]:
            if first == 0 and which == count:
                for buf in used[first]:
                    settle(buf)
            else:

                @pl.when((step >= first) & (step < which))
                def _():
                    for buf in used[first]:
                        settle(buf)

            first = which
    return slot


def call(body, operands, in_blocks, plan, out_shapes, out_blocks, scratch, cost):
    arrays = [a for pair in plan.pairs for a in pair]
    n_ops, n_out, n_buf = len(operands), len(out_shapes), len(plan.bufs)

    def kernel(*refs):
        ins, rest = refs[:n_ops], refs[n_ops:]
        wrefs, rest = rest[: len(arrays)], rest[len(arrays) :]
        outs, rest = rest[:n_out], rest[n_out:]
        bufs, rest = rest[:n_buf], rest[n_buf:]
        sems, extra = rest[:n_buf], rest[n_buf:]
        body(ins, wrefs, outs, bufs, sems, extra)

    return pl.pallas_call(
        kernel,
        grid=(len(plan.steps),),
        in_specs=list(in_blocks) + [pl.BlockSpec(memory_space=pltpu.HBM)] * len(arrays),
        out_specs=tuple(out_blocks),
        out_shape=tuple(out_shapes),
        scratch_shapes=[pltpu.VMEM((2,) + tuple(b), BF16) for b in plan.bufs]
        + [pltpu.SemaphoreType.DMA((2,)) for _ in plan.bufs]
        + list(scratch),
        compiler_params=pltpu.CompilerParams(
            dimension_semantics=("arbitrary",), vmem_limit_bytes=VMEM_LIMIT
        ),
        cost_estimate=pl.CostEstimate(
            flops=int(3 * cost), bytes_accessed=int(cost // 200), transcendentals=0
        ),
    )(*operands, *arrays)


ALL = slice(None)
QUARTER = 128


def self_plan(near, far):
    width = near[0][0].shape[1]
    plan = Plan([(3, width, WIDE), (WIDE, width)])
    qkv, out = plan.add(*near[0]), plan.add(*near[1])
    for g in range(near[0][0].shape[2] // WIDE):
        cols = block(g * WIDE, WIDE)
        plan.steps.append(
            [(qkv, at((ALL, ALL, cols)), 0, at(())), (out, at((cols, ALL)), 1, at(()))]
        )
    for g in range(len(far) // 2):
        copies = []
        for j in range(2):
            first, second, base = far[2 * g + j]
            a, b = plan.add(*first), plan.add(*second)
            lanes = block(j * QUARTER, QUARTER)
            copies.append((a, at((block(0, 2),)), 0, at((block(0, 2), ALL, lanes))))
            copies.append((b, at((base,)), 0, at((2, ALL, lanes))))
            for k in range(width // QUARTER):
                here = block(k * QUARTER, QUARTER)
                copies.append((b, at((base + 1, here, ALL)), 1, at((lanes, here))))
        plan.steps.append(copies)
    return plan


def cross_plan(near, far):
    width = near[0][0].shape[0]
    plan = Plan([(width, WIDE), (width, WIDE)])
    ckv, cvo = plan.add(*near[0]), plan.add(*near[1])
    for g in range(near[0][0].shape[1] // WIDE):
        cols = block(g * WIDE, WIDE)
        plan.steps.append([(ckv, at((ALL, cols)), 0, at(())), (cvo, at((ALL, cols)), 1, at(()))])
    for g in range(len(far) // 2):
        copies = []
        for j in range(2):
            first, second, base = far[2 * g + j]
            a, b = plan.add(*first), plan.add(*second)
            lanes = block(j * QUARTER, QUARTER)
            copies.append((a, at((0,)), 0, at((ALL, lanes))))
            copies.append((b, at((base,)), 1, at((ALL, lanes))))
        plan.steps.append(copies)
    return plan


def branch_plan(near, far, stride):
    width, hidden = near[0][0].shape
    units = near[2][0].shape[1]
    piece = width // 8
    plan = Plan([(width, CHUNK), (CHUNK, width), (width, units), (units, width)])
    up, down, adown, aup = [plan.add(*pair) for pair in near]
    for g in range(hidden // CHUNK):
        cols = block(g * CHUNK, CHUNK)
        plan.steps.append([(up, at((ALL, cols)), 0, at(())), (down, at((cols, ALL)), 1, at(()))])
    adapter = []
    each = CHUNK // (2 * WIDE)
    for j, both in enumerate(far):
        copies = [] if j % each == 0 else copies
        for k, (first, second, base) in enumerate(both):
            a, b = plan.add(first), plan.add(second)
            cols = block((j % each * 2 + k) * WIDE, WIDE)
            copies.append((a, at((block(0, width), ALL)), 0, at((ALL, cols))))
            for n in range(width // WIDE):
                rows = block(base + n * WIDE, WIDE)
                copies.append((b, at((rows, ALL)), 1, at((cols, block(n * WIDE, WIDE)))))

            def spot(j=j, k=k):
                return block(pl.multiple_of(eighth_of(j, k, stride) * piece, piece), piece)

            rows = block(base + width, piece)
            adapter.append((b, at((rows, ALL)), 2, lambda spot=spot: (spot(), ALL)))
            for n in range(units // piece):
                rows = block(base + width + piece, piece)
                here = block(n * piece, piece)
                adapter.append(
                    (b, at((rows, here)), 3, lambda spot=spot, here=here: (here, spot()))
                )
        if j % each == each - 1:
            plan.steps.append(copies)
    plan.steps.append([(adown, at(()), 2, at(())), (aup, at(()), 3, at(()))])
    plan.steps.append(adapter)
    return plan


def share_of(j, stride):
    place = lax.axis_index("dp")
    x = lax.rem(place, 2)
    z = lax.rem(lax.div(place, stride), 2)
    x = 1 - x if j in (1, 3) else x
    z = 1 - z if j in (2, 3) else z
    return 2 * x + z


def eighth_of(j, k, stride):
    core = lax.axis_index("section")
    return 4 * (1 - core if k else core) + share_of(j, stride)


def cut_piece(pairs, layer, shape, moves):
    plan = Plan([])
    plan.pairs = pairs
    firsts = [sum(len(p) for p in pairs[:i]) for i in range(len(pairs))]
    arrays = [a for pair in pairs for a in pair]

    def kernel(*refs):
        ins, out, sem = refs[: len(arrays)], refs[-2], refs[-1]

        def start(side):
            for pair, index, place in moves:
                src = ins[firsts[pair] + side].at[index()]
                pltpu.make_async_copy(src, out.at[place()], sem).start()

        if layer is None:
            start(0)
        else:
            mine = lax.axis_index("section") == layer

            @pl.when(mine)
            def _():
                start(0)

            @pl.when(jnp.logical_not(mine))
            def _():
                start(1)

        pltpu.make_async_copy(out, out, sem).wait()

    return pl.pallas_call(
        kernel,
        in_specs=[pl.BlockSpec(memory_space=pltpu.HBM)] * len(arrays),
        out_specs=pl.BlockSpec(memory_space=pltpu.VMEM),
        out_shape=shaped(shape, BF16),
        scratch_shapes=[pltpu.SemaphoreType.DMA],
        compiler_params=pltpu.CompilerParams(vmem_limit_bytes=8 * 1024 * 1024),
    )(*arrays)


def whole(shape):
    zeros = (0,) * len(shape)
    return pl.BlockSpec(tuple(shape), lambda i: zeros)


def per_step(shape, first=0, last=None):
    def index(i):
        k = jnp.maximum(i - first, 0)
        if last is not None:
            k = jnp.minimum(k, last)
        return (k,) + (0,) * len(shape)

    return pl.BlockSpec((1,) + tuple(shape), index)


def shaped(shape, dtype):
    return jax.ShapeDtypeStruct(tuple(shape), dtype)


def normalized(value):
    center = value - jnp.mean(value, -1, keepdims=True)
    spread = jnp.mean(center * center, -1, keepdims=True)
    inverse = lax.rsqrt(spread + 1e-05)
    return center * inverse, inverse


def norm_slope(grad, hat, inverse, gain):
    scaled = grad * gain
    along = jnp.mean(scaled * hat, -1, keepdims=True)
    return inverse * (scaled - jnp.mean(scaled, -1, keepdims=True) - hat * along)


def gelu_pair(value):
    below = 0.5 + 0.5 * lax.erf(value * (0.5**0.5))
    density = jnp.exp(value * value * -0.5) * 0.3989422804014327
    return value * below, below + value * density


def lanes_of(head):
    first = head * HEADDIM // LANES * LANES
    return slice(first, first + LANES)


def only_head(value, head):
    lane = lax.broadcasted_iota(jnp.int32, (1, LANES), 1)
    inside = head * HEADDIM % LANES
    keep = (lane >= inside) & (lane < inside + HEADDIM)
    part = value[:, lanes_of(head)]
    return jnp.where(keep, part, jnp.zeros_like(part))


def attend(blocks, q_ref, k_ref, v_ref, bias_ref, valid_ref, lse_ref, out_ref):
    units = [(rows, keys, head) for rows, keys in blocks for head in range(BUNCH)]

    def scores_of(unit):
        rows, keys, head = unit
        q_head = only_head(q_ref[rows, :] * jnp.asarray(SCALE, BF16), head)
        return dot_nt(k_ref[keys, lanes_of(head)], q_head)

    ahead = scores_of(units[0])
    for i, (rows, keys, head) in enumerate(units):
        scores = ahead + bias_ref[keys, rows]
        if i + 1 < len(units):
            ahead = scores_of(units[i + 1])
        peak = jnp.max(scores, 0, keepdims=True)
        powers = jnp.exp(scores - peak)
        total = jnp.sum(powers, 0, keepdims=True)
        share = 1.0 / total
        lse = peak + jnp.log(total)
        if valid_ref is not None:
            valid = valid_ref[:, rows] > 0.0
            share = jnp.where(valid, share, 0.0)
            lse = jnp.where(valid, lse, -HIDDEN_MASK)
        lse_ref[head : head + 1, rows] = lse
        mixed = dot_tn((powers * share).astype(BF16), only_head(v_ref[keys, :], head))
        out_ref[rows, lanes_of(head)] += mixed


def attend_slope(blocks, q_ref, k_ref, v_ref, g_ref, bias_ref, lse_ref, dq_ref, dk_ref, dv_ref):
    units = [(rows, keys, head) for rows, keys in blocks for head in range(BUNCH)]

    def products_of(unit):
        rows, keys, head = unit
        q_head = only_head(q_ref[rows, :] * jnp.asarray(SCALE, BF16), head)
        g_head = only_head(g_ref[rows, :], head)
        lanes = lanes_of(head)
        return q_head, g_head, dot_nt(k_ref[keys, lanes], q_head), dot_nt(v_ref[keys, lanes], g_head)

    ahead = products_of(units[0])
    for i, (rows, keys, head) in enumerate(units):
        q_head, g_head, scores, prob_grad = ahead
        if i + 1 < len(units):
            ahead = products_of(units[i + 1])
        lanes = lanes_of(head)
        probs = jnp.exp(scores + bias_ref[keys, rows] - lse_ref[head : head + 1, rows])
        inner = jnp.sum(probs * prob_grad, 0, keepdims=True)
        score_grad = (probs * (prob_grad - inner)).astype(BF16)
        dv_ref[keys, lanes] += dot_nn(probs.astype(BF16), g_head)
        dk_ref[keys, lanes] += dot_nn(score_grad, q_head)
        dq_ref[rows, lanes] += dot_tn(score_grad, only_head(k_ref[keys, :], head))


def fill_bias(bias_ref, key_seg, row_seg, causal):
    seen = key_seg == row_seg
    if causal:
        key = lax.broadcasted_iota(jnp.int32, bias_ref.shape, 0)
        row = lax.broadcasted_iota(jnp.int32, bias_ref.shape, 1)
        seen = seen & (key <= row)
    bias_ref[...] = jnp.where(seen, 0.0, HIDDEN_MASK)


def self_blocks(rows, causal):
    if not causal:
        return [(slice(0, rows), slice(0, rows))]
    count = rows // PART
    parts = [slice(i * PART, (i + 1) * PART) for i in range(count)]
    return [(part, slice(0, part.stop)) for part in parts]


def cross_blocks(rows):
    return [(slice(i, i + PART), slice(0, rows)) for i in range(0, rows, PART)]


def note_active(bias, valid, active, rows):
    for h in range(2):
        best = jnp.max(bias[h], 0, keepdims=True)
        valid[h] = jnp.where(best > 0.5 * HIDDEN_MASK, 1.0, 0.0)
        for i in range(rows // PART):
            some = jnp.max(valid[h, :, i * PART : (i + 1) * PART])
            active[h, i] = (some > 0.0).astype(jnp.int32)


def self_forward(layer, x, seg_col, seg_row, gain, plan):
    rows, width = x.shape
    steps = len(plan.steps)

    def body(ins, wrefs, outs, bufs, sems, extra):
        x_ref, segc_ref, segr_ref, gain_ref = ins
        qkv_ref, lse_ref, hat_ref, inv_ref = outs
        acc, bias, mixed = extra
        step = pl.program_id(0)
        slot = advance(plan, wrefs, bufs, sems, layer, step)

        @pl.when(step == 0)
        def _():
            fill_bias(bias, segc_ref[...], segr_ref[...], layer == 1)
            acc[...] = x_ref[...].astype(F32)

        x_rows = x_ref[...]
        w = bufs[0].at[slot]
        q = dot_nn(x_rows, w[0]).astype(BF16)
        k = dot_nn(x_rows, w[1]).astype(BF16)
        v = dot_nn(x_rows, w[2]).astype(BF16)
        qkv_ref[0, 0] = q
        qkv_ref[0, 1] = k
        qkv_ref[0, 2] = v
        mixed[...] = jnp.zeros_like(mixed)
        attend(
            self_blocks(rows, layer == 1), qkv_ref.at[0, 0], qkv_ref.at[0, 1], qkv_ref.at[0, 2],
            bias, None, lse_ref.at[0], mixed,
        )
        acc[...] += dot_nn(mixed[...].astype(BF16), bufs[1][slot])

        @pl.when(step == steps - 1)
        def _():
            hat, inverse = normalized(acc[...])
            hat_ref[...] = hat.astype(BF16)
            inv_ref[...] = inverse

    return call(
        body,
        [x, seg_col, seg_row, gain],
        [whole(x.shape), whole(seg_col.shape), whole(seg_row.shape), whole(gain.shape)],
        plan,
        [
            shaped((steps, 3, rows, WIDE), BF16),
            shaped((steps, BUNCH, rows), F32),
            shaped((rows, width), BF16),
            shaped((rows, 1), F32),
        ],
        [
            per_step((3, rows, WIDE)),
            per_step((BUNCH, rows)),
            whole((rows, width)),
            whole((rows, 1)),
        ],
        [
            pltpu.VMEM((rows, width), F32),
            pltpu.VMEM((rows, rows), F32),
            pltpu.VMEM((rows, WIDE), F32),
        ],
        steps * (2 * rows * width * WIDE * 4 + 16 * rows * rows * WIDE),
    )


def self_backward(layer, grad, base, saved, lse, seg_col, seg_row, plan, first, count):
    rows, width = grad.shape
    steps = count
    plan = plan.part(first, count)

    def body(ins, wrefs, outs, bufs, sems, extra):
        g_ref, base_ref, saved_ref, lse_ref, segc_ref, segr_ref = ins
        (dx_ref,) = outs
        acc, bias, mixed_grad, dq, dk, dv = extra
        step = pl.program_id(0)
        slot = advance(plan, wrefs, bufs, sems, layer, step)

        @pl.when(step == 0)
        def _():
            fill_bias(bias, segc_ref[...], segr_ref[...], layer == 1)
            acc[...] = base_ref[...].astype(F32)

        mixed_grad[...] = dot_nt(g_ref[...], bufs[1][slot]).astype(BF16)
        for ref in (dq, dk, dv):
            ref[...] = jnp.zeros_like(ref)
        attend_slope(
            self_blocks(rows, layer == 1), saved_ref.at[0, 0], saved_ref.at[0, 1],
            saved_ref.at[0, 2], mixed_grad, bias, lse_ref.at[0], dq, dk, dv,
        )
        w = bufs[0].at[slot]
        acc[...] += (
            dot_nt((dq[...] * SCALE).astype(BF16), w[0])
            + dot_nt(dk[...].astype(BF16), w[1])
            + dot_nt(dv[...].astype(BF16), w[2])
        )

        @pl.when(step == steps - 1)
        def _():
            dx_ref[...] = acc[...].astype(BF16)

    return call(
        body,
        [grad, base, saved, lse, seg_col, seg_row],
        [
            whole(grad.shape),
            whole(grad.shape),
            per_step((3, rows, WIDE), -first),
            per_step((BUNCH, rows), -first),
            whole(seg_col.shape),
            whole(seg_row.shape),
        ],
        plan,
        [shaped((rows, width), BF16)],
        [whole((rows, width))],
        [
            pltpu.VMEM((rows, width), F32),
            pltpu.VMEM((rows, rows), F32),
            pltpu.VMEM((rows, WIDE), BF16),
            pltpu.VMEM((rows, WIDE), F32),
            pltpu.VMEM((rows, WIDE), F32),
            pltpu.VMEM((rows, WIDE), F32),
        ],
        steps * (2 * rows * width * WIDE * 4 + 40 * rows * rows * WIDE),
    )[0]


def cross_forward(hat, gain, kv_own, kv_away, keys_col, seg_row, plan):
    rows, width = hat.shape
    steps = len(plan.steps)

    def body(ins, wrefs, outs, bufs, sems, extra):
        hat_ref, gain_ref, own_ref, away_ref, keysc_ref, segr_ref = ins
        q_ref, lse_ref, nhat_ref, inv_ref = outs
        acc, low, bias, mixed, valid, active = extra
        step = pl.program_id(0)
        slot = advance(plan, wrefs, bufs, sems, 1, step)

        @pl.when(step == 0)
        def _():
            for h in range(2):
                fill_bias(bias.at[h], keysc_ref[h], segr_ref[...], False)
            note_active(bias, valid, active, rows)
            first = hat_ref[...].astype(F32) * gain_ref[...]
            acc[...] = first
            low[...] = first.astype(BF16)

        q = dot_nn(low[...], bufs[0][slot]).astype(BF16)
        q_ref[0] = q
        mixed[...] = jnp.zeros_like(mixed)
        for h, kv_ref in enumerate((own_ref, away_ref)):
            for i, pair in enumerate(cross_blocks(rows)):

                @pl.when(active[h, i] > 0)
                def _():
                    attend(
                        [pair], q_ref.at[0], kv_ref.at[0, 0], kv_ref.at[0, 1],
                        bias.at[h], valid.at[h], lse_ref.at[0, h], mixed,
                    )

        acc[...] += dot_nt(mixed[...].astype(BF16), bufs[1][slot])

        @pl.when(step == steps - 1)
        def _():
            nhat, inverse = normalized(acc[...])
            nhat_ref[...] = nhat.astype(BF16)
            inv_ref[...] = inverse

    return call(
        body,
        [hat, gain, kv_own, kv_away, keys_col, seg_row],
        [
            whole(hat.shape),
            whole(gain.shape),
            per_step((2, rows, WIDE)),
            per_step((2, rows, WIDE)),
            whole(keys_col.shape),
            whole(seg_row.shape),
        ],
        plan,
        [
            shaped((steps, rows, WIDE), BF16),
            shaped((steps, 2, BUNCH, rows), F32),
            shaped((rows, width), BF16),
            shaped((rows, 1), F32),
        ],
        [
            per_step((rows, WIDE)),
            per_step((2, BUNCH, rows)),
            whole((rows, width)),
            whole((rows, 1)),
        ],
        [
            pltpu.VMEM((rows, width), F32),
            pltpu.VMEM((rows, width), BF16),
            pltpu.VMEM((2, rows, rows), F32),
            pltpu.VMEM((rows, WIDE), F32),
            pltpu.VMEM((2, 1, rows), F32),
            pltpu.SMEM((2, rows // PART), jnp.int32),
        ],
        steps * (2 * rows * width * WIDE * 2 + 32 * rows * rows * WIDE),
    )


def cross_backward(grad, hat, inv, gain, saved_q, lse, kv_own, kv_away, keys_col, seg_row, plan):
    rows, width = grad.shape
    steps = len(plan.steps)

    def body(ins, wrefs, outs, bufs, sems, extra):
        g_ref, hat_ref, inv_ref, gain_ref, q_ref, lse_ref, own_ref, away_ref, keysc_ref, segr_ref = ins
        dx_ref, own_grad_ref, away_grad_ref = outs
        acc, bias, mixed_grad, dq, dk, dv, valid, active = extra
        step = pl.program_id(0)
        slot = advance(plan, wrefs, bufs, sems, 1, step)

        @pl.when(step == 0)
        def _():
            for h in range(2):
                fill_bias(bias.at[h], keysc_ref[h], segr_ref[...], False)
            note_active(bias, valid, active, rows)
            acc[...] = g_ref[...].astype(F32)

        mixed_grad[...] = dot_nn(g_ref[...], bufs[1][slot]).astype(BF16)
        for ref in (dq, dk, dv):
            ref[...] = jnp.zeros_like(ref)
        for h, kv_ref in enumerate((own_ref, away_ref)):
            for i, pair in enumerate(cross_blocks(rows)):

                @pl.when(active[h, i] > 0)
                def _():
                    attend_slope(
                        [pair], q_ref.at[0], kv_ref.at[0, 0], kv_ref.at[0, 1], mixed_grad,
                        bias.at[h], lse_ref.at[0, h], dq, dk.at[h], dv.at[h],
                    )

        for h, out_ref in enumerate((own_grad_ref, away_grad_ref)):
            out_ref[0, 0] = dk[h].astype(BF16)
            out_ref[0, 1] = dv[h].astype(BF16)
        acc[...] += dot_nt((dq[...] * SCALE).astype(BF16), bufs[0][slot])

        @pl.when(step == steps - 1)
        def _():
            dx_ref[...] = norm_slope(
                acc[...], hat_ref[...].astype(F32), inv_ref[...], gain_ref[...]
            ).astype(BF16)

    return call(
        body,
        [grad, hat, inv, gain, saved_q, lse, kv_own, kv_away, keys_col, seg_row],
        [
            whole(grad.shape),
            whole(hat.shape),
            whole(inv.shape),
            whole(gain.shape),
            per_step((rows, WIDE)),
            per_step((2, BUNCH, rows)),
            per_step((2, rows, WIDE)),
            per_step((2, rows, WIDE)),
            whole(keys_col.shape),
            whole(seg_row.shape),
        ],
        plan,
        [
            shaped((rows, width), BF16),
            shaped((steps, 2, rows, WIDE), BF16),
            shaped((steps, 2, rows, WIDE), BF16),
        ],
        [whole((rows, width)), per_step((2, rows, WIDE)), per_step((2, rows, WIDE))],
        [
            pltpu.VMEM((rows, width), F32),
            pltpu.VMEM((2, rows, rows), F32),
            pltpu.VMEM((rows, WIDE), BF16),
            pltpu.VMEM((rows, WIDE), F32),
            pltpu.VMEM((2, rows, WIDE), F32),
            pltpu.VMEM((2, rows, WIDE), F32),
            pltpu.VMEM((2, 1, rows), F32),
            pltpu.SMEM((2, rows // PART), jnp.int32),
        ],
        steps * (2 * rows * width * WIDE * 2 + 80 * rows * rows * WIDE),
    )


def keys_forward(y, plan):
    rows, width = y.shape
    steps = len(plan.steps)

    def body(ins, wrefs, outs, bufs, sems, extra):
        (kv_ref,) = outs
        slot = advance(plan, wrefs, bufs, sems, 0, pl.program_id(0))
        kv_ref[0, 0] = dot_nn(ins[0][...], bufs[0][slot]).astype(BF16)
        kv_ref[0, 1] = dot_nn(ins[0][...], bufs[1][slot]).astype(BF16)

    return call(
        body,
        [y],
        [whole(y.shape)],
        plan,
        [shaped((steps, 2, rows, WIDE), BF16)],
        [per_step((2, rows, WIDE))],
        [],
        steps * 4 * rows * width * WIDE,
    )[0]


def keys_backward(out_grad, kv_grad, kv_grad_away, plan):
    rows, width = out_grad.shape
    steps = len(plan.steps)

    def body(ins, wrefs, outs, bufs, sems, extra):
        g_ref, own_ref, away_ref = ins
        (sum_ref,) = outs
        (acc,) = extra
        step = pl.program_id(0)
        slot = advance(plan, wrefs, bufs, sems, 0, step)

        @pl.when(step == 0)
        def _():
            acc[...] = g_ref[...].astype(F32)

        both = (own_ref[0].astype(F32) + away_ref[0].astype(F32)).astype(BF16)
        acc[...] += dot_nt(both[0], bufs[0][slot]) + dot_nt(both[1], bufs[1][slot])

        @pl.when(step == steps - 1)
        def _():
            sum_ref[...] = acc[...].astype(BF16)

    return call(
        body,
        [out_grad, kv_grad, kv_grad_away],
        [whole(out_grad.shape), per_step((2, rows, WIDE)), per_step((2, rows, WIDE))],
        plan,
        [shaped((rows, width), BF16)],
        [whole((rows, width))],
        [pltpu.VMEM((rows, width), F32)],
        steps * 4 * rows * width * WIDE,
    )[0]


def branch_forward(layer, hat, gain, out_gain, down_bias, up_bias, plan):
    rows, width = hat.shape
    nb = 2
    na = len(plan.steps) - nb
    units = down_bias.shape[-1]
    steps = na + nb

    def body(ins, wrefs, outs, bufs, sems, extra):
        hat_ref, gain_ref, ogain_ref, dbias_ref, ubias_ref = ins
        slope_ref, aslope_ref, aact_ref, nhat_ref, inv_ref, y_ref = outs
        acc, low = extra
        step = pl.program_id(0)
        slot = advance(plan, wrefs, bufs, sems, layer, step)

        @pl.when(step == 0)
        def _():
            first = hat_ref[...].astype(F32) * gain_ref[...]
            low[...] = first.astype(BF16)
            acc[...] = first + 4.0 * ubias_ref[...]

        @pl.when(step < na)
        def _():
            for at in range(0, rows, 512):
                part = slice(at, at + 512)
                act, slope = gelu_pair(dot_nn(low[part, :], bufs[0][slot]))
                slope_ref[0, part, :] = slope.astype(BF16)
                acc[part, :] += dot_nn(act.astype(BF16), bufs[1][slot])

        @pl.when(step >= na)
        def _():
            act, slope = gelu_pair(dot_nn(low[...], bufs[2][slot]) + dbias_ref[0])
            low_act = act.astype(BF16)
            aslope_ref[0] = slope.astype(BF16)
            aact_ref[0] = low_act
            acc[...] += dot_nn(low_act * jnp.asarray(4.0, BF16), bufs[3][slot])

        @pl.when(step == steps - 1)
        def _():
            nhat, inverse = normalized(acc[...])
            nhat_ref[...] = nhat.astype(BF16)
            inv_ref[...] = inverse
            y_ref[...] = (nhat * ogain_ref[...]).astype(BF16)

    return call(
        body,
        [hat, gain, out_gain, down_bias, up_bias],
        [
            whole(hat.shape),
            whole(gain.shape),
            whole(out_gain.shape),
            per_step((1, units), na),
            whole(up_bias.shape),
        ],
        plan,
        [
            shaped((na, rows, CHUNK), BF16),
            shaped((nb, rows, units), BF16),
            shaped((nb, rows, units), BF16),
            shaped((rows, width), BF16),
            shaped((rows, 1), F32),
            shaped((rows, width), BF16),
        ],
        [
            per_step((rows, CHUNK), 0, na - 1),
            per_step((rows, units), na),
            per_step((rows, units), na),
            whole((rows, width)),
            whole((rows, 1)),
            whole((rows, width)),
        ],
        [pltpu.VMEM((rows, width), F32), pltpu.VMEM((rows, width), BF16)],
        4 * rows * width * (na * CHUNK + nb * units),
    )


def branch_backward(layer, out_grad, nhat, ninv, out_gain, hat, inv, gain, slope, aslope, aact, plan):
    rows, width = hat.shape
    nb = 2
    na = len(plan.steps) - nb
    units = aact.shape[-1]
    steps = na + nb

    def body(ins, wrefs, outs, bufs, sems, extra):
        g_ref, nhat_ref, ninv_ref, ogain_ref, hat_ref, inv_ref, gain_ref, slope_ref, aslope_ref, aact_ref = ins
        dx_ref, packed_ref = outs
        acc, low, rows_low, up_bias = extra
        step = pl.program_id(0)
        slot = advance(plan, wrefs, bufs, sems, layer, step)

        @pl.when(step == 0)
        def _():
            grad = norm_slope(
                g_ref[...].astype(F32), nhat_ref[...].astype(F32), ninv_ref[...], ogain_ref[...]
            )
            acc[...] = grad
            small = grad.astype(BF16)
            low[...] = small
            up_bias[...] = 4.0 * jnp.sum(small.astype(F32), 0, keepdims=True)
            rows_low[...] = (hat_ref[...].astype(F32) * gain_ref[...]).astype(BF16)

        @pl.when(step < na)
        def _():
            for at in range(0, rows, 512):
                part = slice(at, at + 512)
                hidden = dot_nt(low[part, :], bufs[1][slot]) * slope_ref[0, part, :].astype(F32)
                acc[part, :] += dot_nt(hidden.astype(BF16), bufs[0][slot])

        @pl.when(step >= na)
        def _():
            hidden = 4.0 * dot_nt(low[...], bufs[3][slot]) * aslope_ref[0].astype(F32)
            small = hidden.astype(BF16)
            acc[...] += dot_nt(small, bufs[2][slot])
            down = dot_tn(rows_low[...], small).astype(BF16)
            for n in range(width // units):
                cols = slice(n * units, (n + 1) * units)
                packed_ref[0, 0, :units, cols] = down[cols]
            packed_ref[0, 1, :units] = (4.0 * dot_tn(aact_ref[0], low[...])).astype(BF16)
            bias = jnp.sum(small.astype(F32), 0, keepdims=True)
            bias = jnp.concatenate([bias] + [jnp.zeros_like(bias)] * (width // units - 1), 1)
            row = lax.broadcasted_iota(jnp.int32, (EXTRA, width), 0)
            last = jnp.where(row == 0, bias, jnp.where(row == 1, up_bias[...], 0.0))
            packed_ref[0, 0, units:] = jnp.zeros((EXTRA, width), BF16)
            packed_ref[0, 1, units:] = last.astype(BF16)

        @pl.when(step == steps - 1)
        def _():
            dx_ref[...] = norm_slope(
                acc[...], hat_ref[...].astype(F32), inv_ref[...], gain_ref[...]
            ).astype(BF16)

    return call(
        body,
        [out_grad, nhat, ninv, out_gain, hat, inv, gain, slope, aslope, aact],
        [
            whole(out_grad.shape),
            whole(nhat.shape),
            whole(ninv.shape),
            whole(out_gain.shape),
            whole(hat.shape),
            whole(inv.shape),
            whole(gain.shape),
            per_step((rows, CHUNK), 0, na - 1),
            per_step((rows, units), na),
            per_step((rows, units), na),
        ],
        plan,
        [
            shaped((rows, width), BF16),
            shaped((nb, 2, units + EXTRA, width), BF16),
        ],
        [
            whole((rows, width)),
            per_step((2, units + EXTRA, width), na),
        ],
        [
            pltpu.VMEM((rows, width), F32),
            pltpu.VMEM((rows, width), BF16),
            pltpu.VMEM((rows, width), BF16),
            pltpu.VMEM((1, width), F32),
        ],
        4 * rows * width * (na * CHUNK + nb * units),
    )


class Lane:
    def __init__(self, depth):
        self.depth = depth
        self.sent = []

    def send(self, value, axes, route):
        if len(self.sent) >= self.depth:
            value, _ = lax.optimization_barrier((value, self.sent[-self.depth]))
        got = lax.ppermute(value, axes, route)
        self.sent.append(got)
        return got


MESH_AXES = ("section", "mp", "dp")


def route(axis, flip, core=None):
    sizes = [lax.axis_size(a) for a in MESH_AXES]
    pairs = []
    for s in range(sizes[0]):
        for m in range(sizes[1]):
            for d in range(sizes[2]):
                if core is not None and s != core:
                    continue
                to = [s, m, d]
                to[MESH_AXES.index(axis)] ^= flip
                number = lambda p: (p[0] * sizes[1] + p[1]) * sizes[2] + p[2]
                pairs.append((number((s, m, d)), number(to)))
    return pairs


def after(value, token):
    return lax.optimization_barrier((value, token))[0]


def swap(value, axis):
    return jax.tree.map(lambda a: lax.ppermute(a, axis, [(0, 1), (1, 0)]), value)


def rotated(pieces, start, count):
    return lax.dynamic_slice_in_dim(jnp.concatenate(pieces, 0), start, count, 0)


def per_device(
    inputs,
    segment_ids,
    cotangent,
    norm_gains,
    cross_gain,
    self_qkv,
    self_out,
    cross_kv,
    cross_vo,
    ffn_in,
    ffn_out,
    adapter_down,
    adapter_down_bias,
    adapter_up,
    adapter_up_bias,
):
    core = lax.axis_index("section")
    side = lax.axis_index("mp")
    first_core = core == 0
    seq = segment_ids.shape[2]
    half = seq // 2
    width = inputs.shape[3]
    units = adapter_down.shape[2]

    stride = max(lax.axis_size("dp") // 4, 1)
    lane_y, lane_x, lane_z, lane_core = Lane(1), Lane(2), Lane(2), Lane(3)

    def over_y(value):
        return lane_y.send(value, MESH_AXES, route("mp", 1))

    def over_x(value):
        return lane_x.send(value, MESH_AXES, route("dp", 1))

    def over_z(value):
        return lane_z.send(value, MESH_AXES, route("dp", stride))

    def near_pairs(*arrays):
        return [(a, lane_core.send(a, MESH_AXES, route("section", 1))) for a in arrays]

    def share(j, size):
        return block(pl.multiple_of(share_of(j, stride) * size, size), size)

    def eighth(j, size):
        return block(pl.multiple_of(eighth_of(j, 0, stride) * size, size), size)

    def columns(n, size):
        return block(n * size, size)

    qkv = jnp.transpose(self_qkv[0], (1, 0, 2))
    near_self = near_pairs(qkv, self_out[0])

    def self_piece(j):
        moves = [(0, lambda: (ALL, ALL, share(j, QUARTER)), at((block(0, 3),)))]
        moves += [
            (1, lambda n=n: (share(j, QUARTER), columns(n, QUARTER)), at((3, columns(n, QUARTER))))
            for n in range(width // QUARTER)
        ]
        return cut_piece([(qkv,), (self_out[0],)], None, (4, width, QUARTER), moves)

    piece = width // 8

    def ffn_piece(layer, j):
        moves = [(0, lambda: (ALL, eighth(j, WIDE)), at((block(0, width), ALL)))]
        moves += [
            (1, lambda n=n: (eighth(j, WIDE), columns(n, WIDE)), at((block(width + n * WIDE, WIDE), ALL)))
            for n in range(width // WIDE)
        ]
        moves += [(2, lambda: (eighth(j, piece), ALL), at((block(2 * width, piece), ALL)))]
        moves += [
            (
                3,
                lambda n=n: (columns(n, piece), eighth(j, piece)),
                at((block(2 * width + piece, piece), columns(n, piece))),
            )
            for n in range(units // piece)
        ]
        return cut_piece(near_ffn, layer, (2 * width + 2 * piece, WIDE), moves)

    def cross_piece(j):
        moves = [(n, lambda: (ALL, share(j, QUARTER)), at((n,))) for n in range(2)]
        return cut_piece([(cross_kv[0],), (cross_vo[0],)], None, (2, width, QUARTER), moves)

    def swapped(value):
        return swap(value, "section")

    def quarters(pieces, swaps, base):
        return [((p, q), (p, q), base) for p, q in zip(pieces, swaps)]

    def eighths(pieces, swaps, base):
        return [((p, p, base), (q, q, base)) for p, q in zip(pieces, swaps)]

    def swapped_after(pieces, token):
        return [swapped(after(p, token)) for p in pieces]

    bias_near = adapter_down_bias[0][None]
    bias_far = over_y(bias_near)
    small = jnp.concatenate(
        [
            norm_gains[0],
            adapter_up_bias,
            jnp.concatenate([bias_near, bias_far, jnp.zeros((1, width - 2 * units), F32)], 1),
        ],
        0,
    )
    small_other = swap(small, "section")
    enc_small = jnp.where(first_core, small, small_other)
    dec_small = jnp.where(first_core, small_other, small)

    def small_of(s):
        down_bias = jnp.stack([s[3:4, :units], s[3:4, units : 2 * units]], 0)
        return s[0:1], s[1:2], s[2:3], down_bias

    enc_gain1, enc_gain2, enc_upb, enc_downb = small_of(enc_small)
    dec_gain1, dec_gain2, dec_upb, dec_downb = small_of(dec_small)
    mid_gain = cross_gain[None]

    segs = lax.dynamic_index_in_dim(segment_ids, side, 1, keepdims=False)
    docs = jnp.arange(seq)
    counts = jnp.sum(segs[:, :, None] == docs[None, None, :8], 1)
    largest = jnp.argmax(counts, 1)
    starts = jnp.sum(segs < largest[:, None], 1).astype(jnp.int32)

    def halves_of_seg(seg, start):
        twice = jnp.concatenate([seg, seg], 0)
        mine = lax.dynamic_slice_in_dim(twice, start + half * core, half, 0)
        away = lax.dynamic_slice_in_dim(twice, start + half * (1 - core), half, 0)
        return mine, away

    enc_seg, enc_seg_away = halves_of_seg(segs[0], starts[0])
    dec_seg, _ = halves_of_seg(segs[1], starts[1])
    own_start = jnp.where(first_core, starts[0], starts[1])

    def rows_sent(value, token=None):
        keep = lax.dynamic_index_in_dim(value[0], side, 0, keepdims=False)
        give = lax.dynamic_index_in_dim(value[0], 1 - side, 0, keepdims=False)
        return keep, over_y(give if token is None else after(give, token))

    def rows_here(keep, got):
        start = lax.rem(own_start + seq - half * side, seq)
        ring = (keep, got, keep, got)
        mine = rotated(ring, start + half * core, half)
        away = rotated(ring, lax.rem(start + half * (1 - core), seq), half)
        other = swap(away, "section")
        return jnp.where(first_core, mine, other), jnp.where(first_core, other, mine)

    def slices_back(big, rest, start):
        ring = (big, rest, big, rest)
        keep = rotated(ring, lax.rem(half * side + seq - start, seq), half)
        give = rotated(ring, lax.rem(half * (1 - side) + seq - start, seq), half)
        return keep, give

    def by_row(keep, got):
        return jnp.where(side == 0, jnp.stack([keep, got]), jnp.stack([got, keep]))

    def rows_back(enc, dec):
        mine = jnp.where(first_core, enc, dec)
        away = jnp.where(first_core, dec, enc)
        other = swap(away, "section")
        big = jnp.where(first_core, mine, other)
        rest = jnp.where(first_core, other, mine)
        keep, give = slices_back(big, rest, own_start)
        return by_row(keep, swap(give, "mp"))

    def layer_back(layer, value):
        other = lax.ppermute(value, MESH_AXES, route("section", 1, 1 - layer))
        big, rest = (value, other) if layer == 0 else (other, value)
        keep, give = slices_back(big, rest, starts[layer])
        return by_row(keep, lax.ppermute(give, MESH_AXES, route("mp", 1, layer)))

    x_keep, x_got = rows_sent(inputs)
    near_ffn = near_pairs(ffn_in[0], ffn_out[0], adapter_down[0], adapter_up[0])
    near_cross = near_pairs(cross_kv[0], cross_vo[0])
    near_other = [pair[1] for pair in near_self + near_ffn + near_cross]
    self_0 = over_y(self_piece(0))
    self_3 = over_y(self_piece(3))
    self_1, self_2 = over_x(after(self_0, near_other)), over_z(after(self_0, near_other))
    self_swaps = [swapped(p) for p in (self_0, self_1, self_2)]
    self_swaps.append(swapped(after(self_3, (self_1, self_2))))
    cross_0 = over_y(after(cross_piece(0), (self_1, self_2)))
    enc_0 = over_y(ffn_piece(0, 0))
    lane_y.depth = 2
    x_enc, x_dec = rows_here(x_keep, x_got)
    w_self = self_plan(near_self, quarters((self_0, self_1, self_2, self_3), self_swaps, 2))

    enc_col, enc_row = enc_seg[:, None], enc_seg[None, :]
    dec_col, dec_row = dec_seg[:, None], dec_seg[None, :]
    all_keys = jnp.stack([enc_seg, enc_seg_away], 0)[:, :, None]

    e_qkv, e_lse, e_hat1, e_inv1 = self_forward(0, x_enc, enc_col, enc_row, enc_gain1, w_self)
    enc_1, enc_2 = over_x(after(enc_0, e_inv1)), over_z(after(enc_0, e_inv1))
    enc_3 = over_y(after(ffn_piece(0, 3), e_inv1))
    d_qkv, d_lse, d_hat1, d_inv1 = self_forward(
        1, after(x_dec, e_inv1), dec_col, dec_row, dec_gain1, w_self
    )
    enc = (enc_0, enc_1, enc_2, enc_3)
    w_enc = branch_plan(near_ffn, eighths(enc, swapped_after(enc, d_inv1), width), stride)
    cross_1, cross_2 = over_x(after(cross_0, d_inv1)), over_z(after(cross_0, d_inv1))
    cross_3 = over_y(after(cross_piece(3), d_inv1))
    dec_0 = over_y(after(ffn_piece(1, 0), d_inv1))
    e_slope, e_aslope, e_aact, e_hat2, e_inv2, y_enc = branch_forward(
        0, after(e_hat1, d_inv1), enc_gain1, enc_gain2, enc_downb, enc_upb, w_enc
    )
    crosses = (cross_0, cross_1, cross_2, cross_3)
    cross_swaps = swapped_after(crosses, e_inv2)
    w_cross = cross_plan(near_cross, quarters(crosses, cross_swaps, 1))
    dec_3 = over_y(after(ffn_piece(1, 3), e_inv2))
    kv = keys_forward(after(y_enc, dec_0), w_cross)
    kv_away = swap(kv, "section")
    dec_1, dec_2 = over_x(after(dec_0, kv)), over_z(after(dec_0, kv))
    d_q, c_lse, d_hat2, d_inv2 = cross_forward(
        d_hat1, dec_gain1, kv, kv_away, all_keys, dec_row, w_cross
    )
    dec = (dec_0, dec_1, dec_2, dec_3)
    w_dec = branch_plan(near_ffn, eighths(dec, swapped_after(dec, d_inv2), width), stride)
    g_keep, g_got = rows_sent(cotangent, kv)
    d_slope, d_aslope, d_aact, d_hat3, d_inv3, y_dec = branch_forward(
        1, d_hat2, mid_gain, dec_gain2, dec_downb, dec_upb, w_dec
    )
    g_enc, g_dec = rows_here(g_keep, g_got)

    def summed_here(grads):
        keep = lax.dynamic_index_in_dim(grads, core, 1, keepdims=False)
        give = lax.dynamic_index_in_dim(grads, 1 - core, 1, keepdims=False)
        return (keep.astype(F32) + swap(give, "section").astype(F32)).astype(BF16)

    def summed_side(both, token):
        got = after(swap(both[1], "mp"), token)
        return (both[0].astype(F32) + got.astype(F32)).astype(BF16)

    def summed_rows(value, over, token):
        for flip in over:
            got = after(lax.ppermute(value, MESH_AXES, route("dp", flip)), token)
            value = (value.astype(F32) + got.astype(F32)).astype(BF16)
        return value

    flips = [1 << i for i in range(lax.axis_size("dp").bit_length() - 1)]
    flips = flips[2:3] + flips[:2] + flips[3:]
    d_mid, d_grads = branch_backward(
        1, g_dec, d_hat3, d_inv3, dec_gain2, d_hat2, d_inv2, mid_gain,
        d_slope, d_aslope, d_aact, w_dec,
    )
    d_both = summed_here(d_grads)
    d_first, kv_grad, kv_grad_give = cross_backward(
        after(d_mid, d_both), d_hat1, d_inv1, dec_gain1, d_q, c_lse, kv, kv_away, all_keys, dec_row,
        w_cross,
    )
    kv_grad_away = swap(kv_grad_give, "section")
    e_out = keys_backward(g_enc, kv_grad, kv_grad_away, w_cross)
    e_first, e_grads = branch_backward(
        0, e_out, e_hat2, e_inv2, enc_gain2, e_hat1, e_inv1, enc_gain1,
        e_slope, e_aslope, e_aact, w_enc,
    )
    e_both = summed_here(e_grads)
    d_total = summed_side(d_both, e_first)
    d_first = after(d_first, e_both)
    bunches = len(w_self.steps)

    def self_part(layer, grad, base, saved, lse, col, row, first, count):
        return self_backward(layer, grad, base, saved, lse, col, row, w_self, first, count)

    outputs = rows_back(y_enc, y_dec)
    dx_dec = self_part(1, d_first, d_first, d_qkv, d_lse, dec_col, dec_row, 0, bunches)
    e_total = summed_side(e_both, dx_dec)
    d_total = summed_rows(d_total, flips[:1], dx_dec)
    e_first = after(e_first, (dx_dec, e_total, outputs))
    dx_dec_back = layer_back(1, dx_dec)
    dx_enc = self_part(0, e_first, e_first, e_qkv, e_lse, enc_col, enc_row, 0, bunches)
    e_total = summed_rows(e_total, flips[:1], dx_enc)
    d_total = summed_rows(d_total, flips[1:2], dx_enc)
    e_total = summed_rows(e_total, flips[1:], dx_enc)
    d_total = summed_rows(d_total, flips[2:], dx_enc)
    dx = jnp.where(first_core, layer_back(0, dx_enc), dx_dec_back)
    mine = jnp.where(first_core, e_total, d_total)
    other = swap(jnp.where(first_core, d_total, e_total), "section")
    down_total = jnp.where(first_core, mine, other)[:units].astype(F32)
    down_total = jnp.transpose(down_total.reshape(units, -1, units), (1, 0, 2)).reshape(width, units)
    up_total = jnp.where(first_core, other, mine).astype(F32)
    dx = jnp.where(first_core, layer_back(0, dx_enc), dx_dec_back)

    return (
        outputs[None],
        dx.astype(F32)[None],
        down_total[None],
        up_total[units : units + 1, :units],
        up_total[:units][None],
        up_total[units + 1 : units + 2],
    )


def solution(mesh):
    in_specs = (
        P("section", "dp", "mp", None),
        P(None, "dp", None),
        P("section", "dp", "mp", None),
        P("section", None, None),
        P(),
        P("section", None, None, "mp"),
        P("section", "mp", None),
        P("section", None, "mp"),
        P("section", None, "mp"),
        P("section", None, "mp"),
        P("section", "mp", None),
        P("section", None, "mp"),
        P("section", "mp"),
        P("section", "mp", None),
        P("section", None),
    )
    out_specs = (
        P("section", "dp", "mp", None),
        P("section", "dp", "mp", None),
        P("section", None, "mp"),
        P("section", "mp"),
        P("section", "mp", None),
        P("section", None),
    )
    return jax.shard_map(
        per_device, mesh=mesh, in_specs=in_specs, out_specs=out_specs, check_vma=False
    )
```
